128 devices in a mesh: prow: 16 (over z, y_hi, core), pcol: 8 (over y_lo, x).
Axes of the slice: x: 4, y: 4 (y_hi: 2, y_lo: 2; y = y_hi * 2 + y_lo), z: 4, core: 2. Of those that a mesh axis runs over, the one named last changes fastest.
Arguments:
- s_bar: float32 [3, 16, 512, 6, 8, 512], P(None, 'prow', None, None, 'pcol'), may hold values from -0.02734375 to 0.02734375
- l21: float32 [3, 16, 512, 512], P(None, 'prow', 'pcol'), may hold values from -6 to 6
- panel_column_cotangent: float32 [3, 16, 512, 512], P(None, 'prow', 'pcol'), may hold values from -6 to 6
- l11: float32 [512, 512], replicated, may hold values from -1 to 2, as said below
- l11_bar: float32 [512, 512], replicated, may hold values from -896 to 896
- coords: float32 [2, 24576], replicated, may hold values from 0 to 1
- sigma: float32 [24576], replicated, may hold values from 1 to 4
- length: float32 [24576], replicated, may hold values from 0.02 to 0.3
- tile_block: int32 [48], replicated, may hold values from 0 to 47, each once
Outputs:
- a21_bar: float32 [3, 16, 512, 512], P(None, 'prow', 'pcol')
- a11_bar: float32 [512, 512], replicated
- row_grad: float32 [3, 16, 512], P(None, 'prow', 'pcol')
The draws below stay inside these ranges and needn't reach their ends.
Inputs may be any that keep to these rules, and one draw needn't show every extreme that they name: `l11`: lower triangular, diagonal between 1 and 2, off-diagonal magnitudes of a row summing under 0.9. `tile_block`: each block number once.
All inputs are finite; a program needn't handle non-finite values.
Results may differ from the reference program's by a relative error of at most 0.00011.
Values sent between devices are 32-bit elements; how exact they have to be, the bound alone decides.
No kernel may reach another device: no remote copies, remote signals or barrier semaphores. Data moves between devices by JAX's collectives and lax.ppermute only.
A program may use at most 192 MiB of HBM per device.

```python
import math
import jax
import jax.numpy as jnp
from jax import lax

B = 512
TPR = 3
NT = 48
TPC = 6
M = 24576
N_PROW = 16
N_PCOL = 8


def draw_l11(key, part):
    key = jax.random.fold_in(key, 7)
    first, second = jax.random.split(key)
    diag = jax.random.uniform(first, (B,), jnp.float32, 1.0, 2.0)
    off = jax.random.uniform(second, (B, B), jnp.float32, -0.9, 0.9) / B
    return jnp.tril(off, -1) + jnp.diag(diag)


def level_of(own_key, dims, cuts, smallest, high):
    def one(axis_at, blocks):
        heights = jax.random.uniform(jax.random.fold_in(jax.random.fold_in(own_key, 6), axis_at), (blocks,), jnp.float32, smallest / len(cuts), high / len(cuts))
        return jnp.repeat(jnp.exp(heights), dims[axis_at] // blocks).reshape((-1,) + (1,) * (len(dims) - axis_at - 1))

    factor_of = one(*cuts[0])
    for cut in cuts[1:]:
        factor_of = factor_of * one(*cut)
    return factor_of


def normal_values(rng, shape, width, bound, pieces=(), held_as=jnp.bfloat16):
    level = level_of(rng, shape, pieces, -0.22, 0.18) if pieces else 1.0
    array = jax.random.normal(rng, shape, jnp.float32) * width * level
    return jnp.minimum(jnp.maximum(array, -bound), bound).astype(held_as)


def setup_inputs(seed: int = 0) -> dict:
    streams_of = jax.random.split(jax.random.key(seed), 10)
    s_bar = normal_values(streams_of[0], (TPR, N_PROW, B, TPC, N_PCOL, B), (2 * M) ** -0.5, 0.02734375, ((1, 16), (4, 8)), jnp.float32)
    l21 = normal_values(streams_of[1], (TPR, N_PROW, B, B), 1.0, 6.0, ((1, 16), (2, 8)), jnp.float32)
    panel_column_cotangent = normal_values(streams_of[2], (TPR, N_PROW, B, B), 1.0, 6.0, ((1, 16), (2, 8)), jnp.float32)
    l11 = draw_l11(jax.random.fold_in(streams_of[9], 71), 0)
    l11_bar = normal_values(streams_of[4], (B, B), ((M * 1.0) ** 0.5), 896.0, (), jnp.float32)
    coords = jnp.clip(jax.random.uniform(streams_of[5], (2, M), jnp.float32, 0.0, 1.0), 0.0, 1.0)
    sigma = jnp.clip(jnp.exp(jax.random.uniform(streams_of[6], (M,), jnp.float32, math.log(1.0), math.log(4.0))), 1.0, 4.0)
    length = jnp.clip(jnp.exp(jax.random.uniform(streams_of[7], (M,), jnp.float32, math.log(0.02), math.log(0.3))), 0.02, 0.3)
    tile_block = jax.random.permutation(streams_of[8], NT).astype(jnp.int32)
    return {"s_bar": s_bar, "l21": l21, "panel_column_cotangent": panel_column_cotangent, "l11": l11, "l11_bar": l11_bar, "coords": coords, "sigma": sigma, "length": length, "tile_block": tile_block}


HIGH_PRECISION = lax.Precision.HIGHEST

def matern(row_x, row_y, row_s, row_l, col_x, col_y, col_s, col_l):
    delta_x = row_x[:, None] - col_x[None, :]
    delta_y = row_y[:, None] - col_y[None, :]
    dist = jnp.sqrt(delta_x * delta_x + delta_y * delta_y)
    scale = 0.5 * (row_l[:, None] + col_l[None, :])
    ratio = jnp.sqrt(3.0) * dist / scale
    return row_s[:, None] * col_s[None, :] * (1.0 + ratio) * jnp.exp(-ratio)

def reference(s_bar, l21, panel_column_cotangent, l11, l11_bar, coords, sigma, length, tile_block):
    total = NT * B
    smat = s_bar.reshape(total, total)
    panel = l21.reshape(total, B)
    panel_cotangent = panel_column_cotangent.reshape(total, B)
    order = (tile_block[:, None] * B + jnp.arange(B, dtype=jnp.int32)[None, :]).reshape(total).astype(jnp.int32)
    feats = (coords[0][order], coords[1][order], sigma[order], length[order])

    def step(carry, tile):
        col_acc, trans_acc = carry
        start = tile * B
        srow = lax.dynamic_slice_in_dim(smat, start, B, 0)
        rows = [lax.dynamic_slice_in_dim(f, start, B, 0) for f in feats]
        kern = matern(rows[0], rows[1], rows[2], rows[3], feats[0], feats[1], feats[2], feats[3])
        weighted = srow * kern
        lrow = lax.dynamic_slice_in_dim(panel, start, B, 0)
        direct_product = jnp.dot(srow.astype(jnp.float32), panel.astype(jnp.float32), precision=HIGH_PRECISION, preferred_element_type=jnp.float32)
        trans_acc = trans_acc + lax.dot_general(srow.astype(jnp.float32), lrow.astype(jnp.float32), (((0,), (0,)), ((), ())), precision=HIGH_PRECISION, preferred_element_type=jnp.float32)
        col_acc = col_acc + lax.optimization_barrier(jnp.sum(weighted, axis=0))
        return ((col_acc, trans_acc), (direct_product, lax.optimization_barrier(jnp.sum(weighted, axis=1))))
    init = (jnp.zeros((total,), jnp.float32), jnp.zeros((total, B), jnp.float32))
    (col_sum, transposed_product), (direct_product, row_sum) = lax.scan(step, init, jnp.arange(NT, dtype=jnp.int32))
    direct_product = direct_product.reshape(total, B)
    row_grad = row_sum.reshape(total) + col_sum
    value_matrix = panel_cotangent - direct_product - transposed_product
    lower_inverse = lax.linalg.triangular_solve(l11, jnp.eye(B, dtype=jnp.float32), left_side=True, lower=True)
    gradient_below21 = jnp.dot(value_matrix.astype(jnp.float32), lower_inverse.astype(jnp.float32), precision=HIGH_PRECISION, preferred_element_type=jnp.float32)
    gram = lax.dot_general(gradient_below21.astype(jnp.float32), panel.astype(jnp.float32), (((0,), (0,)), ((), ())), precision=HIGH_PRECISION, preferred_element_type=jnp.float32)
    hmat = l11_bar - gram
    xmat = jnp.dot(l11.T.astype(jnp.float32), hmat.astype(jnp.float32), precision=HIGH_PRECISION, preferred_element_type=jnp.float32)
    pmat = jnp.tril(xmat) - 0.5 * jnp.diag(jnp.diag(xmat))
    qmat = jnp.dot(jnp.dot(lower_inverse.T.astype(jnp.float32), pmat.astype(jnp.float32), precision=HIGH_PRECISION, preferred_element_type=jnp.float32).astype(jnp.float32), lower_inverse.astype(jnp.float32), precision=HIGH_PRECISION, preferred_element_type=jnp.float32)
    grad11 = 0.5 * (qmat + qmat.T)
    return (gradient_below21.reshape(TPR, N_PROW, B, B), grad11, row_grad.reshape(TPR, N_PROW, B))
```

```python
import math

import jax
import jax.numpy as jnp
from jax import lax
from jax.experimental import pallas as pl
from jax.experimental.pallas import tpu as pltpu
from jax.sharding import PartitionSpec as P

HIGH_PRECISION = lax.Precision.HIGHEST
F32 = jnp.float32
BF16 = jnp.bfloat16
SCALE = math.sqrt(12.0) * math.log2(math.e)
MIB = 1024 * 1024


def params(mib, dims=1):
    return pltpu.CompilerParams(
        vmem_limit_bytes=mib * MIB, dimension_semantics=("arbitrary",) * dims
    )


def split(value):
    high = value.astype(BF16)
    low = (value - high.astype(F32)).astype(BF16)
    return high, low


def dot(a, b):
    return jnp.dot(a, b, preferred_element_type=F32)


def dot3(a_high, a_low, b_high, b_low):
    return dot(a_high, b_high) + dot(a_low, b_high) + dot(a_high, b_low)


def full(shape):
    return pl.BlockSpec(shape, lambda *_: (0,) * len(shape))


ROWS = 128
GROUP = 16


def prep_kernel(first, starts, *refs):
    if first == 0:
        s_ref, co_ref, sg_ref, le_ref, hi_ref, lo_ref, rs_ref, cs_ref, cacc, feat, racc_ref = refs
    else:
        s_ref, co_ref, sg_ref, le_ref, _, _, hi_ref, lo_ref, rs_ref, cs_ref, cacc, feat, racc_ref = refs
    step = pl.program_id(0)
    tiles_c = cs_ref.shape[0] // 4
    chunks = 4 * tiles_c
    row_off = pl.multiple_of(starts[first] + step * ROWS, ROWS)

    @pl.when(step == 0)
    def _():
        cacc[...] = jnp.zeros_like(cacc)
        for j in range(tiles_c):
            off = pl.multiple_of(starts[3 + j], 512)
            for k in range(4):
                c = j * 4 + k
                at = pl.ds(pl.multiple_of(off + k * 128, 128), 128)
                feat[0, pl.ds(c, 1), :] = co_ref[0:1, at]
                feat[1, pl.ds(c, 1), :] = co_ref[1:2, at]
                feat[2, pl.ds(c, 1), :] = sg_ref[0:1, at]
                feat[3, pl.ds(c, 1), :] = le_ref[0:1, at] * (1.0 / SCALE)

    at = pl.ds(row_off, ROWS)

    def column(row):
        return jnp.broadcast_to(row, (ROWS, ROWS)).T

    racc_ref[1] = column(co_ref[0:1, at])
    racc_ref[2] = column(co_ref[1:2, at])
    racc_ref[3] = column(sg_ref[0:1, at])
    racc_ref[4] = column(le_ref[0:1, at] * (1.0 / SCALE))

    def body(g, _):
        base = pl.multiple_of(g * GROUP, GROUP)
        rows = pl.ds(base, GROUP)
        row_x, row_y, row_s, row_l = (racc_ref[k, rows, :] for k in range(1, 5))
        acc = jnp.zeros((GROUP, 128), F32)
        for c in range(chunks):
            s = s_ref[pl.ds(base * chunks + c, GROUP, stride=chunks), :]
            dx = row_x - feat[0, c : c + 1, :]
            dy = row_y - feat[1, c : c + 1, :]
            dist2 = dx * dx + dy * dy
            scale = row_l + feat[3, c : c + 1, :]
            g2 = dist2 * lax.rsqrt(jnp.maximum(dist2 * (scale * scale), 1e-30))
            weighted = s * ((1.0 + g2 * math.log(2.0)) * jnp.exp2(-g2))
            acc = acc + weighted * feat[2, c : c + 1, :]
            by_row = weighted * row_s
            cacc[c] += by_row.reshape(GROUP // 8, 8, 128).sum(0)
            high, low = split(s)
            hi_ref[rows, c * 128 : (c + 1) * 128] = high
            lo_ref[rows, c * 128 : (c + 1) * 128] = low
        racc_ref[0, rows, :] = acc * row_s
        return 0

    lax.fori_loop(0, ROWS // GROUP, body, 0)
    rs_ref[0] = racc_ref[0].T.sum(0, keepdims=True)

    @pl.when(step == pl.num_programs(0) - 1)
    def _():
        cs_ref[...] = cacc[...].sum(1) * feat[2]


def prep(first, starts, s_view, coords, sigma, length, bufs, rows, cols):
    chunks = cols // 128
    per = 512 // ROWS
    any_spec = pl.BlockSpec(memory_space=pl.ANY)
    out_map = lambda s, st: (first * per + s, 0)
    args = [starts, s_view, coords, sigma, length]
    in_specs = [
        pl.BlockSpec((ROWS * chunks, 128), out_map),
        full(coords.shape),
        full(sigma.shape),
        full(length.shape),
    ]
    aliases = {}
    if first:
        args += list(bufs)
        in_specs += [any_spec, any_spec]
        aliases = {5: 0, 6: 1}
    elements = 512 * cols
    return pl.pallas_call(
        lambda *refs: prep_kernel(first, *refs),
        grid_spec=pltpu.PrefetchScalarGridSpec(
            num_scalar_prefetch=1,
            grid=(per,),
            in_specs=in_specs,
            out_specs=[
                pl.BlockSpec((ROWS, cols), out_map),
                pl.BlockSpec((ROWS, cols), out_map),
                pl.BlockSpec((1, 1, ROWS), lambda s, st: (s, 0, 0)),
                pl.BlockSpec((chunks, 128), lambda s, st: (0, 0)),
            ],
            scratch_shapes=[
                pltpu.VMEM((chunks, 8, 128), F32),
                pltpu.VMEM((4, chunks, 128), F32),
                pltpu.VMEM((5, ROWS, ROWS), F32),
            ],
        ),
        out_shape=[
            jax.ShapeDtypeStruct((rows, cols), BF16),
            jax.ShapeDtypeStruct((rows, cols), BF16),
            jax.ShapeDtypeStruct((per, 1, ROWS), F32),
            jax.ShapeDtypeStruct((chunks, 128), F32),
        ],
        input_output_aliases=aliases,
        compiler_params=params(32),
        cost_estimate=pl.CostEstimate(
            flops=24 * elements, bytes_accessed=8 * elements, transcendentals=2 * elements
        ),
        name="kernel_sums",
    )(*args)


def rows_kernel(pos, *refs):
    pieces, (th_ref, tl_ref, full_ref) = refs[:8], refs[8:]
    count, part, width = pieces[0].shape
    for r in range(8):
        for i in range(count):
            at = pl.multiple_of(i * 512 + pos[r] * part, part)
            full_ref[pl.ds(at, part), :] = pieces[r][i]
    for k in range(count * 4):
        block = full_ref[k * 128 : (k + 1) * 128, :].T
        high, low = split(block)
        th_ref[:, k * 128 : (k + 1) * 128] = high
        tl_ref[:, k * 128 : (k + 1) * 128] = low


def assemble_rows(pos, pieces):
    count, part, width = pieces[0].shape
    shape = (width, count * 512)
    out = jax.ShapeDtypeStruct(shape, BF16)
    return pl.pallas_call(
        rows_kernel,
        grid_spec=pltpu.PrefetchScalarGridSpec(
            num_scalar_prefetch=1,
            grid=(1,),
            in_specs=[full(p.shape) for p in pieces],
            out_specs=[full(shape)] * 2,
            scratch_shapes=[pltpu.VMEM(shape[::-1], F32)],
        ),
        out_shape=[out] * 2,
        compiler_params=params(32),
        cost_estimate=pl.CostEstimate(flops=0, bytes_accessed=8 * width * shape[1], transcendentals=0),
        name="row_panels",
    )(pos, *pieces)


def cols_kernel(pos, *refs):
    pieces, (h_ref, l_ref) = refs[:16], refs[16:]
    count, part, width = pieces[0].shape
    for r in range(16):
        for i in range(count):
            at = pl.multiple_of(i * 1024 + pos[r] * part, part)
            high, low = split(pieces[r][i])
            h_ref[pl.ds(at, part), :] = high
            l_ref[pl.ds(at, part), :] = low


def assemble_cols(pos, pieces):
    count, part, width = pieces[0].shape
    shape = (count * 1024, width)
    out = jax.ShapeDtypeStruct(shape, BF16)
    return pl.pallas_call(
        cols_kernel,
        grid_spec=pltpu.PrefetchScalarGridSpec(
            num_scalar_prefetch=1,
            grid=(1,),
            in_specs=[full(p.shape) for p in pieces],
            out_specs=[full(shape)] * 2,
        ),
        out_shape=[out] * 2,
        compiler_params=params(40),
        cost_estimate=pl.CostEstimate(flops=0, bytes_accessed=8 * width * shape[0], transcendentals=0),
        name="column_panels",
    )(pos, *pieces)


def trans_product(scal, th, tl, s_hi, s_lo, groups):
    width, rows = th.shape
    count = rows // 512
    n = len(groups)

    def kernel(sc, th_ref, tl_ref, sh_ref, sl_ref, *refs):
        outs, tmp = refs[:-1], refs[-1]
        step = pl.program_id(0)
        out = dot3(th_ref[...], tl_ref[...], sh_ref[...], sl_ref[...])
        tmp[...] = out.T
        for g in range(n):
            @pl.when(step // count == g)
            def _(g=g):
                for dyh in range(2):
                    own = pl.multiple_of(sc[4 + dyh * 2] * 64, 64)
                    other = pl.multiple_of(sc[4 + dyh * 2 + 1] * 64, 64)
                    outs[3 * g + dyh][0] = tmp[pl.ds(own, 64), :]
                    outs[3 * g + 2][dyh, 0] = tmp[pl.ds(other, 64), :]

    def s_map(step, sc):
        z = sc[groups[0]]
        for g in range(1, n):
            z = jnp.where(step // count == g, sc[groups[g]], z)
        return (0, (step % count) * 4 + z)

    out_specs, out_shape = [], []
    for g in range(n):
        at = lambda step, g=g: jnp.clip(step - g * count, 0, count - 1)
        for _ in range(2):
            out_specs.append(pl.BlockSpec((1, 64, width), lambda step, sc, at=at: (at(step), 0, 0)))
            out_shape.append(jax.ShapeDtypeStruct((count, 64, width), F32))
        out_specs.append(pl.BlockSpec((2, 1, 64, width), lambda step, sc, at=at: (0, at(step), 0, 0)))
        out_shape.append(jax.ShapeDtypeStruct((2, count, 64, width), F32))
    flops = 6 * width * rows * 256 * count * n
    return pl.pallas_call(
        kernel,
        grid_spec=pltpu.PrefetchScalarGridSpec(
            num_scalar_prefetch=1,
            grid=(count * n,),
            in_specs=[full(th.shape)] * 2 + [pl.BlockSpec((rows, 256), s_map)] * 2,
            out_specs=out_specs,
            scratch_shapes=[pltpu.VMEM((256, width), F32)],
        ),
        out_shape=out_shape,
        compiler_params=params(48),
        cost_estimate=pl.CostEstimate(
            flops=flops, bytes_accessed=4 * rows * 256 * count * n, transcendentals=0
        ),
        name="transposed_product",
    )(scal, th, tl, s_hi, s_lo)


def direct_product(scal, ch, cl, s_hi, s_lo, th, tl, dyl, gram=None, base=None):
    cols, width = ch.shape
    count = s_hi.shape[0] // 512
    last = gram is not None

    def kernel(sc, ch_ref, cl_ref, sh_ref, sl_ref, th_ref, tl_ref, *refs):
        if last:
            gram_ref, base_ref = refs[:2]
            outs, (eo_ref, ex_ref, tmp, acc) = refs[2:6], refs[6:]
        else:
            outs, (g_ref, tmp, acc) = refs[:4], refs[4:]
        step = pl.program_id(0)
        out = dot3(sh_ref[...], sl_ref[...], ch_ref[...], cl_ref[...])
        tmp[...] = out
        for dx in range(4):
            at = pl.multiple_of(sc[2 + dx] * 64, 64)
            outs[dx][0] = tmp[pl.ds(at, 64), :]
        high, low = split(out)
        part = dot3(th_ref[...], tl_ref[...], high, low)

        @pl.when(step == 0)
        def _():
            acc[...] = (part + gram_ref[...]) if last else part

        @pl.when(step > 0)
        def _():
            acc[...] += part

        @pl.when(step == count - 1)
        def _():
            if last:
                total = acc[...]
                acc[...] = base_ref[...] - total - total.T
                for dx in range(4):
                    own = pl.multiple_of((sc[6] * 4 + sc[2 + dx]) * 64, 64)
                    other = pl.multiple_of(((1 - sc[6]) * 4 + sc[2 + dx]) * 64, 64)
                    eo_ref[dx] = acc[pl.ds(own, 64), :]
                    ex_ref[dx] = acc[pl.ds(other, 64), :]
            else:
                g_ref[...] = acc[...]

    s_map = lambda step, sc: (step * 2 + sc[dyl], 0)
    t_map = lambda step, sc: (0, step * 2 + sc[dyl])
    args = [scal, ch, cl, s_hi, s_lo, th, tl]
    in_specs = (
        [full(ch.shape)] * 2
        + [pl.BlockSpec((256, cols), s_map)] * 2
        + [pl.BlockSpec((width, 256), t_map)] * 2
    )
    out_specs = [pl.BlockSpec((1, 64, width), lambda step, sc: (step, 0, 0))] * 4
    out_shape = [jax.ShapeDtypeStruct((count, 64, width), F32)] * 4
    if last:
        args += [gram, base]
        in_specs += [full(gram.shape)] * 2
        out_specs += [full((4, 64, width))] * 2
        out_shape += [jax.ShapeDtypeStruct((4, 64, width), F32)] * 2
    else:
        out_specs += [full((width, width))]
        out_shape += [jax.ShapeDtypeStruct((width, width), F32)]
    flops = 6 * 256 * count * width * (cols + width)
    return pl.pallas_call(
        kernel,
        grid_spec=pltpu.PrefetchScalarGridSpec(
            num_scalar_prefetch=1,
            grid=(count,),
            in_specs=in_specs,
            out_specs=out_specs,
            scratch_shapes=[pltpu.VMEM((256, width), F32), pltpu.VMEM((width, width), F32)],
        ),
        out_shape=out_shape,
        compiler_params=params(48),
        cost_estimate=pl.CostEstimate(
            flops=flops, bytes_accessed=4 * 256 * cols * count, transcendentals=0
        ),
        name="direct_product",
    )(*args)


def hdot(a, b):
    return jnp.dot(a, b, precision=HIGH_PRECISION, preferred_element_type=F32)


def inverse_kernel(l_ref, bar_ref, inv_ref, invt_ref, c_ref):
    n = l_ref.shape[0]
    size = 128
    row = lax.broadcasted_iota(jnp.int32, (size, size), 0)
    col = lax.broadcasted_iota(jnp.int32, (size, size), 1)
    powers, results, scales = [], [], []
    for k in range(n // size):
        at = slice(k * size, (k + 1) * size)
        block = l_ref[at, at]
        diag = jnp.where(row == col, block, 0.0)
        by_row = 1.0 / diag.sum(1, keepdims=True)
        scales.append(1.0 / diag.sum(0, keepdims=True))
        nil = jnp.where(row > col, block, 0.0) * (-by_row)
        results.append(jnp.where(row == col, 1.0, 0.0) + nil)
        powers.append(nil)
    for _ in range(6):
        powers = [hdot(p, p) for p in powers]
        results = [r + hdot(r, p) for r, p in zip(results, powers)]
    inv_ref[...] = jnp.zeros_like(inv_ref)
    for k in range(n // size):
        at = slice(k * size, (k + 1) * size)
        inv_ref[at, at] = results[k] * scales[k]
    while size < n:
        for k in range(0, n, 2 * size):
            a, b = slice(k, k + size), slice(k + size, k + 2 * size)
            inv_ref[b, a] = -hdot(inv_ref[b, b], hdot(l_ref[b, a], inv_ref[a, a]))
        size *= 2
    invt_ref[...] = inv_ref[...].T
    c_ref[...] = hdot(l_ref[...].T, bar_ref[...])


def inverse(l11, l11_bar):
    out = jax.ShapeDtypeStruct(l11.shape, F32)
    return pl.pallas_call(
        inverse_kernel,
        out_shape=[out] * 3,
        compiler_params=pltpu.CompilerParams(vmem_limit_bytes=32 * MIB),
        cost_estimate=pl.CostEstimate(flops=6 * 10**9, bytes_accessed=5 * MIB, transcendentals=0),
        name="inverse",
    )(l11, l11_bar)


def final_kernel(pos, *refs):
    pieces, (ex_ref, c_ref, inv_ref, invt_ref, out_ref, x_ref) = refs[:4], refs[4:]
    n = c_ref.shape[0]
    for dx in range(4):
        own = pl.multiple_of(pos[dx] * 64, 64)
        other = pl.multiple_of(pos[4 + dx] * 64, 64)
        x_ref[pl.ds(own, 64), :] = pieces[dx][...]
        x_ref[pl.ds(other, 64), :] = ex_ref[dx]
    x = c_ref[...] - x_ref[...]
    row = lax.broadcasted_iota(jnp.int32, (n, n), 0)
    col = lax.broadcasted_iota(jnp.int32, (n, n), 1)
    p = jnp.where(row > col, x, jnp.where(row == col, 0.5 * x, 0.0))
    q = hdot(hdot(invt_ref[...], p), inv_ref[...])
    out_ref[...] = 0.5 * (q + q.T)


def final(pos, pieces, others, c, inv, invt):
    return pl.pallas_call(
        final_kernel,
        grid_spec=pltpu.PrefetchScalarGridSpec(
            num_scalar_prefetch=1,
            grid=(1,),
            in_specs=[full(p.shape) for p in pieces]
            + [full(others.shape)]
            + [full(c.shape)] * 3,
            out_specs=full(c.shape),
            scratch_shapes=[pltpu.VMEM(c.shape, F32)],
        ),
        out_shape=jax.ShapeDtypeStruct(c.shape, F32),
        compiler_params=params(32),
        name="diagonal_tile",
    )(pos, *pieces, others, c, inv, invt)


def permutations():
    def make(move):
        pairs = []
        for z in range(4):
            for yh in range(2):
                for core in range(2):
                    for yl in range(2):
                        for x in range(4):
                            nz, nyh, nc, nyl, nx = move(z, yh, core, yl, x)
                            src = (z * 4 + yh * 2 + core) * 8 + yl * 4 + x
                            dst = (nz * 4 + nyh * 2 + nc) * 8 + nyl * 4 + nx
                            pairs.append((src, dst))
        return pairs

    perms = {
        "x+": make(lambda z, h, c, l, x: (z, h, c, l, (x + 1) % 4)),
        "x-": make(lambda z, h, c, l, x: (z, h, c, l, (x + 3) % 4)),
        "x2": make(lambda z, h, c, l, x: (z, h, c, l, (x + 2) % 4)),
        "z+": make(lambda z, h, c, l, x: ((z + 1) % 4, h, c, l, x)),
        "z-": make(lambda z, h, c, l, x: ((z + 3) % 4, h, c, l, x)),
        "z^1": make(lambda z, h, c, l, x: (z ^ 1, h, c, l, x)),
        "z^2": make(lambda z, h, c, l, x: (z ^ 2, h, c, l, x)),
        "z^3": make(lambda z, h, c, l, x: (z ^ 3, h, c, l, x)),
        "yl": make(lambda z, h, c, l, x: (z, h, c, 1 - l, x)),
        "yh": make(lambda z, h, c, l, x: (z, 1 - h, c, l, x)),
        "yhl": make(lambda z, h, c, l, x: (z, 1 - h, c, 1 - l, x)),
        "core": make(lambda z, h, c, l, x: (z, h, 1 - c, l, x)),
    }
    home = lambda z, h, c, l, x: ((z // 2) * 2 + l, x // 2, x % 2, z % 2, h * 2 + c)
    flip = lambda z, h, c, l, x: ((z // 2) * 2 + l, 1 - x // 2, x % 2, z % 2, h * 2 + c)
    perms["home0"] = make(home)
    perms["home1"] = make(flip)
    perms["back0"] = [(d, s) for s, d in perms["home0"]]
    perms["back1"] = [(d, s) for s, d in perms["home1"]]
    return perms


PERMS = permutations()


def move(value, name):
    return lax.ppermute(value, ("prow", "pcol"), PERMS[name])


def per_device(s_bar, l21, panel_column_cotangent, l11, l11_bar, coords, sigma, length, tile_block):
    row_id = lax.axis_index("prow")
    col_id = lax.axis_index("pcol")
    count, _, width, tiles_c = s_bar.shape[:4]
    part = l21.shape[2]
    rows, cols = count * width, tiles_c * width
    z, yh, core = row_id // 4, (row_id // 2) % 2, row_id % 2
    yl, x = col_id // 4, col_id % 4
    own = l21.reshape(count, part, width)
    own_bar = panel_column_cotangent.reshape(count, part, width)
    ints = lambda vals: jnp.stack([jnp.asarray(v, jnp.int32) for v in vals])

    rw = {(0, 0): own}
    rw[1, 0] = move(own, "yl")
    rw[0, 3] = move(own, "x+")
    rw[0, 1] = move(own, "x-")
    cw = {(0, 0): move(own, "home0"), (1, 0): move(own, "home1")}
    rw[1, 3] = move(rw[1, 0], "x+")
    rw[1, 1] = move(rw[1, 0], "x-")
    rw[0, 2] = move(rw[0, 3], "x+")
    rw[1, 2] = move(rw[1, 1], "x-")
    for k in range(2):
        cw[k, 3] = move(cw[k, 0], "z+")
        cw[k, 1] = move(cw[k, 0], "z-")
    cw[0, 2] = move(cw[0, 3], "z+")
    cw[1, 2] = move(cw[1, 1], "z-")
    cx = {k: move(v, "core") for k, v in cw.items()}

    inv, invt, c_mat = inverse(l11, l11_bar)
    base = lax.dot_general(
        own_bar.reshape(count * part, width),
        own.reshape(count * part, width),
        (((0,), (0,)), ((), ())),
        precision=HIGH_PRECISION,
        preferred_element_type=F32,
    )

    row_tiles = [i * 16 + row_id for i in range(count)]
    col_tiles = [j * 8 + col_id for j in range(tiles_c)]
    starts = jnp.take(tile_block, ints(row_tiles + col_tiles)) * width
    s_view = s_bar.reshape(rows * cols // 128, 128)
    sig, len_ = sigma.reshape(1, -1), length.reshape(1, -1)
    bufs, row_sums, col_sums = None, [], []
    for i in range(count):
        s_hi, s_lo, rsum, csum = prep(i, starts, s_view, coords, sig, len_, bufs, rows, cols)
        bufs = (s_hi, s_lo)
        row_sums.append(rsum.reshape(1, width))
        col_sums.append(csum.reshape(tiles_c, width))
    row_sum = jnp.concatenate(row_sums).reshape(count, 1, width)
    col_sum = sum(col_sums).reshape(tiles_c, 1, width)
    sums = lax.dynamic_update_slice(
        jnp.zeros((count, 16, width), F32), row_sum, (0, row_id, 0)
    ).reshape(-1, width) + lax.dynamic_update_slice(
        jnp.zeros((tiles_c, 8, width), F32), col_sum, (0, col_id, 0)
    ).reshape(-1, width)
    sums = lax.psum(sums, ("prow", "pcol"))
    row_grad = lax.dynamic_slice(
        sums.reshape(count, 16, width), (0, row_id, col_id * part), (count, 1, part)
    )

    row_keys = [(a, b) for a in range(2) for b in range(4)]
    pos = ints([(yl ^ a) * 4 + (x + b) % 4 for a, b in row_keys])
    th, tl = assemble_rows(pos, [rw[k] for k in row_keys])
    scal = ints(
        [(z + d) % 4 for d in range(4)]
        + [(yh ^ a) * 2 + (core ^ b) for a in range(2) for b in range(2)]
    )
    ta = {}
    for groups in ((2,), (1, 3), (0,)):
        outs = trans_product(scal, th, tl, s_hi, s_lo, groups)
        for g, dz in enumerate(groups):
            got = move(outs[3 * g + 2], "core")
            for k in range(2):
                ta[k, dz] = outs[3 * g + k] + got[k]
    r1 = move(ta[0, 2], "z+")
    r2 = move(ta[1, 2], "z-")
    s2 = move(ta[1, 1], "z+")
    s4 = move(ta[0, 3], "z-")
    s1 = move(ta[0, 1] + r1, "z+")
    s3 = move(ta[1, 3] + r2, "z-")
    t0 = move(ta[0, 0] + s1 + s4, "back0")
    t1 = move(ta[1, 0] + s2 + s3, "back1")

    col_keys = [(a, b) for a in range(2) for b in range(4)]
    pos = ints(
        [((z + b) % 4) * 4 + (yh ^ a) * 2 + core for a, b in col_keys]
        + [((z + b) % 4) * 4 + (yh ^ a) * 2 + (1 - core) for a, b in col_keys]
    )
    ch, cl = assemble_cols(pos, [cw[k] for k in col_keys] + [cx[k] for k in col_keys])
    scal = ints([yl, 1 - yl] + [(x + d) % 4 for d in range(4)] + [core])
    y1 = direct_product(scal, ch, cl, s_hi, s_lo, th, tl, 1)
    gram = y1[4]
    y0 = direct_product(scal, ch, cl, s_hi, s_lo, th, tl, 0, gram, base)
    eo, ex = y0[4], y0[5]
    r2 = move(y1[2], "x-")
    s2 = move(y1[1], "x+")
    s3 = move(y1[3] + r2, "x-")
    r1 = move(y0[2], "x+")
    s4 = move(y0[3], "x-")
    s5 = move(y1[0] + s2 + s3, "yl")
    s1 = move(y0[1] + r1, "x+")

    got = move(ex, "core")
    e = [eo[d] + got[d] for d in range(4)]
    e = e[0] + move(e[1], "x+") + move(e[2], "x2") + move(e[3], "x-")
    e = (e + move(e, "z^1")) + (move(e, "z^2") + move(e, "z^3"))
    e = (e + move(e, "yl")) + (move(e, "yh") + move(e, "yhl"))
    e = [e, move(e, "x-"), move(e, "x2"), move(e, "x+")]
    others = move(jnp.stack(e), "core")
    pos = ints([core * 4 + (x + d) % 4 for d in range(4)] + [(1 - core) * 4 + (x + d) % 4 for d in range(4)])
    grad11 = final(pos, e, others, c_mat, inv, invt)

    value = own_bar - (y0[0] + s1 + s4 + s5) - (t0 + t1)
    grad21 = hdot(value.reshape(count * part, width), inv)
    return grad21.reshape(count, 1, part, width), grad11, row_grad


def solution(mesh):
    in_specs = (
        P(None, "prow", None, None, "pcol", None),
        P(None, "prow", "pcol", None),
        P(None, "prow", "pcol", None),
        P(),
        P(),
        P(),
        P(),
        P(),
        P(),
    )
    out_specs = (P(None, "prow", "pcol", None), P(), P(None, "prow", "pcol"))
    return jax.shard_map(
        per_device, mesh=mesh, in_specs=in_specs, out_specs=out_specs, check_vma=False
    )
```

```python
import math

import jax
import jax.numpy as jnp
from jax import lax
from jax.experimental import pallas as pl
from jax.experimental.pallas import tpu as pltpu
from jax.sharding import PartitionSpec as P

HIGH_PRECISION = lax.Precision.HIGHEST
F32 = jnp.float32
BF16 = jnp.bfloat16
SCALE = math.sqrt(12.0) * math.log2(math.e)
MIB = 1024 * 1024
LIMIT = 60


def params(mib, dims=1):
    return pltpu.CompilerParams(
        vmem_limit_bytes=mib * MIB, dimension_semantics=("arbitrary",) * dims
    )


def split(value):
    high = value.astype(BF16)
    low = (value - high.astype(F32)).astype(BF16)
    return high, low


def dot(a, b):
    return jnp.dot(a, b, preferred_element_type=F32)


def dot3(a_high, a_low, b_high, b_low):
    return dot(a_high, b_high) + dot(a_low, b_high) + dot(a_high, b_low)


def full(shape):
    return pl.BlockSpec(shape, lambda *_: (0,) * len(shape))


ROWS = 128
GROUP = 16


def prep_kernel(first, starts, *refs):
    s_ref, co_ref, sg_ref, le_ref = refs[:4]
    hi_ref, lo_ref, rs_ref, cs_ref, cacc, feat, racc_ref = refs[-7:]
    step = pl.program_id(0)
    tiles_c = cs_ref.shape[0] // 4
    chunks = 4 * tiles_c
    row_off = pl.multiple_of(starts[first] + step * ROWS, ROWS)

    @pl.when(step == 0)
    def _():
        cacc[...] = jnp.zeros_like(cacc)
        for j in range(tiles_c):
            off = pl.multiple_of(starts[3 + j], 512)
            for k in range(4):
                c = j * 4 + k
                at = pl.ds(pl.multiple_of(off + k * 128, 128), 128)
                feat[0, pl.ds(c, 1), :] = co_ref[0:1, at]
                feat[1, pl.ds(c, 1), :] = co_ref[1:2, at]
                feat[2, pl.ds(c, 1), :] = sg_ref[0:1, at]
                feat[3, pl.ds(c, 1), :] = le_ref[0:1, at] * (1.0 / SCALE)

    at = pl.ds(row_off, ROWS)

    def column(row):
        return jnp.broadcast_to(row, (ROWS, ROWS)).T

    racc_ref[1] = column(co_ref[0:1, at])
    racc_ref[2] = column(co_ref[1:2, at])
    racc_ref[3] = column(sg_ref[0:1, at])
    racc_ref[4] = column(le_ref[0:1, at] * (1.0 / SCALE))

    def body(g, _):
        base = pl.multiple_of(g * GROUP, GROUP)
        rows = pl.ds(base, GROUP)
        row_x, row_y, row_s, row_l = (racc_ref[k, rows, :] for k in range(1, 5))
        acc = jnp.zeros((GROUP, 128), F32)
        for c in range(chunks):
            s = s_ref[pl.ds(base * chunks + c, GROUP, stride=chunks), :]
            dx = row_x - feat[0, c : c + 1, :]
            dy = row_y - feat[1, c : c + 1, :]
            dist2 = dx * dx + dy * dy
            scale = row_l + feat[3, c : c + 1, :]
            g2 = dist2 * lax.rsqrt(jnp.maximum(dist2 * (scale * scale), 1e-30))
            weighted = s * ((1.0 + g2 * math.log(2.0)) * jnp.exp2(-g2))
            acc = acc + weighted * feat[2, c : c + 1, :]
            by_row = weighted * row_s
            cacc[c] += by_row.reshape(GROUP // 8, 8, 128).sum(0)
            high, low = split(s)
            hi_ref[rows, c * 128 : (c + 1) * 128] = high
            lo_ref[rows, c * 128 : (c + 1) * 128] = low
        racc_ref[0, rows, :] = acc * row_s
        return 0

    lax.fori_loop(0, ROWS // GROUP, body, 0)
    rs_ref[0] = racc_ref[0].T.sum(0, keepdims=True)

    @pl.when(step == pl.num_programs(0) - 1)
    def _():
        total = cacc[...].sum(1) * feat[2]
        cs_ref[...] = total if first == 0 else refs[7][...] + total


def prep(first, starts, s_view, coords, sigma, length, bufs, rows, cols):
    chunks = cols // 128
    per = 512 // ROWS
    any_spec = pl.BlockSpec(memory_space=pl.ANY)
    out_map = lambda s, st: (first * per + s, 0)
    args = [starts, s_view, coords, sigma, length]
    in_specs = [
        pl.BlockSpec((ROWS * chunks, 128), out_map),
        full(coords.shape),
        full(sigma.shape),
        full(length.shape),
    ]
    aliases = {}
    if first:
        args += list(bufs)
        in_specs += [any_spec, any_spec, any_spec, full((chunks, 128))]
        aliases = {5: 0, 6: 1, 7: 2}
    elements = 512 * cols
    return pl.pallas_call(
        lambda *refs: prep_kernel(first, *refs),
        grid_spec=pltpu.PrefetchScalarGridSpec(
            num_scalar_prefetch=1,
            grid=(per,),
            in_specs=in_specs,
            out_specs=[
                pl.BlockSpec((ROWS, cols), out_map),
                pl.BlockSpec((ROWS, cols), out_map),
                pl.BlockSpec((1, 1, ROWS), lambda s, st: (first * per + s, 0, 0)),
                pl.BlockSpec((chunks, 128), lambda s, st: (0, 0)),
            ],
            scratch_shapes=[
                pltpu.VMEM((chunks, 8, 128), F32),
                pltpu.VMEM((4, chunks, 128), F32),
                pltpu.VMEM((5, ROWS, ROWS), F32),
            ],
        ),
        out_shape=[
            jax.ShapeDtypeStruct((rows, cols), BF16),
            jax.ShapeDtypeStruct((rows, cols), BF16),
            jax.ShapeDtypeStruct((rows // ROWS, 1, ROWS), F32),
            jax.ShapeDtypeStruct((chunks, 128), F32),
        ],
        input_output_aliases=aliases,
        compiler_params=params(LIMIT),
        cost_estimate=pl.CostEstimate(
            flops=6000 * elements, bytes_accessed=8 * elements, transcendentals=2 * elements
        ),
        name="kernel_sums",
    )(*args)


def rows_kernel(pos, *refs):
    pieces, (th_ref, tl_ref, full_ref) = refs[:8], refs[8:]
    count, part, width = pieces[0].shape
    for r in range(8):
        for i in range(count):
            at = pl.multiple_of(i * 512 + pos[r] * part, part)
            full_ref[pl.ds(at, part), :] = pieces[r][i]
    for k in range(count * 4):
        block = full_ref[k * 128 : (k + 1) * 128, :].T
        high, low = split(block)
        th_ref[:, k * 128 : (k + 1) * 128] = high
        tl_ref[:, k * 128 : (k + 1) * 128] = low


def assemble_rows(pos, pieces):
    count, part, width = pieces[0].shape
    shape = (width, count * 512)
    out = jax.ShapeDtypeStruct(shape, BF16)
    return pl.pallas_call(
        rows_kernel,
        grid_spec=pltpu.PrefetchScalarGridSpec(
            num_scalar_prefetch=1,
            grid=(1,),
            in_specs=[full(p.shape) for p in pieces],
            out_specs=[full(shape)] * 2,
            scratch_shapes=[pltpu.VMEM(shape[::-1], F32)],
        ),
        out_shape=[out] * 2,
        compiler_params=params(LIMIT),
        cost_estimate=pl.CostEstimate(flops=0, bytes_accessed=8 * width * shape[1], transcendentals=0),
        name="row_panels",
    )(pos, *pieces)


def cols_kernel(pos, *refs):
    pieces, (h_ref, l_ref) = refs[:16], refs[16:]
    count, part, width = pieces[0].shape
    for r in range(16):
        for i in range(count):
            at = pl.multiple_of(i * 1024 + pos[r] * part, part)
            high, low = split(pieces[r][i])
            h_ref[pl.ds(at, part), :] = high
            l_ref[pl.ds(at, part), :] = low


def assemble_cols(pos, pieces):
    count, part, width = pieces[0].shape
    shape = (count * 1024, width)
    out = jax.ShapeDtypeStruct(shape, BF16)
    return pl.pallas_call(
        cols_kernel,
        grid_spec=pltpu.PrefetchScalarGridSpec(
            num_scalar_prefetch=1,
            grid=(1,),
            in_specs=[full(p.shape) for p in pieces],
            out_specs=[full(shape)] * 2,
        ),
        out_shape=[out] * 2,
        compiler_params=params(LIMIT),
        cost_estimate=pl.CostEstimate(flops=0, bytes_accessed=8 * width * shape[0], transcendentals=0),
        name="column_panels",
    )(pos, *pieces)


def put_row(ref, base, at, value):
    rows = pl.ds(base, 8)
    mask = lax.broadcasted_iota(jnp.int32, (8, 128), 0) == at
    ref[rows, :128] = jnp.where(mask, value, ref[rows, :128])


def trans_product(scal, th, tl, s_hi, s_lo, csum, groups):
    width, rows = th.shape
    count = rows // 512
    n = len(groups)
    high = count * 64 + 8

    def kernel(sc, th_ref, tl_ref, sh_ref, sl_ref, cs_ref, *refs):
        outs, tmp = refs[:-1], refs[-1]
        step = pl.program_id(0)
        tile = step % count
        rows_at = pl.ds(pl.multiple_of(tile * 64, 64), 64)
        out = dot3(th_ref[...], tl_ref[...], sh_ref[...], sl_ref[...])
        tmp[...] = out.T
        for g in range(n):
            @pl.when(step == g * count)
            def _(g=g):
                for dyh in range(2):
                    outs[3 * g + dyh][count * 64 :, :] = jnp.zeros((8, width), F32)
                    outs[3 * g + 2][dyh, count * 64 :, :] = jnp.zeros((8, width), F32)

            @pl.when(step // count == g)
            def _(g=g):
                for dyh in range(2):
                    own = pl.multiple_of(sc[4 + dyh * 2] * 64, 64)
                    other = pl.multiple_of(sc[4 + dyh * 2 + 1] * 64, 64)
                    sums = cs_ref[pl.ds(tile * 8 + sc[groups[g]] * 2 + sc[4 + dyh * 2] // 2, 1), :]
                    outs[3 * g + dyh][rows_at, :] = tmp[pl.ds(own, 64), :]
                    put_row(outs[3 * g + dyh], count * 64, tile, sums)
                    outs[3 * g + 2][dyh, rows_at, :] = tmp[pl.ds(other, 64), :]
                    put_row(outs[3 * g + 2].at[dyh], count * 64, tile, sums)

    def s_map(step, sc):
        z = sc[groups[0]]
        for g in range(1, n):
            z = jnp.where(step // count == g, sc[groups[g]], z)
        return (0, (step % count) * 4 + z)

    out_specs, out_shape = [], []
    for g in range(n):
        for shape in ((high, width), (high, width), (2, high, width)):
            out_specs.append(full(shape))
            out_shape.append(jax.ShapeDtypeStruct(shape, F32))
    flops = 6 * width * rows * 256 * count * n
    return pl.pallas_call(
        kernel,
        grid_spec=pltpu.PrefetchScalarGridSpec(
            num_scalar_prefetch=1,
            grid=(count * n,),
            in_specs=[full(th.shape)] * 2
            + [pl.BlockSpec((rows, 256), s_map)] * 2
            + [full(csum.shape)],
            out_specs=out_specs,
            scratch_shapes=[pltpu.VMEM((256, width), F32)],
        ),
        out_shape=out_shape,
        compiler_params=params(LIMIT),
        cost_estimate=pl.CostEstimate(
            flops=flops, bytes_accessed=4 * rows * 256 * count * n, transcendentals=0
        ),
        name="transposed_product",
    )(scal, th, tl, s_hi, s_lo, csum)


def direct_product(scal, ch, cl, s_hi, s_lo, th, tl, rsum, dyl, gram=None, base=None):
    cols, width = ch.shape
    count = s_hi.shape[0] // 512
    last = gram is not None

    high_rows = count * 64 + 8

    def kernel(sc, ch_ref, cl_ref, sh_ref, sl_ref, th_ref, tl_ref, rs_ref, *refs):
        if last:
            gram_ref, base_ref = refs[:2]
            outs, (eo_ref, ex_ref, tmp, acc) = refs[2:6], refs[6:]
        else:
            outs, (g_ref, tmp, acc) = refs[:4], refs[4:]
        step = pl.program_id(0)
        out = dot3(sh_ref[...], sl_ref[...], ch_ref[...], cl_ref[...])
        tmp[...] = out
        rows_at = pl.ds(pl.multiple_of(step * 64, 64), 64)

        @pl.when(step == 0)
        def _():
            for dx in range(4):
                outs[dx][count * 64 :, :] = jnp.zeros((8, width), F32)

        for dx in range(4):
            at = pl.multiple_of(sc[2 + dx] * 64, 64)
            outs[dx][rows_at, :] = tmp[pl.ds(at, 64), :]
            sums = rs_ref[step * 4 + sc[dyl] * 2 + sc[2 + dx] // 2]
            put_row(outs[dx], count * 64, step, sums)
        high, low = split(out)
        part = dot3(th_ref[...], tl_ref[...], high, low)

        @pl.when(step == 0)
        def _():
            acc[...] = (part + gram_ref[...]) if last else part

        @pl.when(step > 0)
        def _():
            acc[...] += part

        @pl.when(step == count - 1)
        def _():
            if last:
                total = acc[...]
                acc[...] = base_ref[...] - total - total.T
                half = width // 2
                eo_ref[...] = acc[pl.ds(pl.multiple_of(sc[6] * half, half), half), :]
                ex_ref[...] = acc[pl.ds(pl.multiple_of((1 - sc[6]) * half, half), half), :]
            else:
                g_ref[...] = acc[...]

    s_map = lambda step, sc: (step * 2 + sc[dyl], 0)
    t_map = lambda step, sc: (0, step * 2 + sc[dyl])
    args = [scal, ch, cl, s_hi, s_lo, th, tl, rsum]
    in_specs = (
        [full(ch.shape)] * 2
        + [pl.BlockSpec((256, cols), s_map)] * 2
        + [pl.BlockSpec((width, 256), t_map)] * 2
        + [full(rsum.shape)]
    )
    out_specs = [full((high_rows, width))] * 4
    out_shape = [jax.ShapeDtypeStruct((high_rows, width), F32)] * 4
    if last:
        args += [gram, base]
        in_specs += [full(gram.shape)] * 2
        out_specs += [full((width // 2, width))] * 2
        out_shape += [jax.ShapeDtypeStruct((width // 2, width), F32)] * 2
    else:
        out_specs += [full((width, width))]
        out_shape += [jax.ShapeDtypeStruct((width, width), F32)]
    flops = 6 * 256 * count * width * (cols + width)
    return pl.pallas_call(
        kernel,
        grid_spec=pltpu.PrefetchScalarGridSpec(
            num_scalar_prefetch=1,
            grid=(count,),
            in_specs=in_specs,
            out_specs=out_specs,
            scratch_shapes=[pltpu.VMEM((256, width), F32), pltpu.VMEM((width, width), F32)],
        ),
        out_shape=out_shape,
        compiler_params=params(LIMIT),
        cost_estimate=pl.CostEstimate(
            flops=flops, bytes_accessed=4 * 256 * cols * count, transcendentals=0
        ),
        name="direct_product",
    )(*args)


def hdot(a, b):
    return jnp.dot(a, b, precision=HIGH_PRECISION, preferred_element_type=F32)


def inverse_kernel(l_ref, bar_ref, inv_ref, invt_ref, c_ref):
    n = l_ref.shape[0]
    size = 128
    row = lax.broadcasted_iota(jnp.int32, (size, size), 0)
    col = lax.broadcasted_iota(jnp.int32, (size, size), 1)
    powers, results, scales = [], [], []
    for k in range(n // size):
        at = slice(k * size, (k + 1) * size)
        block = l_ref[at, at]
        diag = jnp.where(row == col, block, 0.0)
        by_row = 1.0 / diag.sum(1, keepdims=True)
        scales.append(1.0 / diag.sum(0, keepdims=True))
        nil = jnp.where(row > col, block, 0.0) * (-by_row)
        results.append(jnp.where(row == col, 1.0, 0.0) + nil)
        powers.append(nil)
    for _ in range(6):
        powers = [hdot(p, p) for p in powers]
        results = [r + hdot(r, p) for r, p in zip(results, powers)]
    inv_ref[...] = jnp.zeros_like(inv_ref)
    for k in range(n // size):
        at = slice(k * size, (k + 1) * size)
        inv_ref[at, at] = results[k] * scales[k]
    while size < n:
        for k in range(0, n, 2 * size):
            a, b = slice(k, k + size), slice(k + size, k + 2 * size)
            inv_ref[b, a] = -hdot(inv_ref[b, b], hdot(l_ref[b, a], inv_ref[a, a]))
        size *= 2
    invt_ref[...] = inv_ref[...].T
    c_ref[...] = hdot(l_ref[...].T, bar_ref[...])


def inverse(l11, l11_bar):
    out = jax.ShapeDtypeStruct(l11.shape, F32)
    return pl.pallas_call(
        inverse_kernel,
        out_shape=[out] * 3,
        compiler_params=pltpu.CompilerParams(vmem_limit_bytes=LIMIT * MIB),
        cost_estimate=pl.CostEstimate(flops=6 * 10**9, bytes_accessed=5 * MIB, transcendentals=0),
        name="inverse",
    )(l11, l11_bar)


def final_kernel(sc, own_ref, other_ref, c_ref, inv_ref, invt_ref, out_ref, x_ref):
    n = c_ref.shape[0]
    half = n // 2
    x_ref[pl.ds(pl.multiple_of(sc[0] * half, half), half), :] = own_ref[...]
    x_ref[pl.ds(pl.multiple_of((1 - sc[0]) * half, half), half), :] = other_ref[...]
    x = c_ref[...] - x_ref[...]
    row = lax.broadcasted_iota(jnp.int32, (n, n), 0)
    col = lax.broadcasted_iota(jnp.int32, (n, n), 1)
    p = jnp.where(row > col, x, jnp.where(row == col, 0.5 * x, 0.0))
    q = hdot(hdot(invt_ref[...], p), inv_ref[...])
    out_ref[...] = 0.5 * (q + q.T)


def final(scal, own, other, c, inv, invt):
    return pl.pallas_call(
        final_kernel,
        grid_spec=pltpu.PrefetchScalarGridSpec(
            num_scalar_prefetch=1,
            grid=(1,),
            in_specs=[full(own.shape)] * 2 + [full(c.shape)] * 3,
            out_specs=full(c.shape),
            scratch_shapes=[pltpu.VMEM(c.shape, F32)],
        ),
        out_shape=jax.ShapeDtypeStruct(c.shape, F32),
        compiler_params=params(LIMIT),
        name="diagonal_tile",
    )(scal, own, other, c, inv, invt)


def panel_kernel(sc, bar_ref, *refs):
    parts, (inv_ref, out_ref, rg_ref) = refs[:-3], refs[-3:]
    n = bar_ref.shape[0]
    total = parts[0][...]
    for part in parts[1:]:
        total = total + part[...]
    out_ref[...] = hdot(bar_ref[...] - total[:n, :], inv_ref[...])
    sums = total[n:, :128]
    sums = jnp.where(sc[0] == 1, sums[:, 64:], sums[:, :64])
    rg_ref[...] = sums[: rg_ref.shape[0], :]


def panel(scal, bar, parts, inv):
    n, width = bar.shape
    count = n // 64
    return pl.pallas_call(
        panel_kernel,
        grid_spec=pltpu.PrefetchScalarGridSpec(
            num_scalar_prefetch=1,
            grid=(1,),
            in_specs=[full(bar.shape)] + [full(p.shape) for p in parts] + [full(inv.shape)],
            out_specs=[full(bar.shape), full((count, 64))],
        ),
        out_shape=[
            jax.ShapeDtypeStruct(bar.shape, F32),
            jax.ShapeDtypeStruct((count, 64), F32),
        ],
        compiler_params=params(LIMIT),
        name="panel_tiles",
    )(scal, bar, *parts, inv)


def permutations():
    def make(move):
        pairs = []
        for z in range(4):
            for yh in range(2):
                for core in range(2):
                    for yl in range(2):
                        for x in range(4):
                            nz, nyh, nc, nyl, nx = move(z, yh, core, yl, x)
                            src = (z * 4 + yh * 2 + core) * 8 + yl * 4 + x
                            dst = (nz * 4 + nyh * 2 + nc) * 8 + nyl * 4 + nx
                            pairs.append((src, dst))
        return pairs

    perms = {
        "x+": make(lambda z, h, c, l, x: (z, h, c, l, (x + 1) % 4)),
        "x-": make(lambda z, h, c, l, x: (z, h, c, l, (x + 3) % 4)),
        "x2": make(lambda z, h, c, l, x: (z, h, c, l, (x + 2) % 4)),
        "z+": make(lambda z, h, c, l, x: ((z + 1) % 4, h, c, l, x)),
        "z-": make(lambda z, h, c, l, x: ((z + 3) % 4, h, c, l, x)),
        "z^1": make(lambda z, h, c, l, x: (z ^ 1, h, c, l, x)),
        "z^2": make(lambda z, h, c, l, x: (z ^ 2, h, c, l, x)),
        "z^3": make(lambda z, h, c, l, x: (z ^ 3, h, c, l, x)),
        "yl": make(lambda z, h, c, l, x: (z, h, c, 1 - l, x)),
        "yh": make(lambda z, h, c, l, x: (z, 1 - h, c, l, x)),
        "yhl": make(lambda z, h, c, l, x: (z, 1 - h, c, 1 - l, x)),
        "core": make(lambda z, h, c, l, x: (z, h, 1 - c, l, x)),
    }
    home = lambda z, h, c, l, x: ((z // 2) * 2 + l, x // 2, x % 2, z % 2, h * 2 + c)
    flip = lambda z, h, c, l, x: ((z // 2) * 2 + l, 1 - x // 2, x % 2, z % 2, h * 2 + c)
    perms["home0"] = make(home)
    perms["home1"] = make(flip)
    perms["back0"] = [(d, s) for s, d in perms["home0"]]
    perms["back1"] = [(d, s) for s, d in perms["home1"]]
    return perms


PERMS = permutations()


AXES = ("z", "yh", "core", "yl", "x")


def move(value, name):
    return lax.ppermute(value, AXES, PERMS[name])


def after(values, *deps):
    return lax.optimization_barrier((values, deps))[0]


def per_device(s_bar, l21, panel_column_cotangent, l11, l11_bar, coords, sigma, length, tile_block):
    z, yh, core, yl, x = (lax.axis_index(a) for a in AXES)
    row_id = z * 4 + yh * 2 + core
    col_id = yl * 4 + x
    count, _, width, tiles_c = s_bar.shape[:4]
    part = l21.shape[2]
    rows, cols = count * width, tiles_c * width
    own = l21.reshape(count, part, width)
    own_bar = panel_column_cotangent.reshape(count * part, width)
    ints = lambda vals: jnp.stack([jnp.asarray(v, jnp.int32) for v in vals])

    row_tiles = [i * 16 + row_id for i in range(count)]
    col_tiles = [j * 8 + col_id for j in range(tiles_c)]
    starts = jnp.take(tile_block, ints(row_tiles + col_tiles)) * width
    s_view = s_bar.reshape(rows * cols // 128, 128)
    sig, len_ = sigma.reshape(1, -1), length.reshape(1, -1)

    rw = {(0, 0): own}
    rw[1, 0] = move(own, "yl")
    rw[0, 3] = move(own, "x+")
    rw[0, 1] = move(own, "x-")
    cw = {(0, 0): move(own, "home0"), (1, 0): move(own, "home1")}

    bufs = prep(0, starts, s_view, coords, sig, len_, None, rows, cols)
    near, left = after((rw[1, 0], rw[0, 3]), bufs[3])
    rw[1, 3] = move(near, "x+")
    rw[1, 1] = move(near, "x-")
    rw[0, 2] = move(left, "x+")

    bufs = prep(1, after(starts, rw[1, 0]), s_view, coords, sig, len_, bufs, rows, cols)
    first = [after(cw[k, 0], bufs[3]) for k in range(2)]
    for k in range(2):
        cw[k, 3] = move(first[k], "z+")
        cw[k, 1] = move(first[k], "z-")
    rw[1, 2] = move(after(rw[1, 1], bufs[3]), "x-")
    cx = {(k, 0): move(first[k], "core") for k in range(2)}

    s_hi, s_lo, rsum, csum = prep(
        2, after(starts, first), s_view, coords, sig, len_, bufs, rows, cols
    )

    row_keys = [(a, b) for a in range(2) for b in range(4)]
    pos = ints([(yl ^ a) * 4 + (x + b) % 4 for a, b in row_keys])
    th, tl = assemble_rows(after(pos, csum), [rw[k] for k in row_keys])
    scal = ints(
        [(z + d) % 4 for d in range(4)]
        + [(yh ^ a) * 2 + (core ^ b) for a in range(2) for b in range(2)]
    )
    ta = {}

    def trans(th, groups):
        outs = trans_product(scal, th, tl, s_hi, s_lo, csum, groups)
        for g, dz in enumerate(groups):
            got = move(outs[3 * g + 2], "core")
            for k in range(2):
                ta[k, dz] = outs[3 * g + k] + got[k]
        return outs[0]

    mark = trans(th, (2,))
    second = {k: after(cw[k], mark) for k in ((0, 3), (1, 1), (0, 1), (1, 3))}
    cw[0, 2] = move(second[0, 3], "z+")
    cw[1, 2] = move(second[1, 1], "z-")
    for k, v in second.items():
        cx[k] = move(v, "core")
    mark = trans(after(th, mark), (1, 3))
    r1 = move(after(ta[0, 2], mark), "z+")
    r2 = move(after(ta[1, 2], mark), "z-")
    for k in range(2):
        cx[k, 2] = move(after(cw[k, 2], mark), "core")
    mark = trans(after(th, mark), (0,))
    s2 = move(after(ta[1, 1], mark), "z+")
    s4 = move(after(ta[0, 3], mark), "z-")
    s1 = move(ta[0, 1] + after(r1, mark), "z+")
    s3 = move(ta[1, 3] + after(r2, mark), "z-")

    col_keys = [(a, b) for a in range(2) for b in range(4)]
    pos = ints(
        [((z + b) % 4) * 4 + (yh ^ a) * 2 + core for a, b in col_keys]
        + [((z + b) % 4) * 4 + (yh ^ a) * 2 + (1 - core) for a, b in col_keys]
    )
    ch, cl = assemble_cols(
        after(pos, mark), [cw[k] for k in col_keys] + [cx[k] for k in col_keys]
    )
    base = lax.dot_general(
        own_bar,
        own.reshape(count * part, width),
        (((0,), (0,)), ((), ())),
        precision=HIGH_PRECISION,
        preferred_element_type=F32,
    )
    scal = ints([yl, 1 - yl] + [(x + d) % 4 for d in range(4)] + [core])
    y1 = direct_product(scal, ch, cl, s_hi, s_lo, th, tl, rsum, 1)
    gram = y1[4]
    t0 = move(after(ta[0, 0] + s1 + s4, gram), "back0")
    t1 = move(after(ta[1, 0] + s2 + s3, gram), "back1")
    r2 = move(y1[2], "x-")
    s2 = move(y1[1], "x+")
    y0 = direct_product(scal, ch, cl, s_hi, s_lo, th, tl, rsum, 0, gram, base)
    eo, ex = y0[4], y0[5]
    s3 = move(y1[3] + after(r2, eo), "x-")
    r1 = move(y0[2], "x+")
    s4 = move(y0[3], "x-")

    half = width // 2
    e = eo + move(ex, "core")
    others = ("z", "yh", "yl", "x")
    n_others = 64
    e = lax.all_to_all(e.reshape(n_others, -1, width), others, 0, 0).sum(0)
    s5 = move(y1[0] + s2 + s3, "yl")
    s1 = move(y0[1] + r1, "x+")
    inv, invt, c_mat = inverse(after(l11, eo), l11_bar)
    e = lax.all_to_all(jnp.broadcast_to(e[None], (n_others,) + e.shape), others, 0, 0)
    e = e.reshape(half, width)
    grad11 = final(ints([core]), e, move(e, "core"), c_mat, inv, invt)

    grad21, row_grad = panel(ints([x % 2]), own_bar, [y0[0], s1, s4, s5, t0, t1], inv)
    return (
        grad21.reshape(count, 1, part, width),
        grad11,
        row_grad.reshape(count, 1, part),
    )


def solution(mesh):
    fine = jax.sharding.Mesh(mesh.devices.reshape(4, 2, 2, 2, 4), AXES)
    prow, pcol = AXES[:3], AXES[3:]
    in_specs = (
        P(None, prow, None, None, pcol, None),
        P(None, prow, pcol, None),
        P(None, prow, pcol, None),
        P(),
        P(),
        P(),
        P(),
        P(),
        P(),
    )
    out_specs = (P(None, prow, pcol, None), P(), P(None, prow, pcol))
    return jax.shard_map(
        per_device, mesh=fine, in_specs=in_specs, out_specs=out_specs, check_vma=False
    )
```

```python
import math

import jax
import jax.numpy as jnp
from jax import lax
from jax.experimental import pallas as pl
from jax.experimental.pallas import tpu as pltpu
from jax.sharding import PartitionSpec as P

HIGH_PRECISION = lax.Precision.HIGHEST
F32 = jnp.float32
BF16 = jnp.bfloat16
SCALE = math.sqrt(12.0) * math.log2(math.e)
MIB = 1024 * 1024
LIMIT = 60


def params(mib, dims=1):
    return pltpu.CompilerParams(
        vmem_limit_bytes=mib * MIB, dimension_semantics=("arbitrary",) * dims
    )


def split(value):
    high = value.astype(BF16)
    low = (value - high.astype(F32)).astype(BF16)
    return high, low


def dot(a, b):
    return jnp.dot(a, b, preferred_element_type=F32)


def dot3(a_high, a_low, b_high, b_low):
    return dot(a_high, b_high) + dot(a_low, b_high) + dot(a_high, b_low)


def full(shape, **kw):
    return pl.BlockSpec(shape, lambda *_: (0,) * len(shape), **kw)


def once(shape):
    return full(shape, pipeline_mode=pl.Buffered(1))


ROWS = 128
GROUP = 16


def prep_kernel(first, starts, *refs):
    s_ref, co_ref, sg_ref, le_ref = refs[:4]
    hi_ref, lo_ref, rs_ref, cs_ref, cacc, feat, racc_ref = refs[-7:]
    step = pl.program_id(0)
    tiles_c = cs_ref.shape[0] // 4
    chunks = 4 * tiles_c
    block = first + step
    row_off = pl.multiple_of(starts[block // 4] + (block % 4) * ROWS, ROWS)

    @pl.when(step == 0)
    def _():
        cacc[...] = jnp.zeros_like(cacc)
        for j in range(tiles_c):
            off = pl.multiple_of(starts[3 + j], 512)
            for k in range(4):
                c = j * 4 + k
                at = pl.ds(pl.multiple_of(off + k * 128, 128), 128)
                feat[0, pl.ds(c, 1), :] = co_ref[0:1, at]
                feat[1, pl.ds(c, 1), :] = co_ref[1:2, at]
                feat[2, pl.ds(c, 1), :] = sg_ref[0:1, at]
                feat[3, pl.ds(c, 1), :] = le_ref[0:1, at] * (1.0 / SCALE)

    at = pl.ds(row_off, ROWS)

    def column(row):
        return jnp.broadcast_to(row, (ROWS, ROWS)).T

    racc_ref[1] = column(co_ref[0:1, at])
    racc_ref[2] = column(co_ref[1:2, at])
    racc_ref[3] = column(sg_ref[0:1, at])
    racc_ref[4] = column(le_ref[0:1, at] * (1.0 / SCALE))

    def body(g, _):
        base = pl.multiple_of(g * GROUP, GROUP)
        rows = pl.ds(base, GROUP)
        row_x, row_y, row_s, row_l = (racc_ref[k, rows, :] for k in range(1, 5))
        acc = jnp.zeros((GROUP, 128), F32)
        for c in range(chunks):
            s = s_ref[pl.ds(base * chunks + c, GROUP, stride=chunks), :]
            dx = row_x - feat[0, c : c + 1, :]
            dy = row_y - feat[1, c : c + 1, :]
            dist2 = dx * dx + dy * dy
            scale = row_l + feat[3, c : c + 1, :]
            g2 = dist2 * lax.rsqrt(jnp.maximum(dist2 * (scale * scale), 1e-30))
            weighted = s * ((1.0 + g2 * math.log(2.0)) * jnp.exp2(-g2))
            acc = acc + weighted * feat[2, c : c + 1, :]
            by_row = weighted * row_s
            cacc[c] += by_row.reshape(GROUP // 8, 8, 128).sum(0)
            high, low = split(s)
            hi_ref[rows, c * 128 : (c + 1) * 128] = high
            lo_ref[rows, c * 128 : (c + 1) * 128] = low
        racc_ref[0, rows, :] = acc * row_s
        return 0

    lax.fori_loop(0, ROWS // GROUP, body, 0)
    rs_ref[0] = racc_ref[0].T.sum(0, keepdims=True)

    @pl.when(step == pl.num_programs(0) - 1)
    def _():
        total = cacc[...].sum(1) * feat[2]
        cs_ref[...] = total if first == 0 else refs[7][...] + total


def prep(first, per, starts, s_view, coords, sigma, length, bufs, rows, cols):
    chunks = cols // 128
    any_spec = pl.BlockSpec(memory_space=pl.ANY)
    out_map = lambda s, st: (first + s, 0)
    args = [starts, s_view, coords, sigma, length]
    in_specs = [
        pl.BlockSpec((ROWS * chunks, 128), out_map),
        full(coords.shape),
        full(sigma.shape),
        full(length.shape),
    ]
    aliases = {}
    if first:
        args += list(bufs)
        in_specs += [any_spec, any_spec, any_spec, full((chunks, 128))]
        aliases = {5: 0, 6: 1, 7: 2}
    elements = per * ROWS * cols
    return pl.pallas_call(
        lambda *refs: prep_kernel(first, *refs),
        grid_spec=pltpu.PrefetchScalarGridSpec(
            num_scalar_prefetch=1,
            grid=(per,),
            in_specs=in_specs,
            out_specs=[
                pl.BlockSpec((ROWS, cols), out_map),
                pl.BlockSpec((ROWS, cols), out_map),
                pl.BlockSpec((1, 1, ROWS), lambda s, st: (first + s, 0, 0)),
                pl.BlockSpec((chunks, 128), lambda s, st: (0, 0)),
            ],
            scratch_shapes=[
                pltpu.VMEM((chunks, 8, 128), F32),
                pltpu.VMEM((4, chunks, 128), F32),
                pltpu.VMEM((5, ROWS, ROWS), F32),
            ],
        ),
        out_shape=[
            jax.ShapeDtypeStruct((rows, cols), BF16),
            jax.ShapeDtypeStruct((rows, cols), BF16),
            jax.ShapeDtypeStruct((rows // ROWS, 1, ROWS), F32),
            jax.ShapeDtypeStruct((chunks, 128), F32),
        ],
        input_output_aliases=aliases,
        compiler_params=params(LIMIT),
        cost_estimate=pl.CostEstimate(
            flops=6000 * elements, bytes_accessed=8 * elements, transcendentals=2 * elements
        ),
        name="kernel_sums",
    )(*args)


def put_row(ref, base, at, value):
    rows = pl.ds(base, 8)
    mask = lax.broadcasted_iota(jnp.int32, (8, 128), 0) == at
    ref[rows, :128] = jnp.where(mask, value, ref[rows, :128])


def trans_kernel(sc, *refs):
    pieces, (sh_ref, sl_ref, cs_ref) = refs[:8], refs[8:11]
    own_ref, first_ref, other_ref, tth_ref, ttl_ref, tmp, rows_ref, th_ref, tl_ref = refs[11:]
    count, part, width = pieces[0].shape
    step = pl.program_id(0)
    tile = step % count

    @pl.when(step == 0)
    def _():
        for r in range(8):
            for i in range(count):
                at = pl.multiple_of(i * 512 + sc[9 + r] * part, part)
                rows_ref[pl.ds(at, part), :] = pieces[r][i]
        for k in range(count * 4):
            at = slice(k * 128, (k + 1) * 128)
            high, low = split(rows_ref[at, :].T)
            th_ref[:, at] = high
            tl_ref[:, at] = low

    out = dot3(th_ref[...], tl_ref[...], sh_ref[...], sl_ref[...])
    high, low = split(out)
    tth_ref[...] = high
    ttl_ref[...] = low
    tmp[...] = out.T
    rows_at = pl.ds(pl.multiple_of(tile * part, part), part)
    base = count * part

    group = step // count
    zp = sc[group]

    def store(ref, dyh, dcore):
        sub = sc[4 + dyh * 2 + dcore]

        @pl.when(tile == 0)
        def _():
            ref[dyh, base:, :] = jnp.zeros((8, width), F32)

        ref[dyh, rows_at, :] = tmp[pl.ds(pl.multiple_of(sub * part, part), part), :]
        sums = cs_ref[pl.ds(tile * 8 + zp * 2 + sub // 2, 1), :]
        put_row(ref.at[dyh], base, tile, sums)

    for dyh in range(2):
        store(own_ref, dyh, 0)

    @pl.when(group == 0)
    def _():
        for dyh in range(2):
            store(first_ref, dyh, 1)

    @pl.when(group > 0)
    def _():
        for dyh in range(2):
            store(other_ref, dyh, 1)


def trans_product(scal, pieces, s_hi, s_lo, csum):
    count, part, width = pieces[0].shape
    rows, cols = s_hi.shape
    high = count * part + 8
    s_map = lambda step, sc: (0, step % count * 4 + sc[step // count])
    o_spec = pl.BlockSpec((2, high, width), lambda step, sc: (step // count, 0, 0))
    r_spec = pl.BlockSpec(
        (2, high, width), lambda step, sc: (jnp.maximum(step // count - 1, 0), 0, 0)
    )
    t_spec = pl.BlockSpec((width, 256), s_map)
    return pl.pallas_call(
        trans_kernel,
        grid_spec=pltpu.PrefetchScalarGridSpec(
            num_scalar_prefetch=1,
            grid=(4 * count,),
            in_specs=[once(p.shape) for p in pieces]
            + [pl.BlockSpec((rows, 256), s_map)] * 2
            + [full(csum.shape)],
            out_specs=[o_spec, full((2, high, width)), r_spec] + [t_spec] * 2,
            scratch_shapes=[
                pltpu.VMEM((256, width), F32),
                pltpu.VMEM((rows, width), F32),
                pltpu.VMEM((width, rows), BF16),
                pltpu.VMEM((width, rows), BF16),
            ],
        ),
        out_shape=[jax.ShapeDtypeStruct((k, high, width), F32) for k in (8, 2, 6)]
        + [jax.ShapeDtypeStruct((width, cols), BF16)] * 2,
        compiler_params=params(LIMIT),
        cost_estimate=pl.CostEstimate(
            flops=10 * width * rows * cols, bytes_accessed=4 * rows * cols, transcendentals=0
        ),
        name="transposed_product",
    )(scal, *pieces, s_hi, s_lo, csum)


def lower_blocks(n):
    return [(i, j) for i in range(n // 128) for j in range(i + 1)]


def cols_kernel(sc, *refs):
    own_ref, other_ref, tth_ref, ttl_ref, base_ref = refs[:5]
    h_ref, l_ref, eo_ref, ex_ref, acc, packed = refs[5:]
    _, _, part, width = own_ref.shape
    step = pl.program_id(0)
    for ref, core in ((own_ref, sc[0]), (other_ref, 1 - sc[0])):
        for g in range(ref.shape[0]):
            at = pl.ds(pl.multiple_of((g * 2 + core) * part, part), part)
            high, low = split(ref[g, 0])
            h_ref[at, :] = high
            l_ref[at, :] = low
    gram = dot3(tth_ref[...], ttl_ref[...], h_ref[...], l_ref[...])

    @pl.when(step == 0)
    def _():
        acc[...] = gram

    @pl.when(step > 0)
    def _():
        acc[...] += gram

    @pl.when(step == pl.num_programs(0) - 1)
    def _():
        total = acc[...]
        acc[...] = base_ref[...] - total - total.T
        for k, (i, j) in enumerate(lower_blocks(width)):
            packed[k * 128 : (k + 1) * 128, :] = acc[
                i * 128 : (i + 1) * 128, j * 128 : (j + 1) * 128
            ]
        half = packed.shape[0] // 2
        eo_ref[...] = packed[pl.ds(pl.multiple_of(sc[0] * half, half), half), :]
        ex_ref[...] = packed[pl.ds(pl.multiple_of((1 - sc[0]) * half, half), half), :]


def assemble_cols(scal, own, other, tth, ttl, base):
    groups, count, part, width = own.shape
    per = part * groups * 2
    packed = len(lower_blocks(width)) * 128
    block = pl.BlockSpec((per, width), lambda i, sc: (i, 0))
    return pl.pallas_call(
        cols_kernel,
        grid_spec=pltpu.PrefetchScalarGridSpec(
            num_scalar_prefetch=1,
            grid=(count,),
            in_specs=[pl.BlockSpec((groups, 1, part, width), lambda i, sc: (0, i, 0, 0))] * 2
            + [pl.BlockSpec((width, per), lambda i, sc: (0, i))] * 2
            + [full(base.shape)],
            out_specs=[block] * 2 + [full((packed // 2, 128))] * 2,
            scratch_shapes=[pltpu.VMEM((width, width), F32), pltpu.VMEM((packed, 128), F32)],
        ),
        out_shape=[jax.ShapeDtypeStruct((count * per, width), BF16)] * 2
        + [jax.ShapeDtypeStruct((packed // 2, 128), F32)] * 2,
        compiler_params=params(LIMIT),
        cost_estimate=pl.CostEstimate(
            flops=6 * width * width * per * count, bytes_accessed=12 * width * per * count, transcendentals=0
        ),
        name="column_panels",
    )(scal, own, other, tth, ttl, base)


def direct_product(scal, ch, cl, s_hi, s_lo, rsum, offsets):
    cols, width = ch.shape
    rows = s_hi.shape[0]
    count = rows // 512
    deep = 1024
    part = 64
    keys = [(dx, dyl, i) for dx in offsets for dyl in range(2) for i in range(count)]
    n = len(keys)
    high = count * part + 8

    def kernel(sc, ch_ref, cl_ref, rs_ref, *refs):
        s_high = jnp.concatenate([r[...] for r in refs[:n]], 0)
        s_low = jnp.concatenate([r[...] for r in refs[n : 2 * n]], 0)
        outs, acc = refs[2 * n : -1], refs[-1]
        step = pl.program_id(0)
        out = dot3(s_high, s_low, ch_ref[...], cl_ref[...])

        @pl.when(step == 0)
        def _():
            acc[...] = out

        @pl.when(step > 0)
        def _():
            acc[...] += out

        @pl.when(step == pl.num_programs(0) - 1)
        def _():
            for k, dx in enumerate(offsets):
                for dyl in range(2):
                    dst = outs[2 * k + dyl]
                    at = (2 * k + dyl) * count * part
                    dst[: count * part, :] = acc[at : at + count * part, :]
                    dst[count * part :, :] = jnp.zeros((8, width), F32)
                    for i in range(count):
                        row = slice(count * part + i, count * part + i + 1)
                        dst[row, :128] = rs_ref[i * 4 + sc[dyl] * 2 + sc[2 + dx] // 2]

    def s_spec(key):
        dx, dyl, i = key
        return pl.BlockSpec((part, deep), lambda k, sc: (i * 8 + sc[dyl] * 4 + sc[2 + dx], k))

    l_spec = pl.BlockSpec((deep, width), lambda k, sc: (k, 0))
    shapes = [(high, width)] * (2 * len(offsets))
    return pl.pallas_call(
        kernel,
        grid_spec=pltpu.PrefetchScalarGridSpec(
            num_scalar_prefetch=1,
            grid=(cols // deep,),
            in_specs=[l_spec, l_spec, full(rsum.shape)] + [s_spec(k) for k in keys] * 2,
            out_specs=[full(shape) for shape in shapes],
            scratch_shapes=[pltpu.VMEM((n * part, width), F32)],
        ),
        out_shape=[jax.ShapeDtypeStruct(shape, F32) for shape in shapes],
        compiler_params=params(LIMIT),
        cost_estimate=pl.CostEstimate(
            flops=8 * n * part * width * cols, bytes_accessed=4 * n * part * cols, transcendentals=0
        ),
        name="direct_product",
    )(scal, ch, cl, rsum, *[s_hi] * n, *[s_lo] * n)


def hdot(a, b):
    return jnp.dot(a, b, precision=HIGH_PRECISION, preferred_element_type=F32)


def inverse_kernel(l_ref, bar_ref, inv_ref, invt_ref, c_ref):
    n = l_ref.shape[0]
    size = 128
    row = lax.broadcasted_iota(jnp.int32, (size, size), 0)
    col = lax.broadcasted_iota(jnp.int32, (size, size), 1)
    powers, results, scales = [], [], []
    for k in range(n // size):
        at = slice(k * size, (k + 1) * size)
        block = l_ref[at, at]
        diag = jnp.where(row == col, block, 0.0)
        by_row = 1.0 / diag.sum(1, keepdims=True)
        scales.append(1.0 / diag.sum(0, keepdims=True))
        nil = jnp.where(row > col, block, 0.0) * (-by_row)
        results.append(jnp.where(row == col, 1.0, 0.0) + nil)
        powers.append(nil)
    for _ in range(6):
        powers = [hdot(p, p) for p in powers]
        results = [r + hdot(r, p) for r, p in zip(results, powers)]
    inv_ref[...] = jnp.zeros_like(inv_ref)
    for k in range(n // size):
        at = slice(k * size, (k + 1) * size)
        inv_ref[at, at] = results[k] * scales[k]
    while size < n:
        for k in range(0, n, 2 * size):
            a, b = slice(k, k + size), slice(k + size, k + 2 * size)
            inv_ref[b, a] = -hdot(inv_ref[b, b], hdot(l_ref[b, a], inv_ref[a, a]))
        size *= 2
    invt_ref[...] = inv_ref[...].T
    c_ref[...] = hdot(l_ref[...].T, bar_ref[...])


def inverse(l11, l11_bar):
    out = jax.ShapeDtypeStruct(l11.shape, F32)
    return pl.pallas_call(
        inverse_kernel,
        out_shape=[out] * 3,
        compiler_params=pltpu.CompilerParams(vmem_limit_bytes=LIMIT * MIB),
        cost_estimate=pl.CostEstimate(flops=6 * 10**9, bytes_accessed=5 * MIB, transcendentals=0),
        name="inverse",
    )(l11, l11_bar)


def final_kernel(sc, own_ref, other_ref, c_ref, inv_ref, invt_ref, out_ref, packed, p_ref):
    n = c_ref.shape[0]
    half = packed.shape[0] // 2
    packed[pl.ds(pl.multiple_of(sc[0] * half, half), half), :] = own_ref[...]
    packed[pl.ds(pl.multiple_of((1 - sc[0]) * half, half), half), :] = other_ref[...]
    p_ref[...] = jnp.zeros_like(p_ref)
    row = lax.broadcasted_iota(jnp.int32, (128, 128), 0)
    col = lax.broadcasted_iota(jnp.int32, (128, 128), 1)
    for k, (i, j) in enumerate(lower_blocks(n)):
        at = (slice(i * 128, (i + 1) * 128), slice(j * 128, (j + 1) * 128))
        x = c_ref[at] - packed[k * 128 : (k + 1) * 128, :]
        if i == j:
            x = jnp.where(row > col, x, jnp.where(row == col, 0.5 * x, 0.0))
        p_ref[at] = x
    q = hdot(hdot(invt_ref[...], p_ref[...]), inv_ref[...])
    out_ref[...] = 0.5 * (q + q.T)


def final(scal, own, other, c, inv, invt):
    return pl.pallas_call(
        final_kernel,
        grid_spec=pltpu.PrefetchScalarGridSpec(
            num_scalar_prefetch=1,
            grid=(1,),
            in_specs=[full(own.shape)] * 2 + [full(c.shape)] * 3,
            out_specs=full(c.shape),
            scratch_shapes=[
                pltpu.VMEM((2 * own.shape[0], own.shape[1]), F32),
                pltpu.VMEM(c.shape, F32),
            ],
        ),
        out_shape=jax.ShapeDtypeStruct(c.shape, F32),
        compiler_params=params(LIMIT),
        name="diagonal_tile",
    )(scal, own, other, c, inv, invt)


def panel_kernel(sc, bar_ref, inv_ref, *refs):
    parts, (out_ref, rg_ref) = refs[:-2], refs[-2:]
    n = bar_ref.shape[0]
    total = parts[0][...]
    for part in parts[1:]:
        total = total + part[...]
    out_ref[...] = hdot(bar_ref[...] - total[:n, :], inv_ref[...])
    sums = total[n:, :128]
    sums = jnp.where(sc[0] == 1, sums[:, 64:], sums[:, :64])
    rg_ref[...] = sums[: rg_ref.shape[0], :]


def panel(scal, bar, inv, parts):
    n, width = bar.shape
    return pl.pallas_call(
        panel_kernel,
        grid_spec=pltpu.PrefetchScalarGridSpec(
            num_scalar_prefetch=1,
            grid=(1,),
            in_specs=[full(bar.shape), full(inv.shape)] + [full(p.shape) for p in parts],
            out_specs=[full(bar.shape), full((n // 64, 64))],
        ),
        out_shape=[
            jax.ShapeDtypeStruct(bar.shape, F32),
            jax.ShapeDtypeStruct((n // 64, 64), F32),
        ],
        compiler_params=params(LIMIT),
        name="panel_tiles",
    )(scal, bar, inv, *parts)


def permutations():
    def make(move):
        pairs = []
        for z in range(4):
            for yh in range(2):
                for core in range(2):
                    for yl in range(2):
                        for x in range(4):
                            nz, nyh, nc, nyl, nx = move(z, yh, core, yl, x)
                            src = (z * 4 + yh * 2 + core) * 8 + yl * 4 + x
                            dst = (nz * 4 + nyh * 2 + nc) * 8 + nyl * 4 + nx
                            pairs.append((src, dst))
        return pairs

    perms = {
        "x+": make(lambda z, h, c, l, x: (z, h, c, l, (x + 1) % 4)),
        "x-": make(lambda z, h, c, l, x: (z, h, c, l, (x + 3) % 4)),
        "x2": make(lambda z, h, c, l, x: (z, h, c, l, (x + 2) % 4)),
        "z+": make(lambda z, h, c, l, x: ((z + 1) % 4, h, c, l, x)),
        "z-": make(lambda z, h, c, l, x: ((z + 3) % 4, h, c, l, x)),
        "z^1": make(lambda z, h, c, l, x: (z ^ 1, h, c, l, x)),
        "z^2": make(lambda z, h, c, l, x: (z ^ 2, h, c, l, x)),
        "z^3": make(lambda z, h, c, l, x: (z ^ 3, h, c, l, x)),
        "yl": make(lambda z, h, c, l, x: (z, h, c, 1 - l, x)),
        "yh": make(lambda z, h, c, l, x: (z, 1 - h, c, l, x)),
        "yhl": make(lambda z, h, c, l, x: (z, 1 - h, c, 1 - l, x)),
        "core": make(lambda z, h, c, l, x: (z, h, 1 - c, l, x)),
    }
    home = lambda z, h, c, l, x: ((z // 2) * 2 + l, x // 2, x % 2, z % 2, h * 2 + c)
    flip = lambda z, h, c, l, x: ((z // 2) * 2 + l, 1 - x // 2, x % 2, z % 2, h * 2 + c)
    perms["home0"] = make(home)
    perms["home1"] = make(flip)
    perms["back0"] = [(d, s) for s, d in perms["home0"]]
    perms["back1"] = [(d, s) for s, d in perms["home1"]]
    return perms


PERMS = permutations()


AXES = ("z", "yh", "core", "yl", "x")


def move(value, name):
    return lax.ppermute(value, AXES, PERMS[name])


def after(values, *deps):
    return lax.optimization_barrier((values, deps))[0]


def per_device(s_bar, l21, panel_column_cotangent, l11, l11_bar, coords, sigma, length, tile_block):
    z, yh, core, yl, x = (lax.axis_index(a) for a in AXES)
    row_id = z * 4 + yh * 2 + core
    col_id = yl * 4 + x
    count, _, width, tiles_c = s_bar.shape[:4]
    part = l21.shape[2]
    rows, cols = count * width, tiles_c * width
    own = l21.reshape(count, part, width)
    own_bar = panel_column_cotangent.reshape(count * part, width)
    ints = lambda vals: jnp.stack([jnp.asarray(v, jnp.int32) for v in vals])

    row_tiles = [i * 16 + row_id for i in range(count)]
    col_tiles = [j * 8 + col_id for j in range(tiles_c)]
    starts = jnp.take(tile_block, ints(row_tiles + col_tiles)) * width
    s_view = s_bar.reshape(rows * cols // 128, 128)
    sig, len_ = sigma.reshape(1, -1), length.reshape(1, -1)

    rw = {(0, 0): own}
    rw[1, 0] = move(own, "yl")
    rw[0, 3] = move(own, "x+")
    rw[0, 1] = move(own, "x-")
    home = move(own, "home0")

    part_blocks = rows // ROWS // 2
    feats = (s_view, coords, sig, len_)
    bufs = prep(0, part_blocks, starts, *feats, None, rows, cols)
    near, left, right, home = after((rw[1, 0], rw[0, 3], rw[0, 1], home), bufs[3])
    rw[0, 1] = right
    starts = after(starts, near, left, right, home)
    col_own = lax.all_gather(home, ("z", "yh"))
    rw[1, 3] = move(near, "x+")
    rw[1, 1] = move(near, "x-")
    rw[0, 2] = move(left, "x+")
    s_hi, s_lo, rsum, csum = prep(part_blocks, part_blocks, starts, *feats, bufs, rows, cols)
    rw[1, 2] = move(after(rw[1, 1], csum), "x-")

    row_keys = [(a, b) for a in range(2) for b in range(4)]
    scal = ints(
        [(z + d) % 4 for d in (2, 1, 3, 0)]
        + [(yh ^ a) * 2 + (core ^ b) for a in range(2) for b in range(2)]
        + [0]
        + [(yl ^ a) * 4 + (x + b) % 4 for a, b in row_keys]
    )
    own_t, first_t, other_t, tth, ttl = trans_product(
        after(scal, csum), [rw[k] for k in row_keys], s_hi, s_lo, csum
    )
    got = move(first_t, "core")
    more = move(other_t, "core")
    col_other = move(after(col_own, tth), "core")
    base = lax.dot_general(
        after(own_bar, tth),
        own.reshape(count * part, width),
        (((0,), (0,)), ((), ())),
        precision=HIGH_PRECISION,
        preferred_element_type=F32,
    )
    inv, invt, c_mat = inverse(after(l11, tth), l11_bar)
    got, more = after((got, more), inv)
    t_r1 = move(own_t[0] + got[0], "z+")
    t_r2 = move(own_t[1] + got[1], "z-")
    t_u1 = move(own_t[3] + more[1], "z+")
    t_d0 = move(own_t[4] + more[2], "z-")

    ch, cl, eo, ex = assemble_cols(
        after(ints([core]), inv), col_own, col_other, tth, ttl, base
    )
    others, n_others = ("z", "yh", "yl", "x"), 64
    e = eo + move(ex, "core")
    e = e.reshape(n_others, -1, 128)
    t_u0 = move(own_t[2] + more[0] + after(t_r1, eo), "z+")
    t_d1 = move(own_t[5] + more[3] + after(t_r2, eo), "z-")

    scal = ints([yl, 1 - yl] + [(x + d) % 4 for d in range(4)])
    y20, y21 = direct_product(after(scal, e), ch, cl, s_hi, s_lo, rsum, (2,))
    e = lax.all_to_all(e, others, 0, 0).sum(0)
    y_r1 = move(y20, "x+")
    y_r2 = move(y21, "x-")
    scal = after(scal, y20, e)
    outs = direct_product(scal, ch, cl, s_hi, s_lo, rsum, (1, 3, 0))
    y10, y11, y30, y31, y00, y01 = outs
    y_u1 = move(y11, "x+")
    y_d1 = move(y31 + after(y_r2, y10), "x-")
    y_u0 = move(y10 + after(y_r1, y10), "x+")
    y_d0 = move(y30, "x-")
    t_u0, t_u1, t_d0, t_d1 = after((t_u0, t_u1, t_d0, t_d1), y20)
    t0 = move(own_t[6] + more[4] + t_u0 + t_d0, "back0")
    t1 = move(own_t[7] + more[5] + t_u1 + t_d1, "back1")
    e = after(e, y10)
    e = lax.all_to_all(jnp.broadcast_to(e[None], (n_others,) + e.shape), others, 0, 0)
    y_near = move(y01 + y_u1 + y_d1, "yl")

    e = e.reshape(eo.shape)
    grad11 = final(ints([core]), e, move(e, "core"), c_mat, inv, invt)
    grad21, row_grad = panel(ints([x % 2]), own_bar, inv, [y00, y_u0, y_d0, y_near, t0, t1])
    return (
        grad21.reshape(count, 1, part, width),
        grad11,
        row_grad.reshape(count, 1, part),
    )


def solution(mesh):
    fine = jax.sharding.Mesh(mesh.devices.reshape(4, 2, 2, 2, 4), AXES)
    prow, pcol = AXES[:3], AXES[3:]
    in_specs = (
        P(None, prow, None, None, pcol, None),
        P(None, prow, pcol, None),
        P(None, prow, pcol, None),
        P(),
        P(),
        P(),
        P(),
        P(),
        P(),
    )
    out_specs = (P(None, prow, pcol, None), P(), P(None, prow, pcol))
    return jax.shard_map(
        per_device, mesh=fine, in_specs=in_specs, out_specs=out_specs, check_vma=False
    )
```

```python
import math

import jax
import jax.numpy as jnp
from jax import lax
from jax.experimental import pallas as pl
from jax.experimental.pallas import tpu as pltpu
from jax.sharding import PartitionSpec as P

HIGH_PRECISION = lax.Precision.HIGHEST
F32 = jnp.float32
BF16 = jnp.bfloat16
SCALE = math.sqrt(12.0) * math.log2(math.e)
MIB = 1024 * 1024
LIMIT = 60


def params(mib, dims=1):
    return pltpu.CompilerParams(
        vmem_limit_bytes=mib * MIB, dimension_semantics=("arbitrary",) * dims
    )


def split(value):
    high = value.astype(BF16)
    low = (value - high.astype(F32)).astype(BF16)
    return high, low


def dot(a, b):
    return jnp.dot(a, b, preferred_element_type=F32)


def dot3(a_high, a_low, b_high, b_low):
    return dot(a_high, b_high) + dot(a_low, b_high) + dot(a_high, b_low)


def full(shape, **kw):
    return pl.BlockSpec(shape, lambda *_: (0,) * len(shape), **kw)


def once(shape):
    return full(shape, pipeline_mode=pl.Buffered(1))


ROWS = 128
GROUP = 16


def prep_kernel(first, starts, *refs):
    s_ref, co_ref, sg_ref, le_ref = refs[:4]
    hi_ref, lo_ref, rs_ref, cs_ref, cacc, feat, racc_ref = refs[-7:]
    step = pl.program_id(0)
    tiles_c = cs_ref.shape[0] // 4
    chunks = 4 * tiles_c
    block = first + step
    row_off = pl.multiple_of(starts[block // 4] + (block % 4) * ROWS, ROWS)

    @pl.when(step == 0)
    def _():
        cacc[...] = jnp.zeros_like(cacc)
        for j in range(tiles_c):
            off = pl.multiple_of(starts[3 + j], 512)
            for k in range(4):
                c = j * 4 + k
                at = pl.ds(pl.multiple_of(off + k * 128, 128), 128)
                feat[0, pl.ds(c, 1), :] = co_ref[0:1, at]
                feat[1, pl.ds(c, 1), :] = co_ref[1:2, at]
                feat[2, pl.ds(c, 1), :] = sg_ref[0:1, at]
                feat[3, pl.ds(c, 1), :] = le_ref[0:1, at] * (1.0 / SCALE)

    at = pl.ds(row_off, ROWS)

    def column(row):
        return jnp.broadcast_to(row, (ROWS, ROWS)).T

    racc_ref[1] = column(co_ref[0:1, at])
    racc_ref[2] = column(co_ref[1:2, at])
    racc_ref[3] = column(sg_ref[0:1, at])
    racc_ref[4] = column(le_ref[0:1, at] * (1.0 / SCALE))

    def body(g, _):
        base = pl.multiple_of(g * GROUP, GROUP)
        rows = pl.ds(base, GROUP)
        row_x, row_y, row_s, row_l = (racc_ref[k, rows, :] for k in range(1, 5))
        acc = jnp.zeros((GROUP, 128), F32)
        for c in range(chunks):
            s = s_ref[pl.ds(base * chunks + c, GROUP, stride=chunks), :]
            dx = row_x - feat[0, c : c + 1, :]
            dy = row_y - feat[1, c : c + 1, :]
            dist2 = dx * dx + dy * dy
            scale = row_l + feat[3, c : c + 1, :]
            g2 = dist2 * lax.rsqrt(jnp.maximum(dist2 * (scale * scale), 1e-30))
            weighted = s * ((1.0 + g2 * math.log(2.0)) * jnp.exp2(-g2))
            acc = acc + weighted * feat[2, c : c + 1, :]
            by_row = weighted * row_s
            cacc[c] += by_row.reshape(GROUP // 8, 8, 128).sum(0)
            high, low = split(s)
            hi_ref[rows, c * 128 : (c + 1) * 128] = high
            lo_ref[rows, c * 128 : (c + 1) * 128] = low
        racc_ref[0, rows, :] = acc * row_s
        return 0

    lax.fori_loop(0, ROWS // GROUP, body, 0)
    rs_ref[0] = racc_ref[0].T.sum(0, keepdims=True)

    @pl.when(step == pl.num_programs(0) - 1)
    def _():
        total = cacc[...].sum(1) * feat[2]
        cs_ref[...] = total if first == 0 else refs[7][...] + total


def prep(first, per, starts, s_view, coords, sigma, length, bufs, rows, cols):
    chunks = cols // 128
    any_spec = pl.BlockSpec(memory_space=pl.ANY)
    out_map = lambda s, st: (first + s, 0)
    args = [starts, s_view, coords, sigma, length]
    in_specs = [
        pl.BlockSpec((ROWS * chunks, 128), out_map),
        full(coords.shape),
        full(sigma.shape),
        full(length.shape),
    ]
    aliases = {}
    if first:
        args += list(bufs)
        in_specs += [any_spec, any_spec, any_spec, full((chunks, 128))]
        aliases = {5: 0, 6: 1, 7: 2}
    elements = per * ROWS * cols
    return pl.pallas_call(
        lambda *refs: prep_kernel(first, *refs),
        grid_spec=pltpu.PrefetchScalarGridSpec(
            num_scalar_prefetch=1,
            grid=(per,),
            in_specs=in_specs,
            out_specs=[
                pl.BlockSpec((ROWS, cols), out_map),
                pl.BlockSpec((ROWS, cols), out_map),
                pl.BlockSpec((1, 1, ROWS), lambda s, st: (first + s, 0, 0)),
                pl.BlockSpec((chunks, 128), lambda s, st: (0, 0)),
            ],
            scratch_shapes=[
                pltpu.VMEM((chunks, 8, 128), F32),
                pltpu.VMEM((4, chunks, 128), F32),
                pltpu.VMEM((5, ROWS, ROWS), F32),
            ],
        ),
        out_shape=[
            jax.ShapeDtypeStruct((rows, cols), BF16),
            jax.ShapeDtypeStruct((rows, cols), BF16),
            jax.ShapeDtypeStruct((rows // ROWS, 1, ROWS), F32),
            jax.ShapeDtypeStruct((chunks, 128), F32),
        ],
        input_output_aliases=aliases,
        compiler_params=params(LIMIT),
        cost_estimate=pl.CostEstimate(
            flops=6000 * elements, bytes_accessed=8 * elements, transcendentals=2 * elements
        ),
        name="kernel_sums",
    )(*args)


def put_row(ref, base, at, value):
    rows = pl.ds(base, 8)
    mask = lax.broadcasted_iota(jnp.int32, (8, 128), 0) == at
    ref[rows, :128] = jnp.where(mask, value, ref[rows, :128])


def trans_kernel(sc, *refs):
    pieces, refs = refs[:8], refs[8:]
    count, part, width = pieces[0].shape
    s_high, s_low, cs_ref = refs[:count], refs[count : 2 * count], refs[2 * count]
    own_ref, other_ref, th_ref, tl_ref, rows_ref = refs[2 * count + 1 : -count]
    tmps = refs[-count:]
    zp = pl.program_id(0)
    base = count * part

    @pl.when(zp == 0)
    def _():
        for r in range(8):
            for i in range(count):
                at = pl.multiple_of(i * 512 + sc[4 + r] * part, part)
                rows_ref[pl.ds(at, part), :] = pieces[r][i]
        for k in range(count * 4):
            at = slice(k * 128, (k + 1) * 128)
            high, low = split(rows_ref[at, :].T)
            th_ref[:, at] = high
            tl_ref[:, at] = low

    for i in range(count):
        out = dot3(th_ref[...], tl_ref[...], s_high[i][...], s_low[i][...])
        tmps[i][...] = out.T
    for ref, dcore in ((own_ref, 0), (other_ref, 1)):
        for dyh in range(2):
            sub = sc[dyh * 2 + dcore]
            at = pl.ds(pl.multiple_of(sub * part, part), part)
            ref[dyh, base:, :] = jnp.zeros((8, width), F32)
            for i in range(count):
                ref[dyh, i * part : (i + 1) * part, :] = tmps[i][at, :]
                ref[dyh, base + i : base + i + 1, :128] = cs_ref[
                    pl.ds(i * 8 + zp * 2 + sub // 2, 1), :
                ]


def trans_product(scal, pieces, s_hi, s_lo, csum):
    count, part, width = pieces[0].shape
    rows, cols = s_hi.shape
    high = count * part + 8
    s_specs = [
        pl.BlockSpec((rows, 256), lambda step, sc, i=i: (0, i * 4 + step)) for i in range(count)
    ]
    o_spec = pl.BlockSpec((2, high, width), lambda step, sc: (step, 0, 0))
    return pl.pallas_call(
        trans_kernel,
        grid_spec=pltpu.PrefetchScalarGridSpec(
            num_scalar_prefetch=1,
            grid=(4,),
            in_specs=[once(p.shape) for p in pieces] + s_specs * 2 + [full(csum.shape)],
            out_specs=[o_spec] * 2 + [full((width, rows))] * 2,
            scratch_shapes=[pltpu.VMEM((rows, width), F32)]
            + [pltpu.VMEM((256, width), F32)] * count,
        ),
        out_shape=[jax.ShapeDtypeStruct((8, high, width), F32)] * 2
        + [jax.ShapeDtypeStruct((width, rows), BF16)] * 2,
        compiler_params=params(LIMIT),
        cost_estimate=pl.CostEstimate(
            flops=10 * width * rows * cols, bytes_accessed=4 * rows * cols, transcendentals=0
        ),
        name="transposed_product",
    )(scal, *pieces, *[s_hi] * count, *[s_lo] * count, csum)


def lower_blocks(n):
    return [(i, j) for i in range(n // 128) for j in range(i + 1)]


def direct_kernel(sc, own_ref, other_ref, sh_ref, sl_ref, th_ref, tl_ref, rs_ref, base_ref, *refs):
    y_ref, eo_ref, ex_ref, ch_ref, cl_ref, acc, packed = refs
    groups, count, part, width = own_ref.shape
    step = pl.program_id(0)
    tile = step % count
    base = count * part

    @pl.when(step == 0)
    def _():
        for ref, core in ((own_ref, sc[0]), (other_ref, 1 - sc[0])):
            for g in range(groups):
                for i in range(count):
                    at = pl.multiple_of(i * 1024 + (g * 2 + core) * part, part)
                    high, low = split(ref[g, i])
                    ch_ref[pl.ds(at, part), :] = high
                    cl_ref[pl.ds(at, part), :] = low

    out = dot3(sh_ref[...], sl_ref[...], ch_ref[...], cl_ref[...])
    high, low = split(out)
    gram = dot3(th_ref[...], tl_ref[...], high, low)
    rows_at = pl.ds(pl.multiple_of(tile * part, part), part)

    @pl.when(tile == 0)
    def _():
        y_ref[:, base:, :] = jnp.zeros((4, 8, width), F32)

    for x in range(4):
        y_ref[x, rows_at, :] = out[x * part : (x + 1) * part, :]
        put_row(y_ref.at[x], base, tile, rs_ref[tile * 4 + step // count * 2 + x // 2])

    @pl.when(step == 0)
    def _():
        acc[...] = gram

    @pl.when(step > 0)
    def _():
        acc[...] += gram

    @pl.when(step == pl.num_programs(0) - 1)
    def _():
        total = acc[...]
        acc[...] = base_ref[...] - total - total.T
        for k, (i, j) in enumerate(lower_blocks(width)):
            packed[k * 128 : (k + 1) * 128, :] = acc[
                i * 128 : (i + 1) * 128, j * 128 : (j + 1) * 128
            ]
        half = packed.shape[0] // 2
        eo_ref[...] = packed[pl.ds(pl.multiple_of(sc[0] * half, half), half), :]
        ex_ref[...] = packed[pl.ds(pl.multiple_of((1 - sc[0]) * half, half), half), :]


def direct_product(scal, own, other, s_hi, s_lo, th, tl, rsum, base):
    groups, count, part, width = own.shape
    rows, cols = s_hi.shape
    high = count * part + 8
    half = len(lower_blocks(width)) * 64
    row_block = lambda step: step % count * 2 + step // count
    s_spec = pl.BlockSpec((256, cols), lambda step, sc: (row_block(step), 0))
    t_spec = pl.BlockSpec((width, 256), lambda step, sc: (0, row_block(step)))
    return pl.pallas_call(
        direct_kernel,
        grid_spec=pltpu.PrefetchScalarGridSpec(
            num_scalar_prefetch=1,
            grid=(2 * count,),
            in_specs=[once(own.shape)] * 2
            + [s_spec] * 2
            + [t_spec] * 2
            + [full(rsum.shape), once(base.shape)],
            out_specs=[pl.BlockSpec((4, high, width), lambda step, sc: (step // count, 0, 0))]
            + [full((half, 128))] * 2,
            scratch_shapes=[pltpu.VMEM((cols, width), BF16)] * 2
            + [pltpu.VMEM((width, width), F32), pltpu.VMEM((2 * half, 128), F32)],
        ),
        out_shape=[jax.ShapeDtypeStruct((8, high, width), F32)]
        + [jax.ShapeDtypeStruct((half, 128), F32)] * 2,
        compiler_params=params(LIMIT),
        cost_estimate=pl.CostEstimate(
            flops=10 * rows * width * cols, bytes_accessed=4 * rows * cols, transcendentals=0
        ),
        name="direct_product",
    )(scal, own, other, s_hi, s_lo, th, tl, rsum, base)


def hdot(a, b):
    return jnp.dot(a, b, precision=HIGH_PRECISION, preferred_element_type=F32)


def inverse_kernel(l_ref, bar_ref, inv_ref, invt_ref, c_ref):
    n = l_ref.shape[0]
    size = 128
    row = lax.broadcasted_iota(jnp.int32, (size, size), 0)
    col = lax.broadcasted_iota(jnp.int32, (size, size), 1)
    powers, results, scales = [], [], []
    for k in range(n // size):
        at = slice(k * size, (k + 1) * size)
        block = l_ref[at, at]
        diag = jnp.where(row == col, block, 0.0)
        by_row = 1.0 / diag.sum(1, keepdims=True)
        scales.append(1.0 / diag.sum(0, keepdims=True))
        nil = jnp.where(row > col, block, 0.0) * (-by_row)
        results.append(jnp.where(row == col, 1.0, 0.0) + nil)
        powers.append(nil)
    for _ in range(6):
        powers = [hdot(p, p) for p in powers]
        results = [r + hdot(r, p) for r, p in zip(results, powers)]
    inv_ref[...] = jnp.zeros_like(inv_ref)
    for k in range(n // size):
        at = slice(k * size, (k + 1) * size)
        inv_ref[at, at] = results[k] * scales[k]
    while size < n:
        for k in range(0, n, 2 * size):
            a, b = slice(k, k + size), slice(k + size, k + 2 * size)
            inv_ref[b, a] = -hdot(inv_ref[b, b], hdot(l_ref[b, a], inv_ref[a, a]))
        size *= 2
    invt_ref[...] = inv_ref[...].T
    c_ref[...] = hdot(l_ref[...].T, bar_ref[...])


def inverse(l11, l11_bar):
    out = jax.ShapeDtypeStruct(l11.shape, F32)
    return pl.pallas_call(
        inverse_kernel,
        out_shape=[out] * 3,
        compiler_params=pltpu.CompilerParams(vmem_limit_bytes=LIMIT * MIB),
        cost_estimate=pl.CostEstimate(flops=6 * 10**9, bytes_accessed=5 * MIB, transcendentals=0),
        name="inverse",
    )(l11, l11_bar)


def final_kernel(sc, own_ref, other_ref, c_ref, inv_ref, invt_ref, out_ref, packed, p_ref):
    n = c_ref.shape[0]
    half = packed.shape[0] // 2
    packed[pl.ds(pl.multiple_of(sc[0] * half, half), half), :] = own_ref[...]
    packed[pl.ds(pl.multiple_of((1 - sc[0]) * half, half), half), :] = other_ref[...]
    p_ref[...] = jnp.zeros_like(p_ref)
    row = lax.broadcasted_iota(jnp.int32, (128, 128), 0)
    col = lax.broadcasted_iota(jnp.int32, (128, 128), 1)
    for k, (i, j) in enumerate(lower_blocks(n)):
        at = (slice(i * 128, (i + 1) * 128), slice(j * 128, (j + 1) * 128))
        x = c_ref[at] - packed[k * 128 : (k + 1) * 128, :]
        if i == j:
            x = jnp.where(row > col, x, jnp.where(row == col, 0.5 * x, 0.0))
        p_ref[at] = x
    q = hdot(hdot(invt_ref[...], p_ref[...]), inv_ref[...])
    out_ref[...] = 0.5 * (q + q.T)


def final(scal, own, other, c, inv, invt):
    return pl.pallas_call(
        final_kernel,
        grid_spec=pltpu.PrefetchScalarGridSpec(
            num_scalar_prefetch=1,
            grid=(1,),
            in_specs=[full(own.shape)] * 2 + [full(c.shape)] * 3,
            out_specs=full(c.shape),
            scratch_shapes=[
                pltpu.VMEM((2 * own.shape[0], own.shape[1]), F32),
                pltpu.VMEM(c.shape, F32),
            ],
        ),
        out_shape=jax.ShapeDtypeStruct(c.shape, F32),
        compiler_params=params(LIMIT),
        name="diagonal_tile",
    )(scal, own, other, c, inv, invt)


def panel_kernel(sc, bar_ref, inv_ref, *refs):
    parts, (out_ref, rg_ref) = refs[:-2], refs[-2:]
    n = bar_ref.shape[0]
    total = parts[0][...]
    for part in parts[1:]:
        total = total + part[...]
    out_ref[...] = hdot(bar_ref[...] - total[:n, :], inv_ref[...])
    sums = total[n:, :128]
    sums = jnp.where(sc[0] == 1, sums[:, 64:], sums[:, :64])
    rg_ref[...] = sums[: rg_ref.shape[0], :]


def panel(scal, bar, inv, parts):
    n, width = bar.shape
    return pl.pallas_call(
        panel_kernel,
        grid_spec=pltpu.PrefetchScalarGridSpec(
            num_scalar_prefetch=1,
            grid=(1,),
            in_specs=[full(bar.shape), full(inv.shape)] + [full(p.shape) for p in parts],
            out_specs=[full(bar.shape), full((n // 64, 64))],
        ),
        out_shape=[
            jax.ShapeDtypeStruct(bar.shape, F32),
            jax.ShapeDtypeStruct((n // 64, 64), F32),
        ],
        compiler_params=params(LIMIT),
        name="panel_tiles",
    )(scal, bar, inv, *parts)


def permutations():
    def make(move):
        pairs = []
        for z in range(4):
            for yh in range(2):
                for core in range(2):
                    for yl in range(2):
                        for x in range(4):
                            nz, nyh, nc, nyl, nx = move(z, yh, core, yl, x)
                            src = (z * 4 + yh * 2 + core) * 8 + yl * 4 + x
                            dst = (nz * 4 + nyh * 2 + nc) * 8 + nyl * 4 + nx
                            pairs.append((src, dst))
        return pairs

    perms = {
        "x+": make(lambda z, h, c, l, x: (z, h, c, l, (x + 1) % 4)),
        "x-": make(lambda z, h, c, l, x: (z, h, c, l, (x + 3) % 4)),
        "x2": make(lambda z, h, c, l, x: (z, h, c, l, (x + 2) % 4)),
        "z+": make(lambda z, h, c, l, x: ((z + 1) % 4, h, c, l, x)),
        "z-": make(lambda z, h, c, l, x: ((z + 3) % 4, h, c, l, x)),
        "z^1": make(lambda z, h, c, l, x: (z ^ 1, h, c, l, x)),
        "z^2": make(lambda z, h, c, l, x: (z ^ 2, h, c, l, x)),
        "z^3": make(lambda z, h, c, l, x: (z ^ 3, h, c, l, x)),
        "yl": make(lambda z, h, c, l, x: (z, h, c, 1 - l, x)),
        "yh": make(lambda z, h, c, l, x: (z, 1 - h, c, l, x)),
        "yhl": make(lambda z, h, c, l, x: (z, 1 - h, c, 1 - l, x)),
        "core": make(lambda z, h, c, l, x: (z, h, 1 - c, l, x)),
    }
    home = lambda z, h, c, l, x: ((z // 2) * 2 + l, x // 2, x % 2, z % 2, h * 2 + c)
    flip = lambda z, h, c, l, x: ((z // 2) * 2 + l, 1 - x // 2, x % 2, z % 2, h * 2 + c)
    perms["home0"] = make(home)
    perms["home1"] = make(flip)
    perms["back0"] = [(d, s) for s, d in perms["home0"]]
    perms["back1"] = [(d, s) for s, d in perms["home1"]]
    return perms


PERMS = permutations()


AXES = ("z", "yh", "core", "yl", "x")


def move(value, name):
    return lax.ppermute(value, AXES, PERMS[name])


def after(values, *deps):
    return lax.optimization_barrier((values, deps))[0]


def per_device(s_bar, l21, panel_column_cotangent, l11, l11_bar, coords, sigma, length, tile_block):
    z, yh, core, yl, x = (lax.axis_index(a) for a in AXES)
    row_id = z * 4 + yh * 2 + core
    col_id = yl * 4 + x
    count, _, width, tiles_c = s_bar.shape[:4]
    part = l21.shape[2]
    rows, cols = count * width, tiles_c * width
    own = l21.reshape(count, part, width)
    own_bar = panel_column_cotangent.reshape(count * part, width)
    ints = lambda vals: jnp.stack([jnp.asarray(v, jnp.int32) for v in vals])

    row_tiles = [i * 16 + row_id for i in range(count)]
    col_tiles = [j * 8 + col_id for j in range(tiles_c)]
    starts = jnp.take(tile_block, ints(row_tiles + col_tiles)) * width
    s_view = s_bar.reshape(rows * cols // 128, 128)
    sig, len_ = sigma.reshape(1, -1), length.reshape(1, -1)

    rw = {(0, 0): own}
    rw[1, 0] = move(own, "yl")
    rw[0, 3] = move(own, "x+")
    rw[0, 1] = move(own, "x-")
    home = move(own, "home0")

    part_blocks = rows // ROWS // 2
    feats = (s_view, coords, sig, len_)
    bufs = prep(0, part_blocks, starts, *feats, None, rows, cols)
    near, left, right, home = after((rw[1, 0], rw[0, 3], rw[0, 1], home), bufs[3])
    rw[0, 1] = right
    starts = after(starts, near, left, right, home)
    col_own = lax.all_gather(home, ("z", "yh"))
    rw[1, 3] = move(near, "x+")
    rw[1, 1] = move(near, "x-")
    rw[0, 2] = move(left, "x+")
    s_hi, s_lo, rsum, csum = prep(part_blocks, part_blocks, starts, *feats, bufs, rows, cols)
    rw[1, 2] = move(after(rw[1, 1], csum), "x-")

    row_keys = [(a, b) for a in range(2) for b in range(4)]
    scal = ints(
        [(yh ^ a) * 2 + (core ^ b) for a in range(2) for b in range(2)]
        + [(yl ^ a) * 4 + (x + b) % 4 for a, b in row_keys]
    )
    own_t, other_t, th, tl = trans_product(
        after(scal, csum), [rw[k] for k in row_keys], s_hi, s_lo, csum
    )
    other_t = move(other_t, "core")
    col_other = move(after(col_own, th), "core")
    base = lax.dot_general(
        after(own_bar, th),
        own.reshape(count * part, width),
        (((0,), (0,)), ((), ())),
        precision=HIGH_PRECISION,
        preferred_element_type=F32,
    )
    inv, invt, c_mat = inverse(after(l11, th), l11_bar)
    t_sum = own_t + after(other_t, inv)
    t_sum = lax.psum_scatter(t_sum.reshape(4, 2, -1, width), "z", scatter_dimension=0)

    y, eo, ex = direct_product(
        after(ints([core]), inv), col_own, col_other, s_hi, s_lo, th, tl, rsum, base
    )
    y = lax.psum_scatter(y, ("yl", "x"), scatter_dimension=0)
    others, n_others = ("z", "yh", "yl", "x"), 64
    e = eo + move(ex, "core")
    e = lax.all_to_all(e.reshape(n_others, -1, 128), others, 0, 0).sum(0)
    e = lax.all_to_all(jnp.broadcast_to(e[None], (n_others,) + e.shape), others, 0, 0)
    t_sum = after(t_sum, eo)
    t0 = move(t_sum[0], "back0")
    t1 = move(t_sum[1], "back1")
    e = e.reshape(eo.shape)
    grad11 = final(ints([core]), e, move(e, "core"), c_mat, inv, invt)
    grad21, row_grad = panel(ints([x % 2]), own_bar, inv, [y, t0, t1])
    return (
        grad21.reshape(count, 1, part, width),
        grad11,
        row_grad.reshape(count, 1, part),
    )


def solution(mesh):
    fine = jax.sharding.Mesh(mesh.devices.reshape(4, 2, 2, 2, 4), AXES)
    prow, pcol = AXES[:3], AXES[3:]
    in_specs = (
        P(None, prow, None, None, pcol, None),
        P(None, prow, pcol, None),
        P(None, prow, pcol, None),
        P(),
        P(),
        P(),
        P(),
        P(),
        P(),
    )
    out_specs = (P(None, prow, pcol, None), P(), P(None, prow, pcol))
    return jax.shard_map(
        per_device, mesh=fine, in_specs=in_specs, out_specs=out_specs, check_vma=False
    )
```

```python
import math

import jax
import jax.numpy as jnp
from jax import lax
from jax.experimental import pallas as pl
from jax.experimental.pallas import tpu as pltpu
from jax.sharding import PartitionSpec as P

HIGH_PRECISION = lax.Precision.HIGHEST
F32 = jnp.float32
BF16 = jnp.bfloat16
SCALE = math.sqrt(12.0) * math.log2(math.e)
MIB = 1024 * 1024
LIMIT = 60
COST = pl.CostEstimate(flops=10**8, bytes_accessed=10**5, transcendentals=0)


def params(mib, dims=1):
    return pltpu.CompilerParams(
        vmem_limit_bytes=mib * MIB, dimension_semantics=("arbitrary",) * dims
    )


def split(value):
    high = value.astype(BF16)
    low = (value - high.astype(F32)).astype(BF16)
    return high, low


def dot(a, b):
    return jnp.dot(a, b, preferred_element_type=F32)


def dot3(a_high, a_low, b_high, b_low):
    return dot(a_high, b_high) + dot(a_low, b_high) + dot(a_high, b_low)


def full(shape, **kw):
    return pl.BlockSpec(shape, lambda *_: (0,) * len(shape), **kw)


def once(shape):
    return full(shape, pipeline_mode=pl.Buffered(1))


ROWS = 128
GROUP = 16


def prep_kernel(first, starts, *refs):
    s_ref, co_ref, sg_ref, le_ref = refs[:4]
    hi_ref, lo_ref, rs_ref, cs_ref, cacc, feat, racc_ref = refs[-7:]
    step = pl.program_id(0)
    tiles_c = cs_ref.shape[0] // 4
    chunks = 4 * tiles_c
    block = first + step
    row_off = pl.multiple_of(starts[block // 4] + (block % 4) * ROWS, ROWS)

    @pl.when(step == 0)
    def _():
        cacc[...] = jnp.zeros_like(cacc)
        for j in range(tiles_c):
            off = pl.multiple_of(starts[3 + j], 512)
            for k in range(4):
                c = j * 4 + k
                at = pl.ds(pl.multiple_of(off + k * 128, 128), 128)
                feat[0, pl.ds(c, 1), :] = co_ref[0:1, at]
                feat[1, pl.ds(c, 1), :] = co_ref[1:2, at]
                feat[2, pl.ds(c, 1), :] = sg_ref[0:1, at]
                feat[3, pl.ds(c, 1), :] = le_ref[0:1, at] * (1.0 / SCALE)

    at = pl.ds(row_off, ROWS)

    def column(row):
        return jnp.broadcast_to(row, (ROWS, ROWS)).T

    racc_ref[1] = column(co_ref[0:1, at])
    racc_ref[2] = column(co_ref[1:2, at])
    racc_ref[3] = column(sg_ref[0:1, at])
    racc_ref[4] = column(le_ref[0:1, at] * (1.0 / SCALE))

    def body(g, _):
        base = pl.multiple_of(g * GROUP, GROUP)
        rows = pl.ds(base, GROUP)
        row_x, row_y, row_s, row_l = (racc_ref[k, rows, :] for k in range(1, 5))
        acc = jnp.zeros((GROUP, 128), F32)
        for c in range(chunks):
            s = s_ref[pl.ds(base * chunks + c, GROUP, stride=chunks), :]
            dx = row_x - feat[0, c : c + 1, :]
            dy = row_y - feat[1, c : c + 1, :]
            dist2 = dx * dx + dy * dy
            scale = row_l + feat[3, c : c + 1, :]
            g2 = dist2 * lax.rsqrt(jnp.maximum(dist2 * (scale * scale), 1e-30))
            weighted = s * ((1.0 + g2 * math.log(2.0)) * jnp.exp2(-g2))
            acc = acc + weighted * feat[2, c : c + 1, :]
            by_row = weighted * row_s
            cacc[c] += by_row.reshape(GROUP // 8, 8, 128).sum(0)
            high, low = split(s)
            hi_ref[rows, c * 128 : (c + 1) * 128] = high
            lo_ref[rows, c * 128 : (c + 1) * 128] = low
        racc_ref[0, rows, :] = acc * row_s
        return 0

    lax.fori_loop(0, ROWS // GROUP, body, 0)
    rs_ref[0] = racc_ref[0].T.sum(0, keepdims=True)

    @pl.when(step == pl.num_programs(0) - 1)
    def _():
        total = cacc[...].sum(1) * feat[2]
        cs_ref[...] = total if first == 0 else refs[7][...] + total


def prep(first, per, starts, s_view, coords, sigma, length, bufs, rows, cols):
    chunks = cols // 128
    any_spec = pl.BlockSpec(memory_space=pl.ANY)
    out_map = lambda s, st: (first + s, 0)
    args = [starts, s_view, coords, sigma, length]
    in_specs = [
        pl.BlockSpec((ROWS * chunks, 128), out_map),
        full(coords.shape),
        full(sigma.shape),
        full(length.shape),
    ]
    aliases = {}
    if first:
        args += list(bufs)
        in_specs += [any_spec, any_spec, any_spec, full((chunks, 128))]
        aliases = {5: 0, 6: 1, 7: 2}
    return pl.pallas_call(
        lambda *refs: prep_kernel(first, *refs),
        grid_spec=pltpu.PrefetchScalarGridSpec(
            num_scalar_prefetch=1,
            grid=(per,),
            in_specs=in_specs,
            out_specs=[
                pl.BlockSpec((ROWS, cols), out_map),
                pl.BlockSpec((ROWS, cols), out_map),
                pl.BlockSpec((1, 1, ROWS), lambda s, st: (first + s, 0, 0)),
                pl.BlockSpec((chunks, 128), lambda s, st: (0, 0)),
            ],
            scratch_shapes=[
                pltpu.VMEM((chunks, 8, 128), F32),
                pltpu.VMEM((4, chunks, 128), F32),
                pltpu.VMEM((5, ROWS, ROWS), F32),
            ],
        ),
        out_shape=[
            jax.ShapeDtypeStruct((rows, cols), BF16),
            jax.ShapeDtypeStruct((rows, cols), BF16),
            jax.ShapeDtypeStruct((rows // ROWS, 1, ROWS), F32),
            jax.ShapeDtypeStruct((chunks, 128), F32),
        ],
        input_output_aliases=aliases,
        compiler_params=params(LIMIT),
        cost_estimate=COST,
        name="kernel_sums",
    )(*args)


def put_row(ref, base, at, value):
    rows = pl.ds(base, 8)
    mask = lax.broadcasted_iota(jnp.int32, (8, 128), 0) == at
    ref[rows, :128] = jnp.where(mask, value, ref[rows, :128])


def trans_kernel(sc, *refs):
    pieces, refs = refs[:8], refs[8:]
    count, part, width = pieces[0].shape
    s_high, s_low, cs_ref = refs[:count], refs[count : 2 * count], refs[2 * count]
    own_ref, other_ref, tth_ref, ttl_ref, th_ref, tl_ref, rows_ref = refs[2 * count + 1 : -count]
    tmps = refs[-count:]
    zp = pl.program_id(0)
    base = count * part

    @pl.when(zp == 0)
    def _():
        for r in range(8):
            for i in range(count):
                at = pl.multiple_of(i * 512 + sc[4 + r] * part, part)
                rows_ref[pl.ds(at, part), :] = pieces[r][i]
        for k in range(count * 4):
            at = slice(k * 128, (k + 1) * 128)
            high, low = split(rows_ref[at, :].T)
            th_ref[:, at] = high
            tl_ref[:, at] = low

    for i in range(count):
        out = dot3(th_ref[...], tl_ref[...], s_high[i][...], s_low[i][...])
        tmps[i][...] = out.T
        tth_ref[i], ttl_ref[i] = split(out)
    for ref, dcore in ((own_ref, 0), (other_ref, 1)):
        for dyh in range(2):
            sub = sc[dyh * 2 + dcore]
            at = pl.ds(pl.multiple_of(sub * part, part), part)
            ref[dyh, base:, :] = jnp.zeros((8, width), F32)
            for i in range(count):
                ref[dyh, i * part : (i + 1) * part, :] = tmps[i][at, :]
                ref[dyh, base + i : base + i + 1, :128] = cs_ref[
                    pl.ds(i * 8 + zp * 2 + sub // 2, 1), :
                ]


def trans_product(scal, pieces, s_hi, s_lo, csum):
    count, part, width = pieces[0].shape
    rows, cols = s_hi.shape
    high = count * part + 8
    s_specs = [
        pl.BlockSpec((rows, 256), lambda step, sc, i=i: (0, i * 4 + step)) for i in range(count)
    ]
    o_spec = pl.BlockSpec((2, high, width), lambda step, sc: (step, 0, 0))
    return pl.pallas_call(
        trans_kernel,
        grid_spec=pltpu.PrefetchScalarGridSpec(
            num_scalar_prefetch=1,
            grid=(4,),
            in_specs=[once(p.shape) for p in pieces] + s_specs * 2 + [full(csum.shape)],
            out_specs=[o_spec] * 2
            + [pl.BlockSpec((count, width, 256), lambda step, sc: (0, 0, step))] * 2,
            scratch_shapes=[pltpu.VMEM((width, rows), BF16)] * 2
            + [pltpu.VMEM((rows, width), F32)]
            + [pltpu.VMEM((256, width), F32)] * count,
        ),
        out_shape=[jax.ShapeDtypeStruct((8, high, width), F32)] * 2
        + [jax.ShapeDtypeStruct((count, width, 1024), BF16)] * 2,
        compiler_params=params(LIMIT),
        cost_estimate=COST,
        name="transposed_product",
    )(scal, *pieces, *[s_hi] * count, *[s_lo] * count, csum)


def lower_blocks(n):
    return [(i, j) for i in range(n // 128) for j in range(i + 1)]


def cols_kernel(sc, own_ref, other_ref, base_ref, tth_ref, ttl_ref, *refs):
    ch_ref, cl_ref, eo_ref, ex_ref, acc, packed = refs
    groups, _, part, width = own_ref.shape
    step = pl.program_id(0)
    for ref, core in ((own_ref, sc[0]), (other_ref, 1 - sc[0])):
        for g in range(groups):
            at = pl.ds(pl.multiple_of((g * 2 + core) * part, part), part)
            high, low = split(ref[g, 0])
            ch_ref[at, :] = high
            cl_ref[at, :] = low
    gram = dot3(tth_ref[0], ttl_ref[0], ch_ref[...], cl_ref[...])

    @pl.when(step == 0)
    def _():
        acc[...] = gram

    @pl.when(step > 0)
    def _():
        acc[...] += gram

    @pl.when(step == pl.num_programs(0) - 1)
    def _():
        total = acc[...]
        total = base_ref[...] - total - total.T
        for k, (i, j) in enumerate(lower_blocks(width)):
            packed[k * 128 : (k + 1) * 128, :] = total[
                i * 128 : (i + 1) * 128, j * 128 : (j + 1) * 128
            ]
        half = packed.shape[0] // 2
        eo_ref[...] = packed[pl.ds(pl.multiple_of(sc[0] * half, half), half), :]
        ex_ref[...] = packed[pl.ds(pl.multiple_of((1 - sc[0]) * half, half), half), :]


def column_panels(scal, own, other, base, tts):
    groups, count, part, width = own.shape
    cols = groups * count * part * 2
    half = len(lower_blocks(width)) * 64
    return pl.pallas_call(
        cols_kernel,
        grid_spec=pltpu.PrefetchScalarGridSpec(
            num_scalar_prefetch=1,
            grid=(count,),
            in_specs=[pl.BlockSpec((groups, 1, part, width), lambda i, sc: (0, i, 0, 0))] * 2
            + [once(base.shape)]
            + [pl.BlockSpec((1,) + tts[0].shape[1:], lambda i, sc: (i, 0, 0))] * 2,
            out_specs=[pl.BlockSpec((cols // count, width), lambda i, sc: (i, 0))] * 2
            + [full((half, 128))] * 2,
            scratch_shapes=[pltpu.VMEM((width, width), F32), pltpu.VMEM((2 * half, 128), F32)],
        ),
        out_shape=[jax.ShapeDtypeStruct((cols, width), BF16)] * 2
        + [jax.ShapeDtypeStruct((half, 128), F32)] * 2,
        compiler_params=params(LIMIT),
        cost_estimate=COST,
        name="column_panels",
    )(scal, own, other, base, *tts)


def direct_product(ch, cl, s_hi, s_lo, rsum, first, count):
    cols, width = ch.shape
    part = 64
    base = count * part
    row_block = lambda step: (first + step % count) * 2 + step // count

    def kernel(ch_ref, cl_ref, sh_ref, sl_ref, rs_ref, y_ref):
        step = pl.program_id(0)
        tile = step % count
        out = dot3(sh_ref[...], sl_ref[...], ch_ref[...], cl_ref[...])
        rows_at = pl.ds(pl.multiple_of(tile * part, part), part)

        @pl.when(tile == 0)
        def _():
            y_ref[:, base:, :] = jnp.zeros((4, 8, width), F32)

        for x in range(4):
            y_ref[x, rows_at, :] = out[x * part : (x + 1) * part, :]
            sums = rs_ref[(first + tile) * 4 + step // count * 2 + x // 2]
            put_row(y_ref.at[x], base, tile, sums)

    s_spec = pl.BlockSpec((256, cols), lambda step: (row_block(step), 0))
    return pl.pallas_call(
        kernel,
        grid=(2 * count,),
        in_specs=[once(ch.shape)] * 2 + [s_spec] * 2 + [full(rsum.shape)],
        out_specs=pl.BlockSpec((4, base + 8, width), lambda step: (step // count, 0, 0)),
        out_shape=jax.ShapeDtypeStruct((8, base + 8, width), F32),
        compiler_params=params(LIMIT),
        cost_estimate=COST,
        name="direct_product",
    )(ch, cl, s_hi, s_lo, rsum)


def hdot(a, b):
    return jnp.dot(a, b, precision=HIGH_PRECISION, preferred_element_type=F32)


def inverse_kernel(l_ref, bar_ref, own_bar_ref, own_ref, inv_ref, invt_ref, c_ref, base_ref):
    n = l_ref.shape[0]
    size = 128
    row = lax.broadcasted_iota(jnp.int32, (size, size), 0)
    col = lax.broadcasted_iota(jnp.int32, (size, size), 1)
    powers, results, scales = [], [], []
    for k in range(n // size):
        at = slice(k * size, (k + 1) * size)
        block = l_ref[at, at]
        diag = jnp.where(row == col, block, 0.0)
        by_row = 1.0 / diag.sum(1, keepdims=True)
        scales.append(1.0 / diag.sum(0, keepdims=True))
        nil = jnp.where(row > col, block, 0.0) * (-by_row)
        results.append(jnp.where(row == col, 1.0, 0.0) + nil)
        powers.append(nil)
    for _ in range(6):
        powers = [hdot(p, p) for p in powers]
        results = [r + hdot(r, p) for r, p in zip(results, powers)]
    inv_ref[...] = jnp.zeros_like(inv_ref)
    for k in range(n // size):
        at = slice(k * size, (k + 1) * size)
        inv_ref[at, at] = results[k] * scales[k]
    while size < n:
        for k in range(0, n, 2 * size):
            a, b = slice(k, k + size), slice(k + size, k + 2 * size)
            inv_ref[b, a] = -hdot(inv_ref[b, b], hdot(l_ref[b, a], inv_ref[a, a]))
        size *= 2
    invt_ref[...] = inv_ref[...].T
    c_ref[...] = hdot(l_ref[...].T, bar_ref[...])
    base_ref[...] = hdot(own_bar_ref[...].T, own_ref[...])


def inverse(l11, l11_bar, own_bar, own):
    out = jax.ShapeDtypeStruct(l11.shape, F32)
    return pl.pallas_call(
        inverse_kernel,
        out_shape=[out] * 4,
        compiler_params=pltpu.CompilerParams(vmem_limit_bytes=LIMIT * MIB),
        cost_estimate=COST,
        name="inverse",
    )(l11, l11_bar, own_bar, own)


def final_kernel(sc, own_ref, other_ref, c_ref, inv_ref, invt_ref, out_ref, packed, p_ref):
    n = c_ref.shape[0]
    half = packed.shape[0] // 2
    packed[pl.ds(pl.multiple_of(sc[0] * half, half), half), :] = own_ref[...]
    packed[pl.ds(pl.multiple_of((1 - sc[0]) * half, half), half), :] = other_ref[...]
    p_ref[...] = jnp.zeros_like(p_ref)
    row = lax.broadcasted_iota(jnp.int32, (128, 128), 0)
    col = lax.broadcasted_iota(jnp.int32, (128, 128), 1)
    for k, (i, j) in enumerate(lower_blocks(n)):
        at = (slice(i * 128, (i + 1) * 128), slice(j * 128, (j + 1) * 128))
        x = c_ref[at] - packed[k * 128 : (k + 1) * 128, :]
        if i == j:
            x = jnp.where(row > col, x, jnp.where(row == col, 0.5 * x, 0.0))
        p_ref[at] = x
    q = dot3(*split(invt_ref[...]), *split(p_ref[...]))
    q = dot3(*split(q), *split(inv_ref[...]))
    out_ref[...] = 0.5 * (q + q.T)


def final(scal, own, other, c, inv, invt):
    return pl.pallas_call(
        final_kernel,
        grid_spec=pltpu.PrefetchScalarGridSpec(
            num_scalar_prefetch=1,
            grid=(1,),
            in_specs=[full(own.shape)] * 2 + [full(c.shape)] * 3,
            out_specs=full(c.shape),
            scratch_shapes=[
                pltpu.VMEM((2 * own.shape[0], own.shape[1]), F32),
                pltpu.VMEM(c.shape, F32),
            ],
        ),
        out_shape=jax.ShapeDtypeStruct(c.shape, F32),
        compiler_params=params(LIMIT),
        name="diagonal_tile",
    )(scal, own, other, c, inv, invt)


def panel_kernel(sc, bar_ref, inv_ref, y_ref, z_ref, t_ref, u_ref, out_ref, rg_ref):
    n = bar_ref.shape[0]
    cut = y_ref.shape[0] - 8
    rest = z_ref[0]
    for k in range(1, z_ref.shape[0]):
        rest = rest + z_ref[k]
    t = t_ref[...] + u_ref[...]
    total = jnp.concatenate([y_ref[:cut, :], rest[: n - cut, :]], 0) + t[:n, :]
    out_ref[...] = dot3(*split(bar_ref[...] - total), *split(inv_ref[...]))
    tiles = cut // 64
    sums = t[n:, :128]
    take = lambda a: jnp.where(sc[0] == 1, a[:, 64:128], a[:, :64])
    rg_ref[:tiles, :] = take((sums[:tiles, :] + y_ref[cut : cut + tiles, :128]))
    more = n // 64 - tiles
    rg_ref[tiles:, :] = take(sums[tiles : tiles + more, :] + rest[n - cut : n - cut + more, :128])


def panel(scal, bar, inv, parts):
    n, width = bar.shape
    return pl.pallas_call(
        panel_kernel,
        grid_spec=pltpu.PrefetchScalarGridSpec(
            num_scalar_prefetch=1,
            grid=(1,),
            in_specs=[full(bar.shape), full(inv.shape)] + [full(p.shape) for p in parts],
            out_specs=[full(bar.shape), full((n // 64, 64))],
        ),
        out_shape=[
            jax.ShapeDtypeStruct(bar.shape, F32),
            jax.ShapeDtypeStruct((n // 64, 64), F32),
        ],
        compiler_params=params(LIMIT),
        cost_estimate=COST,
        name="panel_tiles",
    )(scal, bar, inv, *parts)


def permutations():
    def make(move):
        pairs = []
        for z in range(4):
            for yh in range(2):
                for core in range(2):
                    for yl in range(2):
                        for x in range(4):
                            nz, nyh, nc, nyl, nx = move(z, yh, core, yl, x)
                            src = (z * 4 + yh * 2 + core) * 8 + yl * 4 + x
                            dst = (nz * 4 + nyh * 2 + nc) * 8 + nyl * 4 + nx
                            pairs.append((src, dst))
        return pairs

    perms = {
        "x+": make(lambda z, h, c, l, x: (z, h, c, l, (x + 1) % 4)),
        "x-": make(lambda z, h, c, l, x: (z, h, c, l, (x + 3) % 4)),
        "x2": make(lambda z, h, c, l, x: (z, h, c, l, (x + 2) % 4)),
        "z+": make(lambda z, h, c, l, x: ((z + 1) % 4, h, c, l, x)),
        "z-": make(lambda z, h, c, l, x: ((z + 3) % 4, h, c, l, x)),
        "z^1": make(lambda z, h, c, l, x: (z ^ 1, h, c, l, x)),
        "z^2": make(lambda z, h, c, l, x: (z ^ 2, h, c, l, x)),
        "z^3": make(lambda z, h, c, l, x: (z ^ 3, h, c, l, x)),
        "yl": make(lambda z, h, c, l, x: (z, h, c, 1 - l, x)),
        "yh": make(lambda z, h, c, l, x: (z, 1 - h, c, l, x)),
        "yhl": make(lambda z, h, c, l, x: (z, 1 - h, c, 1 - l, x)),
        "core": make(lambda z, h, c, l, x: (z, h, 1 - c, l, x)),
    }
    home = lambda z, h, c, l, x: ((z // 2) * 2 + l, x // 2, x % 2, z % 2, h * 2 + c)
    flip = lambda z, h, c, l, x: ((z // 2) * 2 + l, 1 - x // 2, x % 2, z % 2, h * 2 + c)
    perms["home0"] = make(home)
    perms["home1"] = make(flip)
    perms["back0"] = [(d, s) for s, d in perms["home0"]]
    perms["back1"] = [(d, s) for s, d in perms["home1"]]
    return perms


PERMS = permutations()


AXES = ("z", "yh", "core", "yl", "x")


def move(value, name):
    return lax.ppermute(value, AXES, PERMS[name])


def after(values, *deps):
    return lax.optimization_barrier((values, deps))[0]


def per_device(s_bar, l21, panel_column_cotangent, l11, l11_bar, coords, sigma, length, tile_block):
    z, yh, core, yl, x = (lax.axis_index(a) for a in AXES)
    row_id = z * 4 + yh * 2 + core
    col_id = yl * 4 + x
    count, _, width, tiles_c = s_bar.shape[:4]
    part = l21.shape[2]
    rows, cols = count * width, tiles_c * width
    own = l21.reshape(count, part, width)
    own_bar = panel_column_cotangent.reshape(count * part, width)
    ints = lambda vals: jnp.stack([jnp.asarray(v, jnp.int32) for v in vals])

    row_tiles = [i * 16 + row_id for i in range(count)]
    col_tiles = [j * 8 + col_id for j in range(tiles_c)]
    starts = jnp.take(tile_block, ints(row_tiles + col_tiles)) * width
    s_view = s_bar.reshape(rows * cols // 128, 128)
    sig, len_ = sigma.reshape(1, -1), length.reshape(1, -1)

    rw = {(0, 0): own}
    rw[1, 0] = move(own, "yl")
    rw[0, 3] = move(own, "x+")
    rw[0, 1] = move(own, "x-")
    home = move(own, "home0")

    part_blocks = rows // ROWS // 2
    feats = (s_view, coords, sig, len_)
    bufs = prep(0, part_blocks, starts, *feats, None, rows, cols)
    near, left, right, home = after((rw[1, 0], rw[0, 3], rw[0, 1], home), bufs[3])
    rw[0, 1] = right
    starts = after(starts, near, left, right, home)
    col_own = lax.all_gather(home, ("z", "yh"))
    rw[1, 3] = move(near, "x+")
    rw[1, 1] = move(near, "x-")
    rw[0, 2] = move(left, "x+")
    s_hi, s_lo, rsum, csum = prep(part_blocks, part_blocks, starts, *feats, bufs, rows, cols)
    rw[1, 2] = move(after(rw[1, 1], csum), "x-")

    row_keys = [(a, b) for a in range(2) for b in range(4)]
    scal = ints(
        [(yh ^ a) * 2 + (core ^ b) for a in range(2) for b in range(2)]
        + [(yl ^ a) * 4 + (x + b) % 4 for a, b in row_keys]
    )
    own_t, other_t, *tts = trans_product(
        after(scal, csum), [rw[k] for k in row_keys], s_hi, s_lo, csum
    )
    other_t = move(other_t, "core")
    col_other = move(after(col_own, tts[0]), "core")
    flat = own.reshape(count * part, width)
    inv, invt, c_mat, base = inverse(after(l11, tts[0]), l11_bar, own_bar, flat)
    t_sum = own_t + after(other_t, inv)
    t_sum = lax.psum_scatter(t_sum.reshape(4, 2, -1, width), "z", scatter_dimension=0)

    ch, cl, eo, ex = column_panels(after(ints([core]), inv), col_own, col_other, base, tts)
    others, n_others = ("z", "yh", "yl", "x"), 64
    e = eo + move(ex, "core")
    e = e.reshape(n_others, -1, 128)
    y = direct_product(after(ch, e), cl, s_hi, s_lo, rsum, 0, 2)
    e = lax.all_to_all(e, others, 0, 0).sum(0)
    e = jnp.broadcast_to(e[None], (n_others,) + e.shape)
    rest = direct_product(after(ch, y, e), cl, s_hi, s_lo, rsum, 2, 1)
    y = lax.psum_scatter(y, ("yl", "x"), scatter_dimension=0)
    e = lax.all_to_all(e, others, 0, 0)
    rest = lax.all_to_all(rest, ("yl", "x"), 0, 0)
    t0 = move(t_sum[0], "back0")
    t1 = move(t_sum[1], "back1")
    e = e.reshape(eo.shape)
    grad11 = final(ints([core]), e, move(e, "core"), c_mat, inv, invt)
    grad21, row_grad = panel(ints([x % 2]), own_bar, inv, [y, rest, t0, t1])
    return (
        grad21.reshape(count, 1, part, width),
        grad11,
        row_grad.reshape(count, 1, part),
    )


def solution(mesh):
    fine = jax.sharding.Mesh(mesh.devices.reshape(4, 2, 2, 2, 4), AXES)
    prow, pcol = AXES[:3], AXES[3:]
    in_specs = (
        P(None, prow, None, None, pcol, None),
        P(None, prow, pcol, None),
        P(None, prow, pcol, None),
        P(),
        P(),
        P(),
        P(),
        P(),
        P(),
    )
    out_specs = (P(None, prow, pcol, None), P(), P(None, prow, pcol))
    return jax.shard_map(
        per_device, mesh=fine, in_specs=in_specs, out_specs=out_specs, check_vma=False
    )
```

```python
import math

import jax
import jax.numpy as jnp
from jax import lax
from jax.experimental import pallas as pl
from jax.experimental.pallas import tpu as pltpu
from jax.sharding import PartitionSpec as P

HIGH_PRECISION = lax.Precision.HIGHEST
F32 = jnp.float32
BF16 = jnp.bfloat16
SCALE = math.sqrt(12.0) * math.log2(math.e)
MIB = 1024 * 1024
LIMIT = 60
COST = pl.CostEstimate(flops=10**8, bytes_accessed=10**5, transcendentals=0)


def params(mib, dims=1):
    return pltpu.CompilerParams(
        vmem_limit_bytes=mib * MIB, dimension_semantics=("arbitrary",) * dims
    )


def split(value):
    high = value.astype(BF16)
    low = (value - high.astype(F32)).astype(BF16)
    return high, low


def dot(a, b):
    return jnp.dot(a, b, preferred_element_type=F32)


def dot3(a_high, a_low, b_high, b_low):
    return dot(a_high, b_high) + dot(a_low, b_high) + dot(a_high, b_low)


def full(shape, **kw):
    return pl.BlockSpec(shape, lambda *_: (0,) * len(shape), **kw)


def once(shape):
    return full(shape, pipeline_mode=pl.Buffered(1))


ROWS = 128
GROUP = 16


def prep_kernel(first, starts, *refs):
    s_ref, co_ref, sg_ref, le_ref = refs[:4]
    hi_ref, lo_ref, rs_ref, cs_ref, cacc, feat, racc_ref = refs[-7:]
    step = pl.program_id(0)
    tiles_c = cs_ref.shape[0] // 4
    chunks = 4 * tiles_c
    block = first + step
    row_off = pl.multiple_of(starts[block // 4] + (block % 4) * ROWS, ROWS)

    @pl.when(step == 0)
    def _():
        cacc[...] = jnp.zeros_like(cacc)
        for j in range(tiles_c):
            off = pl.multiple_of(starts[3 + j], 512)
            for k in range(4):
                c = j * 4 + k
                at = pl.ds(pl.multiple_of(off + k * 128, 128), 128)
                feat[0, pl.ds(c, 1), :] = co_ref[0:1, at]
                feat[1, pl.ds(c, 1), :] = co_ref[1:2, at]
                feat[2, pl.ds(c, 1), :] = sg_ref[0:1, at]
                feat[3, pl.ds(c, 1), :] = le_ref[0:1, at] * (1.0 / SCALE)

    at = pl.ds(row_off, ROWS)

    def column(row):
        return jnp.broadcast_to(row, (ROWS, ROWS)).T

    racc_ref[1] = column(co_ref[0:1, at])
    racc_ref[2] = column(co_ref[1:2, at])
    racc_ref[3] = column(sg_ref[0:1, at])
    racc_ref[4] = column(le_ref[0:1, at] * (1.0 / SCALE))

    def body(g, _):
        base = pl.multiple_of(g * GROUP, GROUP)
        rows = pl.ds(base, GROUP)
        row_x, row_y, row_s, row_l = (racc_ref[k, rows, :] for k in range(1, 5))
        acc = jnp.zeros((GROUP, 128), F32)
        for c in range(chunks):
            s = s_ref[pl.ds(base * chunks + c, GROUP, stride=chunks), :]
            dx = row_x - feat[0, c : c + 1, :]
            dy = row_y - feat[1, c : c + 1, :]
            dist2 = dx * dx + dy * dy
            scale = row_l + feat[3, c : c + 1, :]
            g2 = dist2 * lax.rsqrt(jnp.maximum(dist2 * (scale * scale), 1e-30))
            weighted = s * ((1.0 + g2 * math.log(2.0)) * jnp.exp2(-g2))
            acc = acc + weighted * feat[2, c : c + 1, :]
            by_row = weighted * row_s
            cacc[c] += by_row.reshape(GROUP // 8, 8, 128).sum(0)
            high, low = split(s)
            hi_ref[rows, c * 128 : (c + 1) * 128] = high
            lo_ref[rows, c * 128 : (c + 1) * 128] = low
        racc_ref[0, rows, :] = acc * row_s
        return 0

    lax.fori_loop(0, ROWS // GROUP, body, 0)
    rs_ref[0] = racc_ref[0].T.sum(0, keepdims=True)

    @pl.when(step == pl.num_programs(0) - 1)
    def _():
        total = cacc[...].sum(1) * feat[2]
        cs_ref[...] = total if first == 0 else refs[7][...] + total


def prep(first, per, starts, s_view, coords, sigma, length, bufs, rows, cols):
    chunks = cols // 128
    any_spec = pl.BlockSpec(memory_space=pl.ANY)
    out_map = lambda s, st: (first + s, 0)
    args = [starts, s_view, coords, sigma, length]
    in_specs = [
        pl.BlockSpec((ROWS * chunks, 128), out_map),
        full(coords.shape),
        full(sigma.shape),
        full(length.shape),
    ]
    aliases = {}
    if first:
        args += list(bufs)
        in_specs += [any_spec, any_spec, any_spec, full((chunks, 128))]
        aliases = {5: 0, 6: 1, 7: 2}
    return pl.pallas_call(
        lambda *refs: prep_kernel(first, *refs),
        grid_spec=pltpu.PrefetchScalarGridSpec(
            num_scalar_prefetch=1,
            grid=(per,),
            in_specs=in_specs,
            out_specs=[
                pl.BlockSpec((ROWS, cols), out_map),
                pl.BlockSpec((ROWS, cols), out_map),
                pl.BlockSpec((1, 1, ROWS), lambda s, st: (first + s, 0, 0)),
                pl.BlockSpec((chunks, 128), lambda s, st: (0, 0)),
            ],
            scratch_shapes=[
                pltpu.VMEM((chunks, 8, 128), F32),
                pltpu.VMEM((4, chunks, 128), F32),
                pltpu.VMEM((5, ROWS, ROWS), F32),
            ],
        ),
        out_shape=[
            jax.ShapeDtypeStruct((rows, cols), BF16),
            jax.ShapeDtypeStruct((rows, cols), BF16),
            jax.ShapeDtypeStruct((rows // ROWS, 1, ROWS), F32),
            jax.ShapeDtypeStruct((chunks, 128), F32),
        ],
        input_output_aliases=aliases,
        compiler_params=params(LIMIT),
        cost_estimate=COST,
        name="kernel_sums",
    )(*args)


def put_row(ref, base, at, value):
    rows = pl.ds(base, 8)
    mask = lax.broadcasted_iota(jnp.int32, (8, 128), 0) == at
    ref[rows, :128] = jnp.where(mask, value, ref[rows, :128])


def trans_kernel(sc, *refs):
    pieces, refs = refs[:8], refs[8:]
    count, part, width = pieces[0].shape
    s_high, s_low, cs_ref = refs[:count], refs[count : 2 * count], refs[2 * count]
    own_ref, other_ref, tth_ref, ttl_ref, th_ref, tl_ref, rows_ref = refs[2 * count + 1 : -count]
    tmps = refs[-count:]
    zp = pl.program_id(0)
    base = count * part

    @pl.when(zp == 0)
    def _():
        for r in range(8):
            for i in range(count):
                at = pl.multiple_of(i * 512 + sc[4 + r] * part, part)
                rows_ref[pl.ds(at, part), :] = pieces[r][i]
        for k in range(count * 4):
            at = slice(k * 128, (k + 1) * 128)
            high, low = split(rows_ref[at, :].T)
            th_ref[:, at] = high
            tl_ref[:, at] = low

    for i in range(count):
        out = dot3(th_ref[...], tl_ref[...], s_high[i][...], s_low[i][...])
        tmps[i][...] = out.T
        tth_ref[i], ttl_ref[i] = split(out)
    for ref, dcore in ((own_ref, 0), (other_ref, 1)):
        for dyh in range(2):
            sub = sc[dyh * 2 + dcore]
            at = pl.ds(pl.multiple_of(sub * part, part), part)
            ref[dyh, base:, :] = jnp.zeros((8, width), F32)
            for i in range(count):
                ref[dyh, i * part : (i + 1) * part, :] = tmps[i][at, :]
                ref[dyh, base + i : base + i + 1, :128] = cs_ref[
                    pl.ds(i * 8 + zp * 2 + sub // 2, 1), :
                ]


def trans_product(scal, pieces, s_hi, s_lo, csum):
    count, part, width = pieces[0].shape
    rows, cols = s_hi.shape
    high = count * part + 8
    s_specs = [
        pl.BlockSpec((rows, 256), lambda step, sc, i=i: (0, i * 4 + step)) for i in range(count)
    ]
    o_spec = pl.BlockSpec((2, high, width), lambda step, sc: (step, 0, 0))
    return pl.pallas_call(
        trans_kernel,
        grid_spec=pltpu.PrefetchScalarGridSpec(
            num_scalar_prefetch=1,
            grid=(4,),
            in_specs=[once(p.shape) for p in pieces] + s_specs * 2 + [full(csum.shape)],
            out_specs=[o_spec] * 2
            + [pl.BlockSpec((count, width, 256), lambda step, sc: (0, 0, step))] * 2,
            scratch_shapes=[pltpu.VMEM((width, rows), BF16)] * 2
            + [pltpu.VMEM((rows, width), F32)]
            + [pltpu.VMEM((256, width), F32)] * count,
        ),
        out_shape=[jax.ShapeDtypeStruct((8, high, width), F32)] * 2
        + [jax.ShapeDtypeStruct((count, width, 1024), BF16)] * 2,
        compiler_params=params(LIMIT),
        cost_estimate=COST,
        name="transposed_product",
    )(scal, *pieces, *[s_hi] * count, *[s_lo] * count, csum)


def lower_blocks(n):
    return [(i, j) for i in range(n // 128) for j in range(i + 1)]


def cols_kernel(sc, own_ref, other_ref, base_ref, tth_ref, ttl_ref, *refs):
    ch_ref, cl_ref, eo_ref, ex_ref, acc, packed = refs
    groups, _, part, width = own_ref.shape
    step = pl.program_id(0)
    for ref, core in ((own_ref, sc[0]), (other_ref, 1 - sc[0])):
        for g in range(groups):
            at = pl.ds(pl.multiple_of((g * 2 + core) * part, part), part)
            high, low = split(ref[g, 0])
            ch_ref[at, :] = high
            cl_ref[at, :] = low
    gram = dot3(tth_ref[0], ttl_ref[0], ch_ref[...], cl_ref[...])

    @pl.when(step == 0)
    def _():
        acc[...] = gram

    @pl.when(step > 0)
    def _():
        acc[...] += gram

    @pl.when(step == pl.num_programs(0) - 1)
    def _():
        total = acc[...]
        total = base_ref[...] - total - total.T
        for k, (i, j) in enumerate(lower_blocks(width)):
            packed[k * 128 : (k + 1) * 128, :] = total[
                i * 128 : (i + 1) * 128, j * 128 : (j + 1) * 128
            ]
        half = packed.shape[0] // 2
        eo_ref[...] = packed[pl.ds(pl.multiple_of(sc[0] * half, half), half), :]
        ex_ref[...] = packed[pl.ds(pl.multiple_of((1 - sc[0]) * half, half), half), :]


def column_panels(scal, own, other, base, tts):
    groups, count, part, width = own.shape
    cols = groups * count * part * 2
    half = len(lower_blocks(width)) * 64
    return pl.pallas_call(
        cols_kernel,
        grid_spec=pltpu.PrefetchScalarGridSpec(
            num_scalar_prefetch=1,
            grid=(count,),
            in_specs=[pl.BlockSpec((groups, 1, part, width), lambda i, sc: (0, i, 0, 0))] * 2
            + [once(base.shape)]
            + [pl.BlockSpec((1,) + tts[0].shape[1:], lambda i, sc: (i, 0, 0))] * 2,
            out_specs=[pl.BlockSpec((cols // count, width), lambda i, sc: (i, 0))] * 2
            + [full((half, 128))] * 2,
            scratch_shapes=[pltpu.VMEM((width, width), F32), pltpu.VMEM((2 * half, 128), F32)],
        ),
        out_shape=[jax.ShapeDtypeStruct((cols, width), BF16)] * 2
        + [jax.ShapeDtypeStruct((half, 128), F32)] * 2,
        compiler_params=params(LIMIT),
        cost_estimate=COST,
        name="column_panels",
    )(scal, own, other, base, *tts)


def direct_product(ch, cl, s_hi, s_lo, rsum, first, count):
    cols, width = ch.shape
    part = 64
    base = count * part
    row_block = lambda step: (first + step % count) * 2 + step // count

    def kernel(ch_ref, cl_ref, sh_ref, sl_ref, rs_ref, y_ref):
        step = pl.program_id(0)
        tile = step % count
        out = dot3(sh_ref[...], sl_ref[...], ch_ref[...], cl_ref[...])
        rows_at = pl.ds(pl.multiple_of(tile * part, part), part)

        @pl.when(tile == 0)
        def _():
            y_ref[:, base:, :] = jnp.zeros((4, 8, width), F32)

        for x in range(4):
            y_ref[x, rows_at, :] = out[x * part : (x + 1) * part, :]
            sums = rs_ref[(first + tile) * 4 + step // count * 2 + x // 2]
            put_row(y_ref.at[x], base, tile, sums)

    s_spec = pl.BlockSpec((256, cols), lambda step: (row_block(step), 0))
    return pl.pallas_call(
        kernel,
        grid=(2 * count,),
        in_specs=[once(ch.shape)] * 2 + [s_spec] * 2 + [full(rsum.shape)],
        out_specs=pl.BlockSpec((4, base + 8, width), lambda step: (step // count, 0, 0)),
        out_shape=jax.ShapeDtypeStruct((8, base + 8, width), F32),
        compiler_params=params(LIMIT),
        cost_estimate=pl.CostEstimate(
            flops=4 * 10**9 * (2 * count + 1), bytes_accessed=10**6, transcendentals=0
        ),
        name="direct_product",
    )(ch, cl, s_hi, s_lo, rsum)


def hdot(a, b):
    return jnp.dot(a, b, precision=HIGH_PRECISION, preferred_element_type=F32)


def inverse_kernel(l_ref, bar_ref, own_bar_ref, own_ref, inv_ref, invt_ref, c_ref, base_ref):
    n = l_ref.shape[0]
    size = 128
    row = lax.broadcasted_iota(jnp.int32, (size, size), 0)
    col = lax.broadcasted_iota(jnp.int32, (size, size), 1)
    powers, results, scales = [], [], []
    for k in range(n // size):
        at = slice(k * size, (k + 1) * size)
        block = l_ref[at, at]
        diag = jnp.where(row == col, block, 0.0)
        by_row = 1.0 / diag.sum(1, keepdims=True)
        scales.append(1.0 / diag.sum(0, keepdims=True))
        nil = jnp.where(row > col, block, 0.0) * (-by_row)
        results.append(jnp.where(row == col, 1.0, 0.0) + nil)
        powers.append(nil)
    for _ in range(6):
        powers = [hdot(p, p) for p in powers]
        results = [r + hdot(r, p) for r, p in zip(results, powers)]
    inv_ref[...] = jnp.zeros_like(inv_ref)
    for k in range(n // size):
        at = slice(k * size, (k + 1) * size)
        inv_ref[at, at] = results[k] * scales[k]
    while size < n:
        for k in range(0, n, 2 * size):
            a, b = slice(k, k + size), slice(k + size, k + 2 * size)
            inv_ref[b, a] = -hdot(inv_ref[b, b], hdot(l_ref[b, a], inv_ref[a, a]))
        size *= 2
    invt_ref[...] = inv_ref[...].T
    c_ref[...] = hdot(l_ref[...].T, bar_ref[...])
    base_ref[...] = hdot(own_bar_ref[...].T, own_ref[...])


def inverse(l11, l11_bar, own_bar, own):
    out = jax.ShapeDtypeStruct(l11.shape, F32)
    return pl.pallas_call(
        inverse_kernel,
        out_shape=[out] * 4,
        compiler_params=pltpu.CompilerParams(vmem_limit_bytes=LIMIT * MIB),
        cost_estimate=COST,
        name="inverse",
    )(l11, l11_bar, own_bar, own)


def final_kernel(sc, own_ref, other_ref, c_ref, inv_ref, invt_ref, out_ref, packed, p_ref):
    n = c_ref.shape[0]
    half = packed.shape[0] // 2
    packed[pl.ds(pl.multiple_of(sc[0] * half, half), half), :] = own_ref[...]
    packed[pl.ds(pl.multiple_of((1 - sc[0]) * half, half), half), :] = other_ref[...]
    p_ref[...] = jnp.zeros_like(p_ref)
    row = lax.broadcasted_iota(jnp.int32, (128, 128), 0)
    col = lax.broadcasted_iota(jnp.int32, (128, 128), 1)
    for k, (i, j) in enumerate(lower_blocks(n)):
        at = (slice(i * 128, (i + 1) * 128), slice(j * 128, (j + 1) * 128))
        x = c_ref[at] - packed[k * 128 : (k + 1) * 128, :]
        if i == j:
            x = jnp.where(row > col, x, jnp.where(row == col, 0.5 * x, 0.0))
        p_ref[at] = x
    q = dot3(*split(invt_ref[...]), *split(p_ref[...]))
    q = dot3(*split(q), *split(inv_ref[...]))
    out_ref[...] = 0.5 * (q + q.T)


def final(scal, own, other, c, inv, invt):
    return pl.pallas_call(
        final_kernel,
        grid_spec=pltpu.PrefetchScalarGridSpec(
            num_scalar_prefetch=1,
            grid=(1,),
            in_specs=[full(own.shape)] * 2 + [full(c.shape)] * 3,
            out_specs=full(c.shape),
            scratch_shapes=[
                pltpu.VMEM((2 * own.shape[0], own.shape[1]), F32),
                pltpu.VMEM(c.shape, F32),
            ],
        ),
        out_shape=jax.ShapeDtypeStruct(c.shape, F32),
        compiler_params=params(LIMIT),
        name="diagonal_tile",
    )(scal, own, other, c, inv, invt)


def panel_kernel(sc, bar_ref, inv_ref, y_ref, z_ref, t_ref, u_ref, out_ref, rg_ref):
    n = bar_ref.shape[0]
    cut = y_ref.shape[0] - 8
    rest = z_ref[0]
    for k in range(1, z_ref.shape[0]):
        rest = rest + z_ref[k]
    t = t_ref[...] + u_ref[...]
    total = jnp.concatenate([y_ref[:cut, :], rest[: n - cut, :]], 0) + t[:n, :]
    out_ref[...] = dot3(*split(bar_ref[...] - total), *split(inv_ref[...]))
    tiles = cut // 64
    sums = t[n:, :128]
    take = lambda a: jnp.where(sc[0] == 1, a[:, 64:128], a[:, :64])
    rg_ref[:tiles, :] = take((sums[:tiles, :] + y_ref[cut : cut + tiles, :128]))
    more = n // 64 - tiles
    rg_ref[tiles:, :] = take(sums[tiles : tiles + more, :] + rest[n - cut : n - cut + more, :128])


def panel(scal, bar, inv, parts):
    n, width = bar.shape
    return pl.pallas_call(
        panel_kernel,
        grid_spec=pltpu.PrefetchScalarGridSpec(
            num_scalar_prefetch=1,
            grid=(1,),
            in_specs=[full(bar.shape), full(inv.shape)] + [full(p.shape) for p in parts],
            out_specs=[full(bar.shape), full((n // 64, 64))],
        ),
        out_shape=[
            jax.ShapeDtypeStruct(bar.shape, F32),
            jax.ShapeDtypeStruct((n // 64, 64), F32),
        ],
        compiler_params=params(LIMIT),
        cost_estimate=COST,
        name="panel_tiles",
    )(scal, bar, inv, *parts)


def permutations():
    def make(move):
        pairs = []
        for z in range(4):
            for yh in range(2):
                for core in range(2):
                    for yl in range(2):
                        for x in range(4):
                            nz, nyh, nc, nyl, nx = move(z, yh, core, yl, x)
                            src = (z * 4 + yh * 2 + core) * 8 + yl * 4 + x
                            dst = (nz * 4 + nyh * 2 + nc) * 8 + nyl * 4 + nx
                            pairs.append((src, dst))
        return pairs

    perms = {
        "x+": make(lambda z, h, c, l, x: (z, h, c, l, (x + 1) % 4)),
        "x-": make(lambda z, h, c, l, x: (z, h, c, l, (x + 3) % 4)),
        "x2": make(lambda z, h, c, l, x: (z, h, c, l, (x + 2) % 4)),
        "z+": make(lambda z, h, c, l, x: ((z + 1) % 4, h, c, l, x)),
        "z-": make(lambda z, h, c, l, x: ((z + 3) % 4, h, c, l, x)),
        "z^1": make(lambda z, h, c, l, x: (z ^ 1, h, c, l, x)),
        "z^2": make(lambda z, h, c, l, x: (z ^ 2, h, c, l, x)),
        "z^3": make(lambda z, h, c, l, x: (z ^ 3, h, c, l, x)),
        "yl": make(lambda z, h, c, l, x: (z, h, c, 1 - l, x)),
        "yh": make(lambda z, h, c, l, x: (z, 1 - h, c, l, x)),
        "yhl": make(lambda z, h, c, l, x: (z, 1 - h, c, 1 - l, x)),
        "core": make(lambda z, h, c, l, x: (z, h, 1 - c, l, x)),
    }
    home = lambda z, h, c, l, x: ((z // 2) * 2 + l, x // 2, x % 2, z % 2, h * 2 + c)
    flip = lambda z, h, c, l, x: ((z // 2) * 2 + l, 1 - x // 2, x % 2, z % 2, h * 2 + c)
    perms["home0"] = make(home)
    perms["home1"] = make(flip)
    perms["back0"] = [(d, s) for s, d in perms["home0"]]
    perms["back1"] = [(d, s) for s, d in perms["home1"]]
    return perms


PERMS = permutations()


AXES = ("z", "yh", "core", "yl", "x")


def move(value, name):
    return lax.ppermute(value, AXES, PERMS[name])


def after(values, *deps):
    return lax.optimization_barrier((values, deps))[0]


def per_device(s_bar, l21, panel_column_cotangent, l11, l11_bar, coords, sigma, length, tile_block):
    z, yh, core, yl, x = (lax.axis_index(a) for a in AXES)
    row_id = z * 4 + yh * 2 + core
    col_id = yl * 4 + x
    count, _, width, tiles_c = s_bar.shape[:4]
    part = l21.shape[2]
    rows, cols = count * width, tiles_c * width
    own = l21.reshape(count, part, width)
    own_bar = panel_column_cotangent.reshape(count * part, width)
    ints = lambda vals: jnp.stack([jnp.asarray(v, jnp.int32) for v in vals])

    row_tiles = [i * 16 + row_id for i in range(count)]
    col_tiles = [j * 8 + col_id for j in range(tiles_c)]
    starts = jnp.take(tile_block, ints(row_tiles + col_tiles)) * width
    s_view = s_bar.reshape(rows * cols // 128, 128)
    sig, len_ = sigma.reshape(1, -1), length.reshape(1, -1)

    rw = {(0, 0): own}
    rw[1, 0] = move(own, "yl")
    rw[0, 3] = move(own, "x+")
    rw[0, 1] = move(own, "x-")
    rw[0, 2] = move(own, "x2")
    home = move(own, "home0")

    part_blocks = rows // ROWS // 2
    feats = (s_view, coords, sig, len_)
    bufs = prep(0, part_blocks, starts, *feats, None, rows, cols)
    near, home = after((rw[1, 0], home), bufs[3])
    starts = after(starts, near, home)
    col_own = lax.all_gather(home, ("z", "yh"))
    rw[1, 3] = move(near, "x+")
    rw[1, 1] = move(near, "x-")
    rw[1, 2] = move(near, "x2")
    s_hi, s_lo, rsum, csum = prep(part_blocks, part_blocks, starts, *feats, bufs, rows, cols)

    row_keys = [(a, b) for a in range(2) for b in range(4)]
    scal = ints(
        [(yh ^ a) * 2 + (core ^ b) for a in range(2) for b in range(2)]
        + [(yl ^ a) * 4 + (x + b) % 4 for a, b in row_keys]
    )
    own_t, other_t, *tts = trans_product(
        after(scal, csum), [rw[k] for k in row_keys], s_hi, s_lo, csum
    )
    other_t = move(other_t, "core")
    col_other = move(after(col_own, tts[0]), "core")
    flat = own.reshape(count * part, width)
    inv, invt, c_mat, base = inverse(after(l11, tts[0]), l11_bar, own_bar, flat)
    t_sum = own_t + after(other_t, inv, col_own)
    t_sum = lax.psum_scatter(t_sum.reshape(4, 2, -1, width), "z", scatter_dimension=0)

    ch, cl, eo, ex = column_panels(after(ints([core]), inv), col_own, col_other, base, tts)
    others, n_others = ("z", "yh", "yl", "x"), 64
    e = eo + move(ex, "core")
    e = e.reshape(n_others, -1, 128)
    y = direct_product(after(ch, e), cl, s_hi, s_lo, rsum, 0, 2)
    e = lax.all_to_all(e, others, 0, 0).sum(0)
    e = jnp.broadcast_to(e[None], (n_others,) + e.shape)
    rest = direct_product(after(ch, y, e, t_sum), cl, s_hi, s_lo, rsum, 2, 1)
    y = lax.psum_scatter(y, ("yl", "x"), scatter_dimension=0)
    e = lax.all_to_all(e, others, 0, 0)
    rest = lax.all_to_all(rest, ("yl", "x"), 0, 0)
    t0 = move(t_sum[0], "back0")
    t1 = move(t_sum[1], "back1")
    e = e.reshape(eo.shape)
    grad11 = final(ints([core]), e, move(e, "core"), c_mat, inv, invt)
    grad21, row_grad = panel(ints([x % 2]), own_bar, inv, [y, rest, t0, t1])
    return (
        grad21.reshape(count, 1, part, width),
        grad11,
        row_grad.reshape(count, 1, part),
    )


def solution(mesh):
    fine = jax.sharding.Mesh(mesh.devices.reshape(4, 2, 2, 2, 4), AXES)
    prow, pcol = AXES[:3], AXES[3:]
    in_specs = (
        P(None, prow, None, None, pcol, None),
        P(None, prow, pcol, None),
        P(None, prow, pcol, None),
        P(),
        P(),
        P(),
        P(),
        P(),
        P(),
    )
    out_specs = (P(None, prow, pcol, None), P(), P(None, prow, pcol))
    return jax.shard_map(
        per_device, mesh=fine, in_specs=in_specs, out_specs=out_specs, check_vma=False
    )
```

```python
import math

import jax
import jax.numpy as jnp
from jax import lax
from jax.experimental import pallas as pl
from jax.experimental.pallas import tpu as pltpu
from jax.sharding import PartitionSpec as P

HIGH_PRECISION = lax.Precision.HIGHEST
F32 = jnp.float32
BF16 = jnp.bfloat16
SCALE = math.sqrt(12.0) * math.log2(math.e)
MIB = 1024 * 1024
LIMIT = 60
COST = pl.CostEstimate(flops=10**8, bytes_accessed=10**5, transcendentals=0)


def params(mib, dims=1):
    return pltpu.CompilerParams(
        vmem_limit_bytes=mib * MIB, dimension_semantics=("arbitrary",) * dims
    )


def split(value):
    high = value.astype(BF16)
    low = (value - high.astype(F32)).astype(BF16)
    return high, low


def dot(a, b):
    return jnp.dot(a, b, preferred_element_type=F32)


def dot3(a_high, a_low, b_high, b_low):
    return dot(a_high, b_high) + dot(a_low, b_high) + dot(a_high, b_low)


def full(shape, **kw):
    return pl.BlockSpec(shape, lambda *_: (0,) * len(shape), **kw)


def once(shape):
    return full(shape, pipeline_mode=pl.Buffered(1))


ROWS = 128
GROUP = 16


def prep_kernel(first, starts, *refs):
    s_ref, co_ref, sg_ref, le_ref = refs[:4]
    hi_ref, lo_ref, rs_ref, cs_ref, cacc, feat, racc_ref = refs[-7:]
    step = pl.program_id(0)
    tiles_c = cs_ref.shape[0] // 4
    chunks = 4 * tiles_c
    block = first + step
    row_off = pl.multiple_of(starts[block // 4] + (block % 4) * ROWS, ROWS)

    @pl.when(step == 0)
    def _():
        cacc[...] = jnp.zeros_like(cacc)
        for j in range(tiles_c):
            off = pl.multiple_of(starts[3 + j], 512)
            for k in range(4):
                c = j * 4 + k
                at = pl.ds(pl.multiple_of(off + k * 128, 128), 128)
                feat[0, pl.ds(c, 1), :] = co_ref[0:1, at]
                feat[1, pl.ds(c, 1), :] = co_ref[1:2, at]
                feat[2, pl.ds(c, 1), :] = sg_ref[0:1, at]
                feat[3, pl.ds(c, 1), :] = le_ref[0:1, at] * (1.0 / SCALE)

    at = pl.ds(row_off, ROWS)

    def column(row):
        return jnp.broadcast_to(row, (ROWS, ROWS)).T

    racc_ref[1] = column(co_ref[0:1, at])
    racc_ref[2] = column(co_ref[1:2, at])
    racc_ref[3] = column(sg_ref[0:1, at])
    racc_ref[4] = column(le_ref[0:1, at] * (1.0 / SCALE))

    def body(g, _):
        base = pl.multiple_of(g * GROUP, GROUP)
        rows = pl.ds(base, GROUP)
        row_x, row_y, row_s, row_l = (racc_ref[k, rows, :] for k in range(1, 5))
        acc = jnp.zeros((GROUP, 128), F32)
        for c in range(chunks):
            s = s_ref[pl.ds(base * chunks + c, GROUP, stride=chunks), :]
            dx = row_x - feat[0, c : c + 1, :]
            dy = row_y - feat[1, c : c + 1, :]
            dist2 = dx * dx + dy * dy
            scale = row_l + feat[3, c : c + 1, :]
            g2 = dist2 * lax.rsqrt(jnp.maximum(dist2 * (scale * scale), 1e-30))
            weighted = s * ((1.0 + g2 * math.log(2.0)) * jnp.exp2(-g2))
            acc = acc + weighted * feat[2, c : c + 1, :]
            by_row = weighted * row_s
            cacc[c] += by_row.reshape(GROUP // 8, 8, 128).sum(0)
            high, low = split(s)
            hi_ref[rows, c * 128 : (c + 1) * 128] = high
            lo_ref[rows, c * 128 : (c + 1) * 128] = low
        racc_ref[0, rows, :] = acc * row_s
        return 0

    lax.fori_loop(0, ROWS // GROUP, body, 0)
    rs_ref[0] = racc_ref[0].T.sum(0, keepdims=True)

    @pl.when(step == pl.num_programs(0) - 1)
    def _():
        total = cacc[...].sum(1) * feat[2]
        cs_ref[...] = total if first == 0 else refs[7][...] + total


def prep(first, per, starts, s_view, coords, sigma, length, bufs, rows, cols):
    chunks = cols // 128
    any_spec = pl.BlockSpec(memory_space=pl.ANY)
    out_map = lambda s, st: (first + s, 0)
    args = [starts, s_view, coords, sigma, length]
    in_specs = [
        pl.BlockSpec((ROWS * chunks, 128), out_map),
        full(coords.shape),
        full(sigma.shape),
        full(length.shape),
    ]
    aliases = {}
    if first:
        args += list(bufs)
        in_specs += [any_spec, any_spec, any_spec, full((chunks, 128))]
        aliases = {5: 0, 6: 1, 7: 2}
    return pl.pallas_call(
        lambda *refs: prep_kernel(first, *refs),
        grid_spec=pltpu.PrefetchScalarGridSpec(
            num_scalar_prefetch=1,
            grid=(per,),
            in_specs=in_specs,
            out_specs=[
                pl.BlockSpec((ROWS, cols), out_map),
                pl.BlockSpec((ROWS, cols), out_map),
                pl.BlockSpec((1, 1, ROWS), lambda s, st: (first + s, 0, 0)),
                pl.BlockSpec((chunks, 128), lambda s, st: (0, 0)),
            ],
            scratch_shapes=[
                pltpu.VMEM((chunks, 8, 128), F32),
                pltpu.VMEM((4, chunks, 128), F32),
                pltpu.VMEM((5, ROWS, ROWS), F32),
            ],
        ),
        out_shape=[
            jax.ShapeDtypeStruct((rows, cols), BF16),
            jax.ShapeDtypeStruct((rows, cols), BF16),
            jax.ShapeDtypeStruct((rows // ROWS, 1, ROWS), F32),
            jax.ShapeDtypeStruct((chunks, 128), F32),
        ],
        input_output_aliases=aliases,
        compiler_params=params(LIMIT),
        cost_estimate=COST,
        name="kernel_sums",
    )(*args)


def put_row(ref, base, at, value):
    rows = pl.ds(base, 8)
    mask = lax.broadcasted_iota(jnp.int32, (8, 128), 0) == at
    ref[rows, :128] = jnp.where(mask, value, ref[rows, :128])


def trans_kernel(sc, *refs):
    pieces, refs = refs[:8], refs[8:]
    count, part, width = pieces[0].shape
    s_high, s_low, cs_ref = refs[:count], refs[count : 2 * count], refs[2 * count]
    own_ref, other_ref, tth_ref, ttl_ref, th_ref, tl_ref, rows_ref = refs[2 * count + 1 : -count]
    tmps = refs[-count:]
    zp = pl.program_id(0)
    base = count * part

    @pl.when(zp == 0)
    def _():
        for r in range(8):
            for i in range(count):
                at = pl.multiple_of(i * 512 + sc[4 + r] * part, part)
                rows_ref[pl.ds(at, part), :] = pieces[r][i]
        for k in range(count * 4):
            at = slice(k * 128, (k + 1) * 128)
            high, low = split(rows_ref[at, :].T)
            th_ref[:, at] = high
            tl_ref[:, at] = low

    for i in range(count):
        out = dot3(th_ref[...], tl_ref[...], s_high[i][...], s_low[i][...])
        tmps[i][...] = out.T
        tth_ref[i], ttl_ref[i] = split(out)
    for ref, dcore in ((own_ref, 0), (other_ref, 1)):
        for dyh in range(2):
            sub = sc[dyh * 2 + dcore]
            at = pl.ds(pl.multiple_of(sub * part, part), part)
            ref[dyh, base:, :] = jnp.zeros((8, width), F32)
            for i in range(count):
                ref[dyh, i * part : (i + 1) * part, :] = tmps[i][at, :]
                ref[dyh, base + i : base + i + 1, :128] = cs_ref[
                    pl.ds(i * 8 + zp * 2 + sub // 2, 1), :
                ]


def trans_product(scal, pieces, s_hi, s_lo, csum):
    count, part, width = pieces[0].shape
    rows, cols = s_hi.shape
    high = count * part + 8
    s_specs = [
        pl.BlockSpec((rows, 256), lambda step, sc, i=i: (0, i * 4 + step)) for i in range(count)
    ]
    o_spec = pl.BlockSpec((2, high, width), lambda step, sc: (step, 0, 0))
    return pl.pallas_call(
        trans_kernel,
        grid_spec=pltpu.PrefetchScalarGridSpec(
            num_scalar_prefetch=1,
            grid=(4,),
            in_specs=[once(p.shape) for p in pieces] + s_specs * 2 + [full(csum.shape)],
            out_specs=[o_spec] * 2
            + [pl.BlockSpec((count, width, 256), lambda step, sc: (0, 0, step))] * 2,
            scratch_shapes=[pltpu.VMEM((width, rows), BF16)] * 2
            + [pltpu.VMEM((rows, width), F32)]
            + [pltpu.VMEM((256, width), F32)] * count,
        ),
        out_shape=[jax.ShapeDtypeStruct((8, high, width), F32)] * 2
        + [jax.ShapeDtypeStruct((count, width, 1024), BF16)] * 2,
        compiler_params=params(LIMIT),
        cost_estimate=COST,
        name="transposed_product",
    )(scal, *pieces, *[s_hi] * count, *[s_lo] * count, csum)


def lower_blocks(n):
    return [(i, j) for i in range(n // 128) for j in range(i + 1)]


def cols_kernel(sc, own_ref, other_ref, base_ref, tth_ref, ttl_ref, *refs):
    ch_ref, cl_ref, eo_ref, ex_ref, acc, packed = refs
    groups, _, part, width = own_ref.shape
    step = pl.program_id(0)
    for ref, core in ((own_ref, sc[0]), (other_ref, 1 - sc[0])):
        for g in range(groups):
            at = pl.ds(pl.multiple_of((g * 2 + core) * part, part), part)
            high, low = split(ref[g, 0])
            ch_ref[at, :] = high
            cl_ref[at, :] = low
    gram = dot3(tth_ref[0], ttl_ref[0], ch_ref[...], cl_ref[...])

    @pl.when(step == 0)
    def _():
        acc[...] = gram

    @pl.when(step > 0)
    def _():
        acc[...] += gram

    @pl.when(step == pl.num_programs(0) - 1)
    def _():
        total = acc[...]
        total = base_ref[...] - total - total.T
        for k, (i, j) in enumerate(lower_blocks(width)):
            packed[k * 128 : (k + 1) * 128, :] = total[
                i * 128 : (i + 1) * 128, j * 128 : (j + 1) * 128
            ]
        half = packed.shape[0] // 2
        eo_ref[...] = packed[pl.ds(pl.multiple_of(sc[0] * half, half), half), :]
        ex_ref[...] = packed[pl.ds(pl.multiple_of((1 - sc[0]) * half, half), half), :]


def column_panels(scal, own, other, base, tts):
    groups, count, part, width = own.shape
    cols = groups * count * part * 2
    half = len(lower_blocks(width)) * 64
    return pl.pallas_call(
        cols_kernel,
        grid_spec=pltpu.PrefetchScalarGridSpec(
            num_scalar_prefetch=1,
            grid=(count,),
            in_specs=[pl.BlockSpec((groups, 1, part, width), lambda i, sc: (0, i, 0, 0))] * 2
            + [once(base.shape)]
            + [pl.BlockSpec((1,) + tts[0].shape[1:], lambda i, sc: (i, 0, 0))] * 2,
            out_specs=[pl.BlockSpec((cols // count, width), lambda i, sc: (i, 0))] * 2
            + [full((half, 128))] * 2,
            scratch_shapes=[pltpu.VMEM((width, width), F32), pltpu.VMEM((2 * half, 128), F32)],
        ),
        out_shape=[jax.ShapeDtypeStruct((cols, width), BF16)] * 2
        + [jax.ShapeDtypeStruct((half, 128), F32)] * 2,
        compiler_params=params(LIMIT),
        cost_estimate=COST,
        name="column_panels",
    )(scal, own, other, base, *tts)


def direct_product(ch, cl, s_hi, s_lo, rsum, first, count):
    cols, width = ch.shape
    part = 64
    base = count * part
    row_block = lambda step: (first + step % count) * 2 + step // count

    def kernel(ch_ref, cl_ref, sh_ref, sl_ref, rs_ref, y_ref):
        step = pl.program_id(0)
        tile = step % count
        out = dot3(sh_ref[...], sl_ref[...], ch_ref[...], cl_ref[...])
        rows_at = pl.ds(pl.multiple_of(tile * part, part), part)

        @pl.when(tile == 0)
        def _():
            y_ref[:, base:, :] = jnp.zeros((4, 8, width), F32)

        for x in range(4):
            y_ref[x, rows_at, :] = out[x * part : (x + 1) * part, :]
            sums = rs_ref[(first + tile) * 4 + step // count * 2 + x // 2]
            put_row(y_ref.at[x], base, tile, sums)

    s_spec = pl.BlockSpec((256, cols), lambda step: (row_block(step), 0))
    return pl.pallas_call(
        kernel,
        grid=(2 * count,),
        in_specs=[once(ch.shape)] * 2 + [s_spec] * 2 + [full(rsum.shape)],
        out_specs=pl.BlockSpec((4, base + 8, width), lambda step: (step // count, 0, 0)),
        out_shape=jax.ShapeDtypeStruct((8, base + 8, width), F32),
        compiler_params=params(LIMIT),
        cost_estimate=pl.CostEstimate(
            flops=4 * 10**9 * (2 * count + 1), bytes_accessed=10**6, transcendentals=0
        ),
        name="direct_product",
    )(ch, cl, s_hi, s_lo, rsum)


def hdot(a, b):
    return jnp.dot(a, b, precision=HIGH_PRECISION, preferred_element_type=F32)


def inverse_kernel(l_ref, bar_ref, own_bar_ref, own_ref, inv_ref, invt_ref, c_ref, base_ref):
    n = l_ref.shape[0]
    size = 128
    row = lax.broadcasted_iota(jnp.int32, (size, size), 0)
    col = lax.broadcasted_iota(jnp.int32, (size, size), 1)
    powers, results, scales = [], [], []
    for k in range(n // size):
        at = slice(k * size, (k + 1) * size)
        block = l_ref[at, at]
        diag = jnp.where(row == col, block, 0.0)
        by_row = 1.0 / diag.sum(1, keepdims=True)
        scales.append(1.0 / diag.sum(0, keepdims=True))
        nil = jnp.where(row > col, block, 0.0) * (-by_row)
        results.append(jnp.where(row == col, 1.0, 0.0) + nil)
        powers.append(nil)
    for _ in range(6):
        powers = [hdot(p, p) for p in powers]
        results = [r + hdot(r, p) for r, p in zip(results, powers)]
    inv_ref[...] = jnp.zeros_like(inv_ref)
    for k in range(n // size):
        at = slice(k * size, (k + 1) * size)
        inv_ref[at, at] = results[k] * scales[k]
    while size < n:
        for k in range(0, n, 2 * size):
            a, b = slice(k, k + size), slice(k + size, k + 2 * size)
            inv_ref[b, a] = -hdot(inv_ref[b, b], hdot(l_ref[b, a], inv_ref[a, a]))
        size *= 2
    invt_ref[...] = inv_ref[...].T
    c_ref[...] = hdot(l_ref[...].T, bar_ref[...])
    base_ref[...] = hdot(own_bar_ref[...].T, own_ref[...])


def inverse(l11, l11_bar, own_bar, own):
    out = jax.ShapeDtypeStruct(l11.shape, F32)
    return pl.pallas_call(
        inverse_kernel,
        out_shape=[out] * 4,
        compiler_params=pltpu.CompilerParams(vmem_limit_bytes=LIMIT * MIB),
        cost_estimate=COST,
        name="inverse",
    )(l11, l11_bar, own_bar, own)


def final_kernel(sc, own_ref, other_ref, c_ref, inv_ref, invt_ref, out_ref, packed, p_ref):
    n = c_ref.shape[0]
    half = packed.shape[0] // 2
    packed[pl.ds(pl.multiple_of(sc[0] * half, half), half), :] = own_ref[...]
    packed[pl.ds(pl.multiple_of((1 - sc[0]) * half, half), half), :] = other_ref[...]
    p_ref[...] = jnp.zeros_like(p_ref)
    row = lax.broadcasted_iota(jnp.int32, (128, 128), 0)
    col = lax.broadcasted_iota(jnp.int32, (128, 128), 1)
    for k, (i, j) in enumerate(lower_blocks(n)):
        at = (slice(i * 128, (i + 1) * 128), slice(j * 128, (j + 1) * 128))
        x = c_ref[at] - packed[k * 128 : (k + 1) * 128, :]
        if i == j:
            x = jnp.where(row > col, x, jnp.where(row == col, 0.5 * x, 0.0))
        p_ref[at] = x
    q = dot3(*split(invt_ref[...]), *split(p_ref[...]))
    q = dot3(*split(q), *split(inv_ref[...]))
    out_ref[...] = 0.5 * (q + q.T)


def final(scal, own, other, c, inv, invt):
    return pl.pallas_call(
        final_kernel,
        grid_spec=pltpu.PrefetchScalarGridSpec(
            num_scalar_prefetch=1,
            grid=(1,),
            in_specs=[full(own.shape)] * 2 + [full(c.shape)] * 3,
            out_specs=full(c.shape),
            scratch_shapes=[
                pltpu.VMEM((2 * own.shape[0], own.shape[1]), F32),
                pltpu.VMEM(c.shape, F32),
            ],
        ),
        out_shape=jax.ShapeDtypeStruct(c.shape, F32),
        compiler_params=params(LIMIT),
        name="diagonal_tile",
    )(scal, own, other, c, inv, invt)


def panel_kernel(sc, bar_ref, inv_ref, y_ref, z_ref, t_ref, u_ref, out_ref, rg_ref):
    n = bar_ref.shape[0]
    cut = y_ref.shape[0] - 8
    rest = z_ref[0]
    for k in range(1, z_ref.shape[0]):
        rest = rest + z_ref[k]
    t = t_ref[...] + u_ref[...]
    total = jnp.concatenate([y_ref[:cut, :], rest[: n - cut, :]], 0) + t[:n, :]
    out_ref[...] = dot3(*split(bar_ref[...] - total), *split(inv_ref[...]))
    tiles = cut // 64
    sums = t[n:, :128]
    take = lambda a: jnp.where(sc[0] == 1, a[:, 64:128], a[:, :64])
    rg_ref[:tiles, :] = take((sums[:tiles, :] + y_ref[cut : cut + tiles, :128]))
    more = n // 64 - tiles
    rg_ref[tiles:, :] = take(sums[tiles : tiles + more, :] + rest[n - cut : n - cut + more, :128])


def panel(scal, bar, inv, parts):
    n, width = bar.shape
    return pl.pallas_call(
        panel_kernel,
        grid_spec=pltpu.PrefetchScalarGridSpec(
            num_scalar_prefetch=1,
            grid=(1,),
            in_specs=[full(bar.shape), full(inv.shape)] + [full(p.shape) for p in parts],
            out_specs=[full(bar.shape), full((n // 64, 64))],
        ),
        out_shape=[
            jax.ShapeDtypeStruct(bar.shape, F32),
            jax.ShapeDtypeStruct((n // 64, 64), F32),
        ],
        compiler_params=params(LIMIT),
        cost_estimate=COST,
        name="panel_tiles",
    )(scal, bar, inv, *parts)


def permutations():
    def make(move):
        pairs = []
        for z in range(4):
            for yh in range(2):
                for core in range(2):
                    for yl in range(2):
                        for x in range(4):
                            nz, nyh, nc, nyl, nx = move(z, yh, core, yl, x)
                            src = (z * 4 + yh * 2 + core) * 8 + yl * 4 + x
                            dst = (nz * 4 + nyh * 2 + nc) * 8 + nyl * 4 + nx
                            pairs.append((src, dst))
        return pairs

    perms = {
        "x+": make(lambda z, h, c, l, x: (z, h, c, l, (x + 1) % 4)),
        "x-": make(lambda z, h, c, l, x: (z, h, c, l, (x + 3) % 4)),
        "x2": make(lambda z, h, c, l, x: (z, h, c, l, (x + 2) % 4)),
        "z+": make(lambda z, h, c, l, x: ((z + 1) % 4, h, c, l, x)),
        "z-": make(lambda z, h, c, l, x: ((z + 3) % 4, h, c, l, x)),
        "z^1": make(lambda z, h, c, l, x: (z ^ 1, h, c, l, x)),
        "z^2": make(lambda z, h, c, l, x: (z ^ 2, h, c, l, x)),
        "z^3": make(lambda z, h, c, l, x: (z ^ 3, h, c, l, x)),
        "yl": make(lambda z, h, c, l, x: (z, h, c, 1 - l, x)),
        "yh": make(lambda z, h, c, l, x: (z, 1 - h, c, l, x)),
        "yhl": make(lambda z, h, c, l, x: (z, 1 - h, c, 1 - l, x)),
        "core": make(lambda z, h, c, l, x: (z, h, 1 - c, l, x)),
    }
    home = lambda z, h, c, l, x: ((z // 2) * 2 + l, x // 2, x % 2, z % 2, h * 2 + c)
    flip = lambda z, h, c, l, x: ((z // 2) * 2 + l, 1 - x // 2, x % 2, z % 2, h * 2 + c)
    perms["home0"] = make(home)
    perms["home1"] = make(flip)
    perms["back0"] = [(d, s) for s, d in perms["home0"]]
    perms["back1"] = [(d, s) for s, d in perms["home1"]]
    return perms


PERMS = permutations()


AXES = ("z", "yh", "core", "yl", "x")


def move(value, name):
    return lax.ppermute(value, AXES, PERMS[name])


def after(values, *deps):
    return lax.optimization_barrier((values, deps))[0]


def per_device(s_bar, l21, panel_column_cotangent, l11, l11_bar, coords, sigma, length, tile_block):
    z, yh, core, yl, x = (lax.axis_index(a) for a in AXES)
    row_id = z * 4 + yh * 2 + core
    col_id = yl * 4 + x
    count, _, width, tiles_c = s_bar.shape[:4]
    part = l21.shape[2]
    rows, cols = count * width, tiles_c * width
    own = l21.reshape(count, part, width)
    own_bar = panel_column_cotangent.reshape(count * part, width)
    ints = lambda vals: jnp.stack([jnp.asarray(v, jnp.int32) for v in vals])

    row_tiles = [i * 16 + row_id for i in range(count)]
    col_tiles = [j * 8 + col_id for j in range(tiles_c)]
    starts = jnp.take(tile_block, ints(row_tiles + col_tiles)) * width
    s_view = s_bar.reshape(rows * cols // 128, 128)
    sig, len_ = sigma.reshape(1, -1), length.reshape(1, -1)

    rw = {(0, 0): own}
    rw[1, 0] = move(own, "yl")
    rw[0, 3] = move(own, "x+")
    rw[0, 1] = move(own, "x-")
    home = move(own, "home0")

    part_blocks = rows // ROWS // 2
    feats = (s_view, coords, sig, len_)
    bufs = prep(0, part_blocks, starts, *feats, None, rows, cols)
    near, left, right, home = after((rw[1, 0], rw[0, 3], rw[0, 1], home), bufs[3])
    rw[0, 1] = right
    starts = after(starts, near, left, right, home)
    col_own = lax.all_gather(home, ("z", "yh"))
    rw[1, 3] = move(near, "x+")
    rw[1, 1] = move(near, "x-")
    rw[0, 2] = move(left, "x+")
    s_hi, s_lo, rsum, csum = prep(part_blocks, part_blocks, starts, *feats, bufs, rows, cols)

    rw[1, 2] = move(after(rw[1, 1], csum), "x-")
    flat = own.reshape(count * part, width)
    inv, invt, c_mat, base = inverse(after(l11, csum), l11_bar, own_bar, flat)

    row_keys = [(a, b) for a in range(2) for b in range(4)]
    scal = ints(
        [(yh ^ a) * 2 + (core ^ b) for a in range(2) for b in range(2)]
        + [(yl ^ a) * 4 + (x + b) % 4 for a, b in row_keys]
    )
    own_t, other_t, *tts = trans_product(
        after(scal, inv), [rw[k] for k in row_keys], s_hi, s_lo, csum
    )
    other_t = move(other_t, "core")
    col_other = move(after(col_own, tts[0]), "core")
    t_sum = own_t + after(other_t, col_own)
    t_part = lax.psum_scatter(t_sum.reshape(4, 2, -1, width), "z", scatter_dimension=0)

    ch, cl, eo, ex = column_panels(after(ints([core]), t_sum), col_own, col_other, base, tts)
    others, n_others = ("z", "yh", "yl", "x"), 64
    e = eo + move(ex, "core")
    e = e.reshape(n_others, -1, 128)
    y = direct_product(after(ch, e), cl, s_hi, s_lo, rsum, 0, 2)
    e = lax.all_to_all(e, others, 0, 0).sum(0)
    e = jnp.broadcast_to(e[None], (n_others,) + e.shape)
    y_part = lax.psum_scatter(after(y, e), ("yl", "x"), scatter_dimension=0)
    rest = direct_product(after(ch, e, y, t_part), cl, s_hi, s_lo, rsum, 2, 1)
    e = lax.all_to_all(e, others, 0, 0)
    rest = lax.all_to_all(rest, ("yl", "x"), 0, 0)
    t0 = move(t_part[0], "back0")
    t1 = move(t_part[1], "back1")
    e = e.reshape(eo.shape)
    grad11 = final(ints([core]), e, move(e, "core"), c_mat, inv, invt)
    grad21, row_grad = panel(ints([x % 2]), own_bar, inv, [y_part, rest, t0, t1])
    return (
        grad21.reshape(count, 1, part, width),
        grad11,
        row_grad.reshape(count, 1, part),
    )


def solution(mesh):
    fine = jax.sharding.Mesh(mesh.devices.reshape(4, 2, 2, 2, 4), AXES)
    prow, pcol = AXES[:3], AXES[3:]
    in_specs = (
        P(None, prow, None, None, pcol, None),
        P(None, prow, pcol, None),
        P(None, prow, pcol, None),
        P(),
        P(),
        P(),
        P(),
        P(),
        P(),
    )
    out_specs = (P(None, prow, pcol, None), P(), P(None, prow, pcol))
    return jax.shard_map(
        per_device, mesh=fine, in_specs=in_specs, out_specs=out_specs, check_vma=False
    )
```

```python
import math

import jax
import jax.numpy as jnp
from jax import lax
from jax.experimental import pallas as pl
from jax.experimental.pallas import tpu as pltpu
from jax.sharding import PartitionSpec as P

HIGH_PRECISION = lax.Precision.HIGHEST
F32 = jnp.float32
BF16 = jnp.bfloat16
SCALE = math.sqrt(12.0) * math.log2(math.e)
MIB = 1024 * 1024
LIMIT = 60
COST = pl.CostEstimate(flops=10**8, bytes_accessed=10**5, transcendentals=0)


def params(mib, dims=1):
    return pltpu.CompilerParams(
        vmem_limit_bytes=mib * MIB, dimension_semantics=("arbitrary",) * dims
    )


def split(value):
    high = value.astype(BF16)
    low = (value - high.astype(F32)).astype(BF16)
    return high, low


def dot(a, b):
    return jnp.dot(a, b, preferred_element_type=F32)


def dot3(a_high, a_low, b_high, b_low):
    return dot(a_high, b_high) + dot(a_low, b_high) + dot(a_high, b_low)


def full(shape, **kw):
    return pl.BlockSpec(shape, lambda *_: (0,) * len(shape), **kw)


def once(shape):
    return full(shape, pipeline_mode=pl.Buffered(1))


ROWS = 128
GROUP = 16


def prep_kernel(first, starts, *refs):
    s_ref, co_ref, sg_ref, le_ref = refs[:4]
    hi_ref, lo_ref, rs_ref, cs_ref, cacc, feat, racc_ref = refs[-7:]
    step = pl.program_id(0)
    tiles_c = cs_ref.shape[0] // 4
    chunks = 4 * tiles_c
    block = first + step
    row_off = pl.multiple_of(starts[block // 4] + (block % 4) * ROWS, ROWS)

    @pl.when(step == 0)
    def _():
        cacc[...] = jnp.zeros_like(cacc)
        for j in range(tiles_c):
            off = pl.multiple_of(starts[3 + j], 512)
            for k in range(4):
                c = j * 4 + k
                at = pl.ds(pl.multiple_of(off + k * 128, 128), 128)
                feat[0, pl.ds(c, 1), :] = co_ref[0:1, at]
                feat[1, pl.ds(c, 1), :] = co_ref[1:2, at]
                feat[2, pl.ds(c, 1), :] = sg_ref[0:1, at]
                feat[3, pl.ds(c, 1), :] = le_ref[0:1, at] * (1.0 / SCALE)

    at = pl.ds(row_off, ROWS)

    def column(row):
        return jnp.broadcast_to(row, (ROWS, ROWS)).T

    racc_ref[1] = column(co_ref[0:1, at])
    racc_ref[2] = column(co_ref[1:2, at])
    racc_ref[3] = column(sg_ref[0:1, at])
    racc_ref[4] = column(le_ref[0:1, at] * (1.0 / SCALE))

    def body(g, _):
        base = pl.multiple_of(g * GROUP, GROUP)
        rows = pl.ds(base, GROUP)
        row_x, row_y, row_s, row_l = (racc_ref[k, rows, :] for k in range(1, 5))
        acc = jnp.zeros((GROUP, 128), F32)
        for c in range(chunks):
            s = s_ref[pl.ds(base * chunks + c, GROUP, stride=chunks), :]
            dx = row_x - feat[0, c : c + 1, :]
            dy = row_y - feat[1, c : c + 1, :]
            dist2 = dx * dx + dy * dy
            scale = row_l + feat[3, c : c + 1, :]
            g2 = dist2 * lax.rsqrt(jnp.maximum(dist2 * (scale * scale), 1e-30))
            weighted = s * ((1.0 + g2 * math.log(2.0)) * jnp.exp2(-g2))
            acc = acc + weighted * feat[2, c : c + 1, :]
            by_row = weighted * row_s
            cacc[c] += by_row.reshape(GROUP // 8, 8, 128).sum(0)
            high, low = split(s)
            hi_ref[rows, c * 128 : (c + 1) * 128] = high
            lo_ref[rows, c * 128 : (c + 1) * 128] = low
        racc_ref[0, rows, :] = acc * row_s
        return 0

    lax.fori_loop(0, ROWS // GROUP, body, 0)
    rs_ref[0] = racc_ref[0].T.sum(0, keepdims=True)

    @pl.when(step == pl.num_programs(0) - 1)
    def _():
        total = cacc[...].sum(1) * feat[2]
        cs_ref[...] = total if first == 0 else refs[7][...] + total


def prep(first, per, starts, s_view, coords, sigma, length, bufs, rows, cols):
    chunks = cols // 128
    any_spec = pl.BlockSpec(memory_space=pl.ANY)
    out_map = lambda s, st: (first + s, 0)
    args = [starts, s_view, coords, sigma, length]
    in_specs = [
        pl.BlockSpec((ROWS * chunks, 128), out_map),
        full(coords.shape),
        full(sigma.shape),
        full(length.shape),
    ]
    aliases = {}
    if first:
        args += list(bufs)
        in_specs += [any_spec, any_spec, any_spec, full((chunks, 128))]
        aliases = {5: 0, 6: 1, 7: 2}
    return pl.pallas_call(
        lambda *refs: prep_kernel(first, *refs),
        grid_spec=pltpu.PrefetchScalarGridSpec(
            num_scalar_prefetch=1,
            grid=(per,),
            in_specs=in_specs,
            out_specs=[
                pl.BlockSpec((ROWS, cols), out_map),
                pl.BlockSpec((ROWS, cols), out_map),
                pl.BlockSpec((1, 1, ROWS), lambda s, st: (first + s, 0, 0)),
                pl.BlockSpec((chunks, 128), lambda s, st: (0, 0)),
            ],
            scratch_shapes=[
                pltpu.VMEM((chunks, 8, 128), F32),
                pltpu.VMEM((4, chunks, 128), F32),
                pltpu.VMEM((5, ROWS, ROWS), F32),
            ],
        ),
        out_shape=[
            jax.ShapeDtypeStruct((rows, cols), BF16),
            jax.ShapeDtypeStruct((rows, cols), BF16),
            jax.ShapeDtypeStruct((rows // ROWS, 1, ROWS), F32),
            jax.ShapeDtypeStruct((chunks, 128), F32),
        ],
        input_output_aliases=aliases,
        compiler_params=params(LIMIT),
        cost_estimate=COST,
        name="kernel_sums",
    )(*args)


def put_row(ref, base, at, value):
    rows = pl.ds(base, 8)
    mask = lax.broadcasted_iota(jnp.int32, (8, 128), 0) == at
    ref[rows, :128] = jnp.where(mask, value, ref[rows, :128])


def trans_kernel(sc, *refs):
    pieces, refs = refs[:8], refs[8:]
    count, part, width = pieces[0].shape
    s_high, s_low, cs_ref = refs[:count], refs[count : 2 * count], refs[2 * count]
    own_ref, other_ref, th_ref, tl_ref, rows_ref = refs[2 * count + 1 : -count]
    tmps = refs[-count:]
    zp = pl.program_id(0)
    base = count * part

    @pl.when(zp == 0)
    def _():
        for r in range(8):
            for i in range(count):
                at = pl.multiple_of(i * 512 + sc[4 + r] * part, part)
                rows_ref[pl.ds(at, part), :] = pieces[r][i]
        for k in range(count * 4):
            at = slice(k * 128, (k + 1) * 128)
            high, low = split(rows_ref[at, :].T)
            th_ref[:, at] = high
            tl_ref[:, at] = low

    for i in range(count):
        out = dot3(th_ref[...], tl_ref[...], s_high[i][...], s_low[i][...])
        tmps[i][...] = out.T
    for ref, dcore in ((own_ref, 0), (other_ref, 1)):
        for dyh in range(2):
            sub = sc[dyh * 2 + dcore]
            at = pl.ds(pl.multiple_of(sub * part, part), part)
            ref[dyh, base:, :] = jnp.zeros((8, width), F32)
            for i in range(count):
                ref[dyh, i * part : (i + 1) * part, :] = tmps[i][at, :]
                ref[dyh, base + i : base + i + 1, :128] = cs_ref[
                    pl.ds(i * 8 + zp * 2 + sub // 2, 1), :
                ]


def trans_product(scal, pieces, s_hi, s_lo, csum):
    count, part, width = pieces[0].shape
    rows, cols = s_hi.shape
    high = count * part + 8
    s_specs = [
        pl.BlockSpec((rows, 256), lambda step, sc, i=i: (0, i * 4 + step)) for i in range(count)
    ]
    o_spec = pl.BlockSpec((2, high, width), lambda step, sc: (step, 0, 0))
    return pl.pallas_call(
        trans_kernel,
        grid_spec=pltpu.PrefetchScalarGridSpec(
            num_scalar_prefetch=1,
            grid=(4,),
            in_specs=[once(p.shape) for p in pieces] + s_specs * 2 + [full(csum.shape)],
            out_specs=[o_spec] * 2 + [full((width, rows))] * 2,
            scratch_shapes=[pltpu.VMEM((rows, width), F32)]
            + [pltpu.VMEM((256, width), F32)] * count,
        ),
        out_shape=[jax.ShapeDtypeStruct((8, high, width), F32)] * 2
        + [jax.ShapeDtypeStruct((width, rows), BF16)] * 2,
        compiler_params=params(LIMIT),
        cost_estimate=COST,
        name="transposed_product",
    )(scal, *pieces, *[s_hi] * count, *[s_lo] * count, csum)


def lower_blocks(n):
    return [(i, j) for i in range(n // 128) for j in range(i + 1)]


def direct_kernel(sc, own_ref, other_ref, sh_ref, sl_ref, th_ref, tl_ref, rs_ref, base_ref, *refs):
    y_ref, eo_ref, ex_ref, ch_ref, cl_ref, acc, packed = refs
    groups, count, part, width = own_ref.shape
    step = pl.program_id(0)
    tile = step % count
    base = count * part

    @pl.when(step == 0)
    def _():
        for ref, core in ((own_ref, sc[0]), (other_ref, 1 - sc[0])):
            for g in range(groups):
                for i in range(count):
                    at = pl.multiple_of(i * 1024 + (g * 2 + core) * part, part)
                    high, low = split(ref[g, i])
                    ch_ref[pl.ds(at, part), :] = high
                    cl_ref[pl.ds(at, part), :] = low

    out = dot3(sh_ref[...], sl_ref[...], ch_ref[...], cl_ref[...])
    high, low = split(out)
    gram = dot3(th_ref[...], tl_ref[...], high, low)
    rows_at = pl.ds(pl.multiple_of(tile * part, part), part)

    @pl.when(tile == 0)
    def _():
        y_ref[:, base:, :] = jnp.zeros((4, 8, width), F32)

    for x in range(4):
        y_ref[x, rows_at, :] = out[x * part : (x + 1) * part, :]
        put_row(y_ref.at[x], base, tile, rs_ref[tile * 4 + step // count * 2 + x // 2])

    @pl.when(step == 0)
    def _():
        acc[...] = gram

    @pl.when(step > 0)
    def _():
        acc[...] += gram

    @pl.when(step == pl.num_programs(0) - 1)
    def _():
        total = acc[...]
        acc[...] = base_ref[...] - total - total.T
        for k, (i, j) in enumerate(lower_blocks(width)):
            packed[k * 128 : (k + 1) * 128, :] = acc[
                i * 128 : (i + 1) * 128, j * 128 : (j + 1) * 128
            ]
        half = packed.shape[0] // 2
        eo_ref[...] = packed[pl.ds(pl.multiple_of(sc[0] * half, half), half), :]
        ex_ref[...] = packed[pl.ds(pl.multiple_of((1 - sc[0]) * half, half), half), :]


def direct_product(scal, own, other, s_hi, s_lo, th, tl, rsum, base):
    groups, count, part, width = own.shape
    rows, cols = s_hi.shape
    high = count * part + 8
    half = len(lower_blocks(width)) * 64
    row_block = lambda step: step % count * 2 + step // count
    s_spec = pl.BlockSpec((256, cols), lambda step, sc: (row_block(step), 0))
    t_spec = pl.BlockSpec((width, 256), lambda step, sc: (0, row_block(step)))
    return pl.pallas_call(
        direct_kernel,
        grid_spec=pltpu.PrefetchScalarGridSpec(
            num_scalar_prefetch=1,
            grid=(2 * count,),
            in_specs=[once(own.shape)] * 2
            + [s_spec] * 2
            + [t_spec] * 2
            + [full(rsum.shape), once(base.shape)],
            out_specs=[pl.BlockSpec((4, high, width), lambda step, sc: (step // count, 0, 0))]
            + [full((half, 128))] * 2,
            scratch_shapes=[pltpu.VMEM((cols, width), BF16)] * 2
            + [pltpu.VMEM((width, width), F32), pltpu.VMEM((2 * half, 128), F32)],
        ),
        out_shape=[jax.ShapeDtypeStruct((8, high, width), F32)]
        + [jax.ShapeDtypeStruct((half, 128), F32)] * 2,
        compiler_params=params(LIMIT),
        cost_estimate=COST,
        name="direct_product",
    )(scal, own, other, s_hi, s_lo, th, tl, rsum, base)


def hdot(a, b):
    return jnp.dot(a, b, precision=HIGH_PRECISION, preferred_element_type=F32)


def inverse_kernel(l_ref, bar_ref, own_bar_ref, own_ref, inv_ref, invt_ref, c_ref, base_ref):
    n = l_ref.shape[0]
    size = 128
    row = lax.broadcasted_iota(jnp.int32, (size, size), 0)
    col = lax.broadcasted_iota(jnp.int32, (size, size), 1)
    powers, results, scales = [], [], []
    for k in range(n // size):
        at = slice(k * size, (k + 1) * size)
        block = l_ref[at, at]
        diag = jnp.where(row == col, block, 0.0)
        by_row = 1.0 / diag.sum(1, keepdims=True)
        scales.append(1.0 / diag.sum(0, keepdims=True))
        nil = jnp.where(row > col, block, 0.0) * (-by_row)
        results.append(jnp.where(row == col, 1.0, 0.0) + nil)
        powers.append(nil)
    for _ in range(6):
        powers = [hdot(p, p) for p in powers]
        results = [r + hdot(r, p) for r, p in zip(results, powers)]
    inv_ref[...] = jnp.zeros_like(inv_ref)
    for k in range(n // size):
        at = slice(k * size, (k + 1) * size)
        inv_ref[at, at] = results[k] * scales[k]
    while size < n:
        for k in range(0, n, 2 * size):
            a, b = slice(k, k + size), slice(k + size, k + 2 * size)
            inv_ref[b, a] = -hdot(inv_ref[b, b], hdot(l_ref[b, a], inv_ref[a, a]))
        size *= 2
    invt_ref[...] = inv_ref[...].T
    c_ref[...] = hdot(l_ref[...].T, bar_ref[...])
    base_ref[...] = hdot(own_bar_ref[...].T, own_ref[...])


def inverse(l11, l11_bar, own_bar, own):
    out = jax.ShapeDtypeStruct(l11.shape, F32)
    return pl.pallas_call(
        inverse_kernel,
        out_shape=[out] * 4,
        compiler_params=pltpu.CompilerParams(vmem_limit_bytes=LIMIT * MIB),
        cost_estimate=COST,
        name="inverse",
    )(l11, l11_bar, own_bar, own)


def final_kernel(sc, own_ref, other_ref, c_ref, inv_ref, invt_ref, out_ref, packed, p_ref):
    n = c_ref.shape[0]
    half = packed.shape[0] // 2
    packed[pl.ds(pl.multiple_of(sc[0] * half, half), half), :] = own_ref[...]
    packed[pl.ds(pl.multiple_of((1 - sc[0]) * half, half), half), :] = other_ref[...]
    p_ref[...] = jnp.zeros_like(p_ref)
    row = lax.broadcasted_iota(jnp.int32, (128, 128), 0)
    col = lax.broadcasted_iota(jnp.int32, (128, 128), 1)
    for k, (i, j) in enumerate(lower_blocks(n)):
        at = (slice(i * 128, (i + 1) * 128), slice(j * 128, (j + 1) * 128))
        x = c_ref[at] - packed[k * 128 : (k + 1) * 128, :]
        if i == j:
            x = jnp.where(row > col, x, jnp.where(row == col, 0.5 * x, 0.0))
        p_ref[at] = x
    q = dot3(*split(invt_ref[...]), *split(p_ref[...]))
    q = dot3(*split(q), *split(inv_ref[...]))
    out_ref[...] = 0.5 * (q + q.T)


def final(scal, own, other, c, inv, invt):
    return pl.pallas_call(
        final_kernel,
        grid_spec=pltpu.PrefetchScalarGridSpec(
            num_scalar_prefetch=1,
            grid=(1,),
            in_specs=[full(own.shape)] * 2 + [full(c.shape)] * 3,
            out_specs=full(c.shape),
            scratch_shapes=[
                pltpu.VMEM((2 * own.shape[0], own.shape[1]), F32),
                pltpu.VMEM(c.shape, F32),
            ],
        ),
        out_shape=jax.ShapeDtypeStruct(c.shape, F32),
        compiler_params=params(LIMIT),
        name="diagonal_tile",
    )(scal, own, other, c, inv, invt)


def panel_kernel(sc, bar_ref, inv_ref, *refs):
    parts, (out_ref, rg_ref) = refs[:-2], refs[-2:]
    n = bar_ref.shape[0]
    total = parts[0][...]
    for part in parts[1:]:
        total = total + part[...]
    out_ref[...] = dot3(*split(bar_ref[...] - total[:n, :]), *split(inv_ref[...]))
    sums = total[n:, :128]
    sums = jnp.where(sc[0] == 1, sums[:, 64:], sums[:, :64])
    rg_ref[...] = sums[: rg_ref.shape[0], :]


def panel(scal, bar, inv, parts):
    n, width = bar.shape
    return pl.pallas_call(
        panel_kernel,
        grid_spec=pltpu.PrefetchScalarGridSpec(
            num_scalar_prefetch=1,
            grid=(1,),
            in_specs=[full(bar.shape), full(inv.shape)] + [full(p.shape) for p in parts],
            out_specs=[full(bar.shape), full((n // 64, 64))],
        ),
        out_shape=[
            jax.ShapeDtypeStruct(bar.shape, F32),
            jax.ShapeDtypeStruct((n // 64, 64), F32),
        ],
        compiler_params=params(LIMIT),
        name="panel_tiles",
    )(scal, bar, inv, *parts)


def permutations():
    def make(move):
        pairs = []
        for z in range(4):
            for yh in range(2):
                for core in range(2):
                    for yl in range(2):
                        for x in range(4):
                            nz, nyh, nc, nyl, nx = move(z, yh, core, yl, x)
                            src = (z * 4 + yh * 2 + core) * 8 + yl * 4 + x
                            dst = (nz * 4 + nyh * 2 + nc) * 8 + nyl * 4 + nx
                            pairs.append((src, dst))
        return pairs

    perms = {
        "x+": make(lambda z, h, c, l, x: (z, h, c, l, (x + 1) % 4)),
        "x-": make(lambda z, h, c, l, x: (z, h, c, l, (x + 3) % 4)),
        "x2": make(lambda z, h, c, l, x: (z, h, c, l, (x + 2) % 4)),
        "z+": make(lambda z, h, c, l, x: ((z + 1) % 4, h, c, l, x)),
        "z-": make(lambda z, h, c, l, x: ((z + 3) % 4, h, c, l, x)),
        "z^1": make(lambda z, h, c, l, x: (z ^ 1, h, c, l, x)),
        "z^2": make(lambda z, h, c, l, x: (z ^ 2, h, c, l, x)),
        "z^3": make(lambda z, h, c, l, x: (z ^ 3, h, c, l, x)),
        "yl": make(lambda z, h, c, l, x: (z, h, c, 1 - l, x)),
        "yh": make(lambda z, h, c, l, x: (z, 1 - h, c, l, x)),
        "yhl": make(lambda z, h, c, l, x: (z, 1 - h, c, 1 - l, x)),
        "core": make(lambda z, h, c, l, x: (z, h, 1 - c, l, x)),
    }
    home = lambda z, h, c, l, x: ((z // 2) * 2 + l, x // 2, x % 2, z % 2, h * 2 + c)
    flip = lambda z, h, c, l, x: ((z // 2) * 2 + l, 1 - x // 2, x % 2, z % 2, h * 2 + c)
    perms["home0"] = make(home)
    perms["home1"] = make(flip)
    perms["back0"] = [(d, s) for s, d in perms["home0"]]
    perms["back1"] = [(d, s) for s, d in perms["home1"]]
    return perms


PERMS = permutations()


AXES = ("z", "yh", "core", "yl", "x")


def move(value, name):
    return lax.ppermute(value, AXES, PERMS[name])


def after(values, *deps):
    return lax.optimization_barrier((values, deps))[0]


def per_device(s_bar, l21, panel_column_cotangent, l11, l11_bar, coords, sigma, length, tile_block):
    z, yh, core, yl, x = (lax.axis_index(a) for a in AXES)
    row_id = z * 4 + yh * 2 + core
    col_id = yl * 4 + x
    count, _, width, tiles_c = s_bar.shape[:4]
    part = l21.shape[2]
    rows, cols = count * width, tiles_c * width
    own = l21.reshape(count, part, width)
    own_bar = panel_column_cotangent.reshape(count * part, width)
    ints = lambda vals: jnp.stack([jnp.asarray(v, jnp.int32) for v in vals])

    row_tiles = [i * 16 + row_id for i in range(count)]
    col_tiles = [j * 8 + col_id for j in range(tiles_c)]
    starts = jnp.take(tile_block, ints(row_tiles + col_tiles)) * width
    s_view = s_bar.reshape(rows * cols // 128, 128)
    sig, len_ = sigma.reshape(1, -1), length.reshape(1, -1)

    rw = {(0, 0): own}
    rw[1, 0] = move(own, "yl")
    rw[0, 3] = move(own, "x+")
    rw[0, 1] = move(own, "x-")
    home = move(own, "home0")

    part_blocks = rows // ROWS // 2
    feats = (s_view, coords, sig, len_)
    bufs = prep(0, part_blocks, starts, *feats, None, rows, cols)
    near, left, right, home = after((rw[1, 0], rw[0, 3], rw[0, 1], home), bufs[3])
    rw[0, 1] = right
    starts = after(starts, near, left, right, home)
    col_own = lax.all_gather(home, ("z", "yh"))
    rw[1, 3] = move(near, "x+")
    rw[1, 1] = move(near, "x-")
    rw[0, 2] = move(left, "x+")
    s_hi, s_lo, rsum, csum = prep(part_blocks, part_blocks, starts, *feats, bufs, rows, cols)
    rw[1, 2] = move(after(rw[1, 1], csum), "x-")

    flat = own.reshape(count * part, width)
    inv, invt, c_mat, base = inverse(after(l11, csum), l11_bar, own_bar, flat)

    row_keys = [(a, b) for a in range(2) for b in range(4)]
    scal = ints(
        [(yh ^ a) * 2 + (core ^ b) for a in range(2) for b in range(2)]
        + [(yl ^ a) * 4 + (x + b) % 4 for a, b in row_keys]
    )
    own_t, other_t, th, tl = trans_product(
        after(scal, inv), [rw[k] for k in row_keys], s_hi, s_lo, csum
    )
    other_t = move(other_t, "core")
    col_other = move(after(col_own, th), "core")
    t_sum = own_t + after(other_t, col_own[0, 0, 0, :1])
    t_sum = lax.psum_scatter(t_sum.reshape(4, 2, -1, width), "z", scatter_dimension=0)

    y, eo, ex = direct_product(
        after(ints([core]), inv), col_own, col_other, s_hi, s_lo, th, tl, rsum, base
    )
    y = lax.psum_scatter(y, ("yl", "x"), scatter_dimension=0)
    others, n_others = ("z", "yh", "yl", "x"), 64
    t0 = move(t_sum[0], "back0")
    t1 = move(t_sum[1], "back1")
    e = eo + move(ex, "core") + t_sum[0, -1, -1]
    e = lax.all_to_all(e.reshape(n_others, -1, 128), others, 0, 0).sum(0)
    e = e + (t0[-1, -1] + t1[-1, -1])
    e = lax.all_to_all(jnp.broadcast_to(e[None], (n_others,) + e.shape), others, 0, 0)
    e = e.reshape(eo.shape)
    grad11 = final(ints([core]), e, move(e, "core"), c_mat, inv, invt)
    grad21, row_grad = panel(ints([x % 2]), own_bar, inv, [y, t0, t1])
    return (
        grad21.reshape(count, 1, part, width),
        grad11,
        row_grad.reshape(count, 1, part),
    )


def solution(mesh):
    fine = jax.sharding.Mesh(mesh.devices.reshape(4, 2, 2, 2, 4), AXES)
    prow, pcol = AXES[:3], AXES[3:]
    in_specs = (
        P(None, prow, None, None, pcol, None),
        P(None, prow, pcol, None),
        P(None, prow, pcol, None),
        P(),
        P(),
        P(),
        P(),
        P(),
        P(),
    )
    out_specs = (P(None, prow, pcol, None), P(), P(None, prow, pcol))
    return jax.shard_map(
        per_device, mesh=fine, in_specs=in_specs, out_specs=out_specs, check_vma=False
    )
```

```python
import math

import jax
import jax.numpy as jnp
from jax import lax
from jax.experimental import pallas as pl
from jax.experimental.pallas import tpu as pltpu
from jax.sharding import PartitionSpec as P

HIGH_PRECISION = lax.Precision.HIGHEST
F32 = jnp.float32
BF16 = jnp.bfloat16
SCALE = math.sqrt(12.0) * math.log2(math.e)
MIB = 1024 * 1024
LIMIT = 60
COST = pl.CostEstimate(flops=10**8, bytes_accessed=10**5, transcendentals=0)


def params(mib, dims=1):
    return pltpu.CompilerParams(
        vmem_limit_bytes=mib * MIB, dimension_semantics=("arbitrary",) * dims
    )


def split(value):
    high = value.astype(BF16)
    low = (value - high.astype(F32)).astype(BF16)
    return high, low


def dot(a, b):
    return jnp.dot(a, b, preferred_element_type=F32)


def dot3(a_high, a_low, b_high, b_low):
    return dot(a_high, b_high) + dot(a_low, b_high) + dot(a_high, b_low)


def full(shape, **kw):
    return pl.BlockSpec(shape, lambda *_: (0,) * len(shape), **kw)


def once(shape):
    return full(shape, pipeline_mode=pl.Buffered(1))


ROWS = 128
GROUP = 16


def prep_kernel(first, starts, *refs):
    s_ref, co_ref, sg_ref, le_ref = refs[:4]
    hi_ref, lo_ref, rs_ref, cs_ref, cacc, feat, racc_ref = refs[-7:]
    step = pl.program_id(0)
    tiles_c = cs_ref.shape[0] // 4
    chunks = 4 * tiles_c
    block = first + step
    row_off = pl.multiple_of(starts[block // 4] + (block % 4) * ROWS, ROWS)

    @pl.when(step == 0)
    def _():
        cacc[...] = jnp.zeros_like(cacc)
        for j in range(tiles_c):
            off = pl.multiple_of(starts[3 + j], 512)
            for k in range(4):
                c = j * 4 + k
                at = pl.ds(pl.multiple_of(off + k * 128, 128), 128)
                feat[0, pl.ds(c, 1), :] = co_ref[0:1, at]
                feat[1, pl.ds(c, 1), :] = co_ref[1:2, at]
                feat[2, pl.ds(c, 1), :] = sg_ref[0:1, at]
                feat[3, pl.ds(c, 1), :] = le_ref[0:1, at] * (1.0 / SCALE)

    at = pl.ds(row_off, ROWS)

    def column(row):
        return jnp.broadcast_to(row, (ROWS, ROWS)).T

    racc_ref[1] = column(co_ref[0:1, at])
    racc_ref[2] = column(co_ref[1:2, at])
    racc_ref[3] = column(sg_ref[0:1, at])
    racc_ref[4] = column(le_ref[0:1, at] * (1.0 / SCALE))

    def body(g, _):
        base = pl.multiple_of(g * GROUP, GROUP)
        rows = pl.ds(base, GROUP)
        row_x, row_y, row_s, row_l = (racc_ref[k, rows, :] for k in range(1, 5))
        acc = jnp.zeros((GROUP, 128), F32)
        for c in range(chunks):
            s = s_ref[pl.ds(base * chunks + c, GROUP, stride=chunks), :]
            dx = row_x - feat[0, c : c + 1, :]
            dy = row_y - feat[1, c : c + 1, :]
            dist2 = dx * dx + dy * dy
            scale = row_l + feat[3, c : c + 1, :]
            g2 = dist2 * lax.rsqrt(jnp.maximum(dist2 * (scale * scale), 1e-30))
            weighted = s * ((1.0 + g2 * math.log(2.0)) * jnp.exp2(-g2))
            acc = acc + weighted * feat[2, c : c + 1, :]
            by_row = weighted * row_s
            cacc[c] += by_row.reshape(GROUP // 8, 8, 128).sum(0)
            high, low = split(s)
            hi_ref[rows, c * 128 : (c + 1) * 128] = high
            lo_ref[rows, c * 128 : (c + 1) * 128] = low
        racc_ref[0, rows, :] = acc * row_s
        return 0

    lax.fori_loop(0, ROWS // GROUP, body, 0)
    rs_ref[0] = racc_ref[0].T.sum(0, keepdims=True)

    @pl.when(step == pl.num_programs(0) - 1)
    def _():
        total = cacc[...].sum(1) * feat[2]
        cs_ref[...] = total if first == 0 else refs[7][...] + total


def prep(first, per, starts, s_view, coords, sigma, length, bufs, rows, cols):
    chunks = cols // 128
    any_spec = pl.BlockSpec(memory_space=pl.ANY)
    out_map = lambda s, st: (first + s, 0)
    args = [starts, s_view, coords, sigma, length]
    in_specs = [
        pl.BlockSpec((ROWS * chunks, 128), out_map),
        full(coords.shape),
        full(sigma.shape),
        full(length.shape),
    ]
    aliases = {}
    if first:
        args += list(bufs)
        in_specs += [any_spec, any_spec, any_spec, full((chunks, 128))]
        aliases = {5: 0, 6: 1, 7: 2}
    return pl.pallas_call(
        lambda *refs: prep_kernel(first, *refs),
        grid_spec=pltpu.PrefetchScalarGridSpec(
            num_scalar_prefetch=1,
            grid=(per,),
            in_specs=in_specs,
            out_specs=[
                pl.BlockSpec((ROWS, cols), out_map),
                pl.BlockSpec((ROWS, cols), out_map),
                pl.BlockSpec((1, 1, ROWS), lambda s, st: (first + s, 0, 0)),
                pl.BlockSpec((chunks, 128), lambda s, st: (0, 0)),
            ],
            scratch_shapes=[
                pltpu.VMEM((chunks, 8, 128), F32),
                pltpu.VMEM((4, chunks, 128), F32),
                pltpu.VMEM((5, ROWS, ROWS), F32),
            ],
        ),
        out_shape=[
            jax.ShapeDtypeStruct((rows, cols), BF16),
            jax.ShapeDtypeStruct((rows, cols), BF16),
            jax.ShapeDtypeStruct((rows // ROWS, 1, ROWS), F32),
            jax.ShapeDtypeStruct((chunks, 128), F32),
        ],
        input_output_aliases=aliases,
        compiler_params=params(LIMIT),
        cost_estimate=COST,
        name="kernel_sums",
    )(*args)


def put_row(ref, base, at, value):
    rows = pl.ds(base, 8)
    mask = lax.broadcasted_iota(jnp.int32, (8, 128), 0) == at
    ref[rows, :128] = jnp.where(mask, value, ref[rows, :128])


def trans_kernel(sc, *refs):
    pieces, refs = refs[:8], refs[8:]
    count, part, width = pieces[0].shape
    s_high, s_low, cs_ref = refs[:count], refs[count : 2 * count], refs[2 * count]
    own_ref, other_ref, th_ref, tl_ref, rows_ref = refs[2 * count + 1 : -count]
    tmps = refs[-count:]
    zp = pl.program_id(0)
    base = count * part

    @pl.when(zp == 0)
    def _():
        for r in range(8):
            for i in range(count):
                at = pl.multiple_of(i * 512 + sc[4 + r] * part, part)
                rows_ref[pl.ds(at, part), :] = pieces[r][i]
        for k in range(count * 4):
            at = slice(k * 128, (k + 1) * 128)
            high, low = split(rows_ref[at, :].T)
            th_ref[:, at] = high
            tl_ref[:, at] = low

    for i in range(count):
        out = dot3(th_ref[...], tl_ref[...], s_high[i][...], s_low[i][...])
        tmps[i][...] = out.T
    for ref, dcore in ((own_ref, 0), (other_ref, 1)):
        for dyh in range(2):
            sub = sc[dyh * 2 + dcore]
            at = pl.ds(pl.multiple_of(sub * part, part), part)
            ref[dyh, base:, :] = jnp.zeros((8, width), F32)
            for i in range(count):
                ref[dyh, i * part : (i + 1) * part, :] = tmps[i][at, :]
                ref[dyh, base + i : base + i + 1, :128] = cs_ref[
                    pl.ds(i * 8 + zp * 2 + sub // 2, 1), :
                ]


def trans_product(scal, pieces, s_hi, s_lo, csum):
    count, part, width = pieces[0].shape
    rows, cols = s_hi.shape
    high = count * part + 8
    s_specs = [
        pl.BlockSpec((rows, 256), lambda step, sc, i=i: (0, i * 4 + step)) for i in range(count)
    ]
    o_spec = pl.BlockSpec((2, high, width), lambda step, sc: (step, 0, 0))
    return pl.pallas_call(
        trans_kernel,
        grid_spec=pltpu.PrefetchScalarGridSpec(
            num_scalar_prefetch=1,
            grid=(4,),
            in_specs=[once(p.shape) for p in pieces] + s_specs * 2 + [full(csum.shape)],
            out_specs=[o_spec] * 2 + [full((width, rows))] * 2,
            scratch_shapes=[pltpu.VMEM((rows, width), F32)]
            + [pltpu.VMEM((256, width), F32)] * count,
        ),
        out_shape=[jax.ShapeDtypeStruct((8, high, width), F32)] * 2
        + [jax.ShapeDtypeStruct((width, rows), BF16)] * 2,
        compiler_params=params(LIMIT),
        cost_estimate=COST,
        name="transposed_product",
    )(scal, *pieces, *[s_hi] * count, *[s_lo] * count, csum)


def lower_blocks(n):
    return [(i, j) for i in range(n // 128) for j in range(i + 1)]


def direct_kernel(sc, own_ref, other_ref, sh_ref, sl_ref, th_ref, tl_ref, rs_ref, base_ref, *refs):
    y_ref, eo_ref, ex_ref, ch_ref, cl_ref, acc, packed = refs
    groups, count, part, width = own_ref.shape
    step = pl.program_id(0)
    tile = step % count
    base = count * part

    @pl.when(step == 0)
    def _():
        for ref, core in ((own_ref, sc[0]), (other_ref, 1 - sc[0])):
            for g in range(groups):
                for i in range(count):
                    at = pl.multiple_of(i * 1024 + (g * 2 + core) * part, part)
                    high, low = split(ref[g, i])
                    ch_ref[pl.ds(at, part), :] = high
                    cl_ref[pl.ds(at, part), :] = low

    out = dot3(sh_ref[...], sl_ref[...], ch_ref[...], cl_ref[...])
    high, low = split(out)
    gram = dot3(th_ref[...], tl_ref[...], high, low)
    rows_at = pl.ds(pl.multiple_of(tile * part, part), part)

    @pl.when(tile == 0)
    def _():
        y_ref[:, base:, :] = jnp.zeros((4, 8, width), F32)

    for x in range(4):
        y_ref[x, rows_at, :] = out[x * part : (x + 1) * part, :]
        put_row(y_ref.at[x], base, tile, rs_ref[tile * 4 + step // count * 2 + x // 2])

    @pl.when(step == 0)
    def _():
        acc[...] = gram

    @pl.when(step > 0)
    def _():
        acc[...] += gram

    @pl.when(step == pl.num_programs(0) - 1)
    def _():
        total = acc[...]
        acc[...] = base_ref[...] - total - total.T
        for k, (i, j) in enumerate(lower_blocks(width)):
            packed[k * 128 : (k + 1) * 128, :] = acc[
                i * 128 : (i + 1) * 128, j * 128 : (j + 1) * 128
            ]
        half = packed.shape[0] // 2
        eo_ref[...] = packed[pl.ds(pl.multiple_of(sc[0] * half, half), half), :]
        ex_ref[...] = packed[pl.ds(pl.multiple_of((1 - sc[0]) * half, half), half), :]


def direct_product(scal, own, other, s_hi, s_lo, th, tl, rsum, base):
    groups, count, part, width = own.shape
    rows, cols = s_hi.shape
    high = count * part + 8
    half = len(lower_blocks(width)) * 64
    row_block = lambda step: step % count * 2 + step // count
    s_spec = pl.BlockSpec((256, cols), lambda step, sc: (row_block(step), 0))
    t_spec = pl.BlockSpec((width, 256), lambda step, sc: (0, row_block(step)))
    return pl.pallas_call(
        direct_kernel,
        grid_spec=pltpu.PrefetchScalarGridSpec(
            num_scalar_prefetch=1,
            grid=(2 * count,),
            in_specs=[once(own.shape)] * 2
            + [s_spec] * 2
            + [t_spec] * 2
            + [full(rsum.shape), once(base.shape)],
            out_specs=[pl.BlockSpec((4, high, width), lambda step, sc: (step // count, 0, 0))]
            + [full((half, 128))] * 2,
            scratch_shapes=[pltpu.VMEM((cols, width), BF16)] * 2
            + [pltpu.VMEM((width, width), F32), pltpu.VMEM((2 * half, 128), F32)],
        ),
        out_shape=[jax.ShapeDtypeStruct((8, high, width), F32)]
        + [jax.ShapeDtypeStruct((half, 128), F32)] * 2,
        compiler_params=params(LIMIT),
        cost_estimate=COST,
        name="direct_product",
    )(scal, own, other, s_hi, s_lo, th, tl, rsum, base)


def hdot(a, b):
    return jnp.dot(a, b, precision=HIGH_PRECISION, preferred_element_type=F32)


def inverse_kernel(l_ref, bar_ref, own_bar_ref, own_ref, inv_ref, invt_ref, c_ref, base_ref):
    n = l_ref.shape[0]
    size = 128
    row = lax.broadcasted_iota(jnp.int32, (size, size), 0)
    col = lax.broadcasted_iota(jnp.int32, (size, size), 1)
    powers, results, scales = [], [], []
    for k in range(n // size):
        at = slice(k * size, (k + 1) * size)
        block = l_ref[at, at]
        diag = jnp.where(row == col, block, 0.0)
        by_row = 1.0 / diag.sum(1, keepdims=True)
        scales.append(1.0 / diag.sum(0, keepdims=True))
        nil = jnp.where(row > col, block, 0.0) * (-by_row)
        results.append(jnp.where(row == col, 1.0, 0.0) + nil)
        powers.append(nil)
    for _ in range(6):
        powers = [hdot(p, p) for p in powers]
        results = [r + hdot(r, p) for r, p in zip(results, powers)]
    inv_ref[...] = jnp.zeros_like(inv_ref)
    for k in range(n // size):
        at = slice(k * size, (k + 1) * size)
        inv_ref[at, at] = results[k] * scales[k]
    while size < n:
        for k in range(0, n, 2 * size):
            a, b = slice(k, k + size), slice(k + size, k + 2 * size)
            inv_ref[b, a] = -hdot(inv_ref[b, b], hdot(l_ref[b, a], inv_ref[a, a]))
        size *= 2
    invt_ref[...] = inv_ref[...].T
    c_ref[...] = hdot(l_ref[...].T, bar_ref[...])
    base_ref[...] = hdot(own_bar_ref[...].T, own_ref[...])


def inverse(l11, l11_bar, own_bar, own):
    out = jax.ShapeDtypeStruct(l11.shape, F32)
    return pl.pallas_call(
        inverse_kernel,
        out_shape=[out] * 4,
        compiler_params=pltpu.CompilerParams(vmem_limit_bytes=LIMIT * MIB),
        cost_estimate=COST,
        name="inverse",
    )(l11, l11_bar, own_bar, own)


def final_kernel(sc, own_ref, other_ref, c_ref, inv_ref, invt_ref, out_ref, packed, p_ref):
    n = c_ref.shape[0]
    half = packed.shape[0] // 2
    packed[pl.ds(pl.multiple_of(sc[0] * half, half), half), :] = own_ref[...]
    packed[pl.ds(pl.multiple_of((1 - sc[0]) * half, half), half), :] = other_ref[...]
    p_ref[...] = jnp.zeros_like(p_ref)
    row = lax.broadcasted_iota(jnp.int32, (128, 128), 0)
    col = lax.broadcasted_iota(jnp.int32, (128, 128), 1)
    for k, (i, j) in enumerate(lower_blocks(n)):
        at = (slice(i * 128, (i + 1) * 128), slice(j * 128, (j + 1) * 128))
        x = c_ref[at] - packed[k * 128 : (k + 1) * 128, :]
        if i == j:
            x = jnp.where(row > col, x, jnp.where(row == col, 0.5 * x, 0.0))
        p_ref[at] = x
    q = dot3(*split(invt_ref[...]), *split(p_ref[...]))
    q = dot3(*split(q), *split(inv_ref[...]))
    out_ref[...] = 0.5 * (q + q.T)


def final(scal, own, other, c, inv, invt):
    return pl.pallas_call(
        final_kernel,
        grid_spec=pltpu.PrefetchScalarGridSpec(
            num_scalar_prefetch=1,
            grid=(1,),
            in_specs=[full(own.shape)] * 2 + [full(c.shape)] * 3,
            out_specs=full(c.shape),
            scratch_shapes=[
                pltpu.VMEM((2 * own.shape[0], own.shape[1]), F32),
                pltpu.VMEM(c.shape, F32),
            ],
        ),
        out_shape=jax.ShapeDtypeStruct(c.shape, F32),
        compiler_params=params(LIMIT),
        name="diagonal_tile",
    )(scal, own, other, c, inv, invt)


def panel_kernel(sc, bar_ref, inv_ref, *refs):
    parts, (out_ref, rg_ref) = refs[:-2], refs[-2:]
    n = bar_ref.shape[0]
    total = parts[0][...]
    for part in parts[1:]:
        total = total + part[...]
    out_ref[...] = dot3(*split(bar_ref[...] - total[:n, :]), *split(inv_ref[...]))
    sums = total[n:, :128]
    sums = jnp.where(sc[0] == 1, sums[:, 64:], sums[:, :64])
    rg_ref[...] = sums[: rg_ref.shape[0], :]


def panel(scal, bar, inv, parts):
    n, width = bar.shape
    return pl.pallas_call(
        panel_kernel,
        grid_spec=pltpu.PrefetchScalarGridSpec(
            num_scalar_prefetch=1,
            grid=(1,),
            in_specs=[full(bar.shape), full(inv.shape)] + [full(p.shape) for p in parts],
            out_specs=[full(bar.shape), full((n // 64, 64))],
        ),
        out_shape=[
            jax.ShapeDtypeStruct(bar.shape, F32),
            jax.ShapeDtypeStruct((n // 64, 64), F32),
        ],
        compiler_params=params(LIMIT),
        name="panel_tiles",
    )(scal, bar, inv, *parts)


def permutations():
    def make(move):
        pairs = []
        for z in range(4):
            for yh in range(2):
                for core in range(2):
                    for yl in range(2):
                        for x in range(4):
                            nz, nyh, nc, nyl, nx = move(z, yh, core, yl, x)
                            src = (z * 4 + yh * 2 + core) * 8 + yl * 4 + x
                            dst = (nz * 4 + nyh * 2 + nc) * 8 + nyl * 4 + nx
                            pairs.append((src, dst))
        return pairs

    perms = {
        "x+": make(lambda z, h, c, l, x: (z, h, c, l, (x + 1) % 4)),
        "x-": make(lambda z, h, c, l, x: (z, h, c, l, (x + 3) % 4)),
        "x2": make(lambda z, h, c, l, x: (z, h, c, l, (x + 2) % 4)),
        "z+": make(lambda z, h, c, l, x: ((z + 1) % 4, h, c, l, x)),
        "z-": make(lambda z, h, c, l, x: ((z + 3) % 4, h, c, l, x)),
        "z^1": make(lambda z, h, c, l, x: (z ^ 1, h, c, l, x)),
        "z^2": make(lambda z, h, c, l, x: (z ^ 2, h, c, l, x)),
        "z^3": make(lambda z, h, c, l, x: (z ^ 3, h, c, l, x)),
        "yl": make(lambda z, h, c, l, x: (z, h, c, 1 - l, x)),
        "yh": make(lambda z, h, c, l, x: (z, 1 - h, c, l, x)),
        "yhl": make(lambda z, h, c, l, x: (z, 1 - h, c, 1 - l, x)),
        "core": make(lambda z, h, c, l, x: (z, h, 1 - c, l, x)),
    }
    home = lambda z, h, c, l, x: ((z // 2) * 2 + l, x // 2, x % 2, z % 2, h * 2 + c)
    flip = lambda z, h, c, l, x: ((z // 2) * 2 + l, 1 - x // 2, x % 2, z % 2, h * 2 + c)
    perms["home0"] = make(home)
    perms["home1"] = make(flip)
    perms["back0"] = [(d, s) for s, d in perms["home0"]]
    perms["back1"] = [(d, s) for s, d in perms["home1"]]
    return perms


PERMS = permutations()


AXES = ("z", "yh", "core", "yl", "x")


def move(value, name):
    return lax.ppermute(value, AXES, PERMS[name])


def after(values, *deps):
    return lax.optimization_barrier((values, deps))[0]


def per_device(s_bar, l21, panel_column_cotangent, l11, l11_bar, coords, sigma, length, tile_block):
    z, yh, core, yl, x = (lax.axis_index(a) for a in AXES)
    row_id = z * 4 + yh * 2 + core
    col_id = yl * 4 + x
    count, _, width, tiles_c = s_bar.shape[:4]
    part = l21.shape[2]
    rows, cols = count * width, tiles_c * width
    own = l21.reshape(count, part, width)
    own_bar = panel_column_cotangent.reshape(count * part, width)
    ints = lambda vals: jnp.stack([jnp.asarray(v, jnp.int32) for v in vals])

    row_tiles = [i * 16 + row_id for i in range(count)]
    col_tiles = [j * 8 + col_id for j in range(tiles_c)]
    starts = jnp.take(tile_block, ints(row_tiles + col_tiles)) * width
    s_view = s_bar.reshape(rows * cols // 128, 128)
    sig, len_ = sigma.reshape(1, -1), length.reshape(1, -1)

    rw = {(0, 0): own}
    rw[1, 0] = move(own, "yl")
    rw[0, 3] = move(own, "x+")
    rw[0, 1] = move(own, "x-")
    home = move(own, "home0")

    part_blocks = rows // ROWS // 2
    feats = (s_view, coords, sig, len_)
    bufs = prep(0, part_blocks, starts, *feats, None, rows, cols)
    near, left, right, home = after((rw[1, 0], rw[0, 3], rw[0, 1], home), bufs[3])
    rw[0, 1] = right
    starts = after(starts, near, left, right, home)
    col_own = lax.all_gather(home, ("z", "yh"))
    rw[1, 3] = move(near, "x+")
    rw[1, 1] = move(near, "x-")
    rw[0, 2] = move(left, "x+")
    s_hi, s_lo, rsum, csum = prep(part_blocks, part_blocks, starts, *feats, bufs, rows, cols)
    rw[1, 2] = move(after(rw[1, 1], csum), "x-")

    flat = own.reshape(count * part, width)
    inv, invt, c_mat, base = inverse(after(l11, csum), l11_bar, own_bar, flat)

    row_keys = [(a, b) for a in range(2) for b in range(4)]
    scal = ints(
        [(yh ^ a) * 2 + (core ^ b) for a in range(2) for b in range(2)]
        + [(yl ^ a) * 4 + (x + b) % 4 for a, b in row_keys]
    )
    own_t, other_t, th, tl = trans_product(
        after(scal, inv), [rw[k] for k in row_keys], s_hi, s_lo, csum
    )
    other_t = move(other_t, "core")
    col_other = move(after(col_own, th), "core")
    t_sum = own_t + other_t
    t_sum = lax.psum_scatter(t_sum.reshape(4, 2, -1, width), "z", scatter_dimension=0)

    y, eo, ex = direct_product(
        after(ints([core]), inv), col_own, col_other, s_hi, s_lo, th, tl, rsum, base
    )
    y = lax.psum_scatter(y, ("yl", "x"), scatter_dimension=0)
    others, n_others = ("z", "yh", "yl", "x"), 64
    e = eo + move(ex, "core")
    e = lax.all_to_all(e.reshape(n_others, -1, 128), others, 0, 0).sum(0)
    e = lax.all_to_all(jnp.broadcast_to(e[None], (n_others,) + e.shape), others, 0, 0)
    t_sum = after(t_sum, eo)
    t0 = move(t_sum[0], "back0")
    t1 = move(t_sum[1], "back1")
    e = e.reshape(eo.shape)
    grad11 = final(ints([core]), e, move(e, "core"), c_mat, inv, invt)
    grad21, row_grad = panel(ints([x % 2]), own_bar, inv, [y, t0, t1])
    return (
        grad21.reshape(count, 1, part, width),
        grad11,
        row_grad.reshape(count, 1, part),
    )


def solution(mesh):
    fine = jax.sharding.Mesh(mesh.devices.reshape(4, 2, 2, 2, 4), AXES)
    prow, pcol = AXES[:3], AXES[3:]
    in_specs = (
        P(None, prow, None, None, pcol, None),
        P(None, prow, pcol, None),
        P(None, prow, pcol, None),
        P(),
        P(),
        P(),
        P(),
        P(),
        P(),
    )
    out_specs = (P(None, prow, pcol, None), P(), P(None, prow, pcol))
    return jax.shard_map(
        per_device, mesh=fine, in_specs=in_specs, out_specs=out_specs, check_vma=False
    )
```

```python
import math

import jax
import jax.numpy as jnp
from jax import lax
from jax.experimental import pallas as pl
from jax.experimental.pallas import tpu as pltpu
from jax.sharding import PartitionSpec as P

HIGH_PRECISION = lax.Precision.HIGHEST
F32 = jnp.float32
BF16 = jnp.bfloat16
SCALE = math.sqrt(12.0) * math.log2(math.e)
MIB = 1024 * 1024
LIMIT = 64
COST = pl.CostEstimate(flops=10**8, bytes_accessed=10**5, transcendentals=0)


def params(mib, dims=1):
    return pltpu.CompilerParams(
        vmem_limit_bytes=mib * MIB, dimension_semantics=("arbitrary",) * dims
    )


def split(value):
    high = value.astype(BF16)
    low = (value - high.astype(F32)).astype(BF16)
    return high, low


def dot(a, b):
    return jnp.dot(a, b, preferred_element_type=F32)


def dot3(a_high, a_low, b_high, b_low):
    return dot(a_high, b_high) + dot(a_low, b_high) + dot(a_high, b_low)


def full(shape, **kw):
    return pl.BlockSpec(shape, lambda *_: (0,) * len(shape), **kw)


def once(shape):
    return full(shape, pipeline_mode=pl.Buffered(1))


ROWS = 128
GROUP = 16


def prep_kernel(first, starts, *refs):
    s_ref, co_ref, sg_ref, le_ref = refs[:4]
    hi_ref, lo_ref, rs_ref, cs_ref, cacc, feat, racc_ref = refs[-7:]
    step = pl.program_id(0)
    tiles_c = cs_ref.shape[0] // 4
    chunks = 4 * tiles_c
    block = first + step
    row_off = pl.multiple_of(starts[block // 4] + (block % 4) * ROWS, ROWS)

    @pl.when(step == 0)
    def _():
        cacc[...] = jnp.zeros_like(cacc)
        for j in range(tiles_c):
            off = pl.multiple_of(starts[3 + j], 512)
            for k in range(4):
                c = j * 4 + k
                at = pl.ds(pl.multiple_of(off + k * 128, 128), 128)
                feat[0, pl.ds(c, 1), :] = co_ref[0:1, at]
                feat[1, pl.ds(c, 1), :] = co_ref[1:2, at]
                feat[2, pl.ds(c, 1), :] = sg_ref[0:1, at]
                feat[3, pl.ds(c, 1), :] = le_ref[0:1, at] * (1.0 / SCALE)

    at = pl.ds(row_off, ROWS)

    def column(row):
        return jnp.broadcast_to(row, (ROWS, ROWS)).T

    racc_ref[1] = column(co_ref[0:1, at])
    racc_ref[2] = column(co_ref[1:2, at])
    racc_ref[3] = column(sg_ref[0:1, at])
    racc_ref[4] = column(le_ref[0:1, at] * (1.0 / SCALE))

    def body(g, _):
        base = pl.multiple_of(g * GROUP, GROUP)
        rows = pl.ds(base, GROUP)
        row_x, row_y, row_s, row_l = (racc_ref[k, rows, :] for k in range(1, 5))
        acc = jnp.zeros((GROUP, 128), F32)
        for c in range(chunks):
            s = s_ref[pl.ds(base * chunks + c, GROUP, stride=chunks), :]
            dx = row_x - feat[0, c : c + 1, :]
            dy = row_y - feat[1, c : c + 1, :]
            dist2 = dx * dx + dy * dy
            scale = row_l + feat[3, c : c + 1, :]
            g2 = dist2 * lax.rsqrt(jnp.maximum(dist2 * (scale * scale), 1e-30))
            weighted = s * ((1.0 + g2 * math.log(2.0)) * jnp.exp2(-g2))
            acc = acc + weighted * feat[2, c : c + 1, :]
            by_row = weighted * row_s
            cacc[c] += by_row.reshape(GROUP // 8, 8, 128).sum(0)
            high, low = split(s)
            hi_ref[rows, c * 128 : (c + 1) * 128] = high
            lo_ref[rows, c * 128 : (c + 1) * 128] = low
        racc_ref[0, rows, :] = acc * row_s
        return 0

    lax.fori_loop(0, ROWS // GROUP, body, 0)
    rs_ref[0] = racc_ref[0].T.sum(0, keepdims=True)

    @pl.when(step == pl.num_programs(0) - 1)
    def _():
        total = cacc[...].sum(1) * feat[2]
        cs_ref[...] = total if first == 0 else refs[7][...] + total


def prep(first, per, starts, s_view, coords, sigma, length, bufs, rows, cols):
    chunks = cols // 128
    any_spec = pl.BlockSpec(memory_space=pl.ANY)
    out_map = lambda s, st: (first + s, 0)
    args = [starts, s_view, coords, sigma, length]
    in_specs = [
        pl.BlockSpec((ROWS * chunks, 128), out_map),
        full(coords.shape),
        full(sigma.shape),
        full(length.shape),
    ]
    aliases = {}
    if first:
        args += list(bufs)
        in_specs += [any_spec, any_spec, any_spec, full((chunks, 128))]
        aliases = {5: 0, 6: 1, 7: 2}
    return pl.pallas_call(
        lambda *refs: prep_kernel(first, *refs),
        grid_spec=pltpu.PrefetchScalarGridSpec(
            num_scalar_prefetch=1,
            grid=(per,),
            in_specs=in_specs,
            out_specs=[
                pl.BlockSpec((ROWS, cols), out_map),
                pl.BlockSpec((ROWS, cols), out_map),
                pl.BlockSpec((1, 1, ROWS), lambda s, st: (first + s, 0, 0)),
                pl.BlockSpec((chunks, 128), lambda s, st: (0, 0)),
            ],
            scratch_shapes=[
                pltpu.VMEM((chunks, 8, 128), F32),
                pltpu.VMEM((4, chunks, 128), F32),
                pltpu.VMEM((5, ROWS, ROWS), F32),
            ],
        ),
        out_shape=[
            jax.ShapeDtypeStruct((rows, cols), BF16),
            jax.ShapeDtypeStruct((rows, cols), BF16),
            jax.ShapeDtypeStruct((rows // ROWS, 1, ROWS), F32),
            jax.ShapeDtypeStruct((chunks, 128), F32),
        ],
        input_output_aliases=aliases,
        compiler_params=params(LIMIT),
        cost_estimate=COST,
        name="kernel_sums",
    )(*args)


def put_row(ref, base, at, value):
    rows = pl.ds(base, 8)
    mask = lax.broadcasted_iota(jnp.int32, (8, 128), 0) == at
    ref[rows, :128] = jnp.where(mask, value, ref[rows, :128])


def trans_kernel(sc, *refs):
    pieces, refs = refs[:8], refs[8:]
    count, part, width = pieces[0].shape
    s_high, s_low, cs_ref = refs[:count], refs[count : 2 * count], refs[2 * count]
    own_ref, other_ref, th_ref, tl_ref, rows_ref = refs[2 * count + 1 : -count]
    tmps = refs[-count:]
    zp = pl.program_id(0)
    base = count * part

    @pl.when(zp == 0)
    def _():
        for r in range(8):
            for i in range(count):
                at = pl.multiple_of(i * 512 + sc[4 + r] * part, part)
                rows_ref[pl.ds(at, part), :] = pieces[r][i]
        for k in range(count * 4):
            at = slice(k * 128, (k + 1) * 128)
            high, low = split(rows_ref[at, :].T)
            th_ref[:, at] = high
            tl_ref[:, at] = low

    for i in range(count):
        out = dot3(th_ref[...], tl_ref[...], s_high[i][...], s_low[i][...])
        tmps[i][...] = out.T
    for ref, dcore in ((own_ref, 0), (other_ref, 1)):
        for dyh in range(2):
            sub = sc[dyh * 2 + dcore]
            at = pl.ds(pl.multiple_of(sub * part, part), part)
            ref[dyh, base:, :] = jnp.zeros((8, width), F32)
            for i in range(count):
                ref[dyh, i * part : (i + 1) * part, :] = tmps[i][at, :]
                ref[dyh, base + i : base + i + 1, :128] = cs_ref[
                    pl.ds(i * 8 + zp * 2 + sub // 2, 1), :
                ]


def trans_product(scal, pieces, s_hi, s_lo, csum):
    count, part, width = pieces[0].shape
    rows, cols = s_hi.shape
    high = count * part + 8
    s_specs = [
        pl.BlockSpec((rows, 256), lambda step, sc, i=i: (0, i * 4 + step)) for i in range(count)
    ]
    o_spec = pl.BlockSpec((2, high, width), lambda step, sc: (step, 0, 0))
    return pl.pallas_call(
        trans_kernel,
        grid_spec=pltpu.PrefetchScalarGridSpec(
            num_scalar_prefetch=1,
            grid=(4,),
            in_specs=[once(p.shape) for p in pieces] + s_specs * 2 + [full(csum.shape)],
            out_specs=[o_spec] * 2 + [full((width, rows))] * 2,
            scratch_shapes=[pltpu.VMEM((rows, width), F32)]
            + [pltpu.VMEM((256, width), F32)] * count,
        ),
        out_shape=[jax.ShapeDtypeStruct((8, high, width), F32)] * 2
        + [jax.ShapeDtypeStruct((width, rows), BF16)] * 2,
        compiler_params=params(LIMIT),
        cost_estimate=COST,
        name="transposed_product",
    )(scal, *pieces, *[s_hi] * count, *[s_lo] * count, csum)


def lower_blocks(n):
    return [(i, j) for i in range(n // 128) for j in range(i + 1)]


def direct_kernel(sc, own_ref, other_ref, sh_ref, sl_ref, th_ref, tl_ref, rs_ref, base_ref, *refs):
    y_ref, eo_ref, ex_ref, ch_ref, cl_ref, acc, packed = refs
    groups, count, part, width = own_ref.shape
    step = pl.program_id(0)
    tile = step % count
    base = count * part

    @pl.when(step == 0)
    def _():
        for ref, core in ((own_ref, sc[0]), (other_ref, 1 - sc[0])):
            for g in range(groups):
                for i in range(count):
                    at = pl.multiple_of(i * 1024 + (g * 2 + core) * part, part)
                    high, low = split(ref[g, i])
                    ch_ref[pl.ds(at, part), :] = high
                    cl_ref[pl.ds(at, part), :] = low

    out = dot3(sh_ref[...], sl_ref[...], ch_ref[...], cl_ref[...])
    high, low = split(out)
    gram = dot3(th_ref[...], tl_ref[...], high, low)
    rows_at = pl.ds(pl.multiple_of(tile * part, part), part)

    @pl.when(tile == 0)
    def _():
        y_ref[:, base:, :] = jnp.zeros((4, 8, width), F32)

    for x in range(4):
        y_ref[x, rows_at, :] = out[x * part : (x + 1) * part, :]
        put_row(y_ref.at[x], base, tile, rs_ref[tile * 4 + step // count * 2 + x // 2])

    @pl.when(step == 0)
    def _():
        acc[...] = gram

    @pl.when(step > 0)
    def _():
        acc[...] += gram

    @pl.when(step == pl.num_programs(0) - 1)
    def _():
        total = acc[...]
        acc[...] = base_ref[...] - total - total.T
        for k, (i, j) in enumerate(lower_blocks(width)):
            packed[k * 128 : (k + 1) * 128, :] = acc[
                i * 128 : (i + 1) * 128, j * 128 : (j + 1) * 128
            ]
        half = packed.shape[0] // 2
        eo_ref[...] = packed[pl.ds(pl.multiple_of(sc[0] * half, half), half), :]
        ex_ref[...] = packed[pl.ds(pl.multiple_of((1 - sc[0]) * half, half), half), :]


def direct_product(scal, own, other, s_hi, s_lo, th, tl, rsum, base):
    groups, count, part, width = own.shape
    rows, cols = s_hi.shape
    high = count * part + 8
    half = len(lower_blocks(width)) * 64
    row_block = lambda step: step % count * 2 + step // count
    s_spec = pl.BlockSpec((256, cols), lambda step, sc: (row_block(step), 0))
    t_spec = pl.BlockSpec((width, 256), lambda step, sc: (0, row_block(step)))
    return pl.pallas_call(
        direct_kernel,
        grid_spec=pltpu.PrefetchScalarGridSpec(
            num_scalar_prefetch=1,
            grid=(2 * count,),
            in_specs=[once(own.shape)] * 2
            + [s_spec] * 2
            + [t_spec] * 2
            + [full(rsum.shape), once(base.shape)],
            out_specs=[pl.BlockSpec((4, high, width), lambda step, sc: (step // count, 0, 0))]
            + [full((half, 128))] * 2,
            scratch_shapes=[pltpu.VMEM((cols, width), BF16)] * 2
            + [pltpu.VMEM((width, width), F32), pltpu.VMEM((2 * half, 128), F32)],
        ),
        out_shape=[jax.ShapeDtypeStruct((8, high, width), F32)]
        + [jax.ShapeDtypeStruct((half, 128), F32)] * 2,
        compiler_params=params(LIMIT),
        cost_estimate=COST,
        name="direct_product",
    )(scal, own, other, s_hi, s_lo, th, tl, rsum, base)


def hdot(a, b):
    return jnp.dot(a, b, precision=HIGH_PRECISION, preferred_element_type=F32)


def inverse_kernel(l_ref, bar_ref, own_bar_ref, own_ref, inv_ref, invt_ref, c_ref, base_ref):
    n = l_ref.shape[0]
    size = 128
    row = lax.broadcasted_iota(jnp.int32, (size, size), 0)
    col = lax.broadcasted_iota(jnp.int32, (size, size), 1)
    powers, results, scales = [], [], []
    for k in range(n // size):
        at = slice(k * size, (k + 1) * size)
        block = l_ref[at, at]
        diag = jnp.where(row == col, block, 0.0)
        by_row = 1.0 / diag.sum(1, keepdims=True)
        scales.append(1.0 / diag.sum(0, keepdims=True))
        nil = jnp.where(row > col, block, 0.0) * (-by_row)
        results.append(jnp.where(row == col, 1.0, 0.0) + nil)
        powers.append(nil)
    for _ in range(6):
        powers = [hdot(p, p) for p in powers]
        results = [r + hdot(r, p) for r, p in zip(results, powers)]
    inv_ref[...] = jnp.zeros_like(inv_ref)
    for k in range(n // size):
        at = slice(k * size, (k + 1) * size)
        inv_ref[at, at] = results[k] * scales[k]
    while size < n:
        for k in range(0, n, 2 * size):
            a, b = slice(k, k + size), slice(k + size, k + 2 * size)
            inv_ref[b, a] = -hdot(inv_ref[b, b], hdot(l_ref[b, a], inv_ref[a, a]))
        size *= 2
    invt_ref[...] = inv_ref[...].T
    c_ref[...] = dot3(*split(l_ref[...].T), *split(bar_ref[...]))
    base_ref[...] = dot3(*split(own_bar_ref[...].T), *split(own_ref[...]))


def inverse(l11, l11_bar, own_bar, own):
    out = jax.ShapeDtypeStruct(l11.shape, F32)
    return pl.pallas_call(
        inverse_kernel,
        out_shape=[out] * 4,
        compiler_params=pltpu.CompilerParams(vmem_limit_bytes=LIMIT * MIB),
        cost_estimate=COST,
        name="inverse",
    )(l11, l11_bar, own_bar, own)


def final_kernel(sc, own_ref, other_ref, c_ref, inv_ref, invt_ref, out_ref, packed, p_ref):
    n = c_ref.shape[0]
    half = packed.shape[0] // 2
    packed[pl.ds(pl.multiple_of(sc[0] * half, half), half), :] = own_ref[...]
    packed[pl.ds(pl.multiple_of((1 - sc[0]) * half, half), half), :] = other_ref[...]
    p_ref[...] = jnp.zeros_like(p_ref)
    row = lax.broadcasted_iota(jnp.int32, (128, 128), 0)
    col = lax.broadcasted_iota(jnp.int32, (128, 128), 1)
    for k, (i, j) in enumerate(lower_blocks(n)):
        at = (slice(i * 128, (i + 1) * 128), slice(j * 128, (j + 1) * 128))
        x = c_ref[at] - packed[k * 128 : (k + 1) * 128, :]
        if i == j:
            x = jnp.where(row > col, x, jnp.where(row == col, 0.5 * x, 0.0))
        p_ref[at] = x
    q = dot3(*split(invt_ref[...]), *split(p_ref[...]))
    q = dot3(*split(q), *split(inv_ref[...]))
    out_ref[...] = 0.5 * (q + q.T)


def final(scal, own, other, c, inv, invt):
    return pl.pallas_call(
        final_kernel,
        grid_spec=pltpu.PrefetchScalarGridSpec(
            num_scalar_prefetch=1,
            grid=(1,),
            in_specs=[full(own.shape)] * 2 + [full(c.shape)] * 3,
            out_specs=full(c.shape),
            scratch_shapes=[
                pltpu.VMEM((2 * own.shape[0], own.shape[1]), F32),
                pltpu.VMEM(c.shape, F32),
            ],
        ),
        out_shape=jax.ShapeDtypeStruct(c.shape, F32),
        compiler_params=params(LIMIT),
        name="diagonal_tile",
    )(scal, own, other, c, inv, invt)


def panel_kernel(sc, bar_ref, inv_ref, *refs):
    parts, (out_ref, rg_ref) = refs[:-2], refs[-2:]
    n = bar_ref.shape[0]
    total = parts[0][...]
    for part in parts[1:]:
        total = total + part[...]
    out_ref[...] = dot3(*split(bar_ref[...] - total[:n, :]), *split(inv_ref[...]))
    sums = total[n:, :128]
    sums = jnp.where(sc[0] == 1, sums[:, 64:], sums[:, :64])
    rg_ref[...] = sums[: rg_ref.shape[0], :]


def panel(scal, bar, inv, parts):
    n, width = bar.shape
    return pl.pallas_call(
        panel_kernel,
        grid_spec=pltpu.PrefetchScalarGridSpec(
            num_scalar_prefetch=1,
            grid=(1,),
            in_specs=[full(bar.shape), full(inv.shape)] + [full(p.shape) for p in parts],
            out_specs=[full(bar.shape), full((n // 64, 64))],
        ),
        out_shape=[
            jax.ShapeDtypeStruct(bar.shape, F32),
            jax.ShapeDtypeStruct((n // 64, 64), F32),
        ],
        compiler_params=params(LIMIT),
        name="panel_tiles",
    )(scal, bar, inv, *parts)


def permutations():
    def make(move):
        pairs = []
        for z in range(4):
            for yh in range(2):
                for core in range(2):
                    for yl in range(2):
                        for x in range(4):
                            nz, nyh, nc, nyl, nx = move(z, yh, core, yl, x)
                            src = (z * 4 + yh * 2 + core) * 8 + yl * 4 + x
                            dst = (nz * 4 + nyh * 2 + nc) * 8 + nyl * 4 + nx
                            pairs.append((src, dst))
        return pairs

    perms = {
        "x+": make(lambda z, h, c, l, x: (z, h, c, l, (x + 1) % 4)),
        "x-": make(lambda z, h, c, l, x: (z, h, c, l, (x + 3) % 4)),
        "x2": make(lambda z, h, c, l, x: (z, h, c, l, (x + 2) % 4)),
        "z+": make(lambda z, h, c, l, x: ((z + 1) % 4, h, c, l, x)),
        "z-": make(lambda z, h, c, l, x: ((z + 3) % 4, h, c, l, x)),
        "z^1": make(lambda z, h, c, l, x: (z ^ 1, h, c, l, x)),
        "z^2": make(lambda z, h, c, l, x: (z ^ 2, h, c, l, x)),
        "z^3": make(lambda z, h, c, l, x: (z ^ 3, h, c, l, x)),
        "yl": make(lambda z, h, c, l, x: (z, h, c, 1 - l, x)),
        "yh": make(lambda z, h, c, l, x: (z, 1 - h, c, l, x)),
        "yhl": make(lambda z, h, c, l, x: (z, 1 - h, c, 1 - l, x)),
        "core": make(lambda z, h, c, l, x: (z, h, 1 - c, l, x)),
    }
    home = lambda z, h, c, l, x: ((z // 2) * 2 + l, x // 2, x % 2, z % 2, h * 2 + c)
    flip = lambda z, h, c, l, x: ((z // 2) * 2 + l, 1 - x // 2, x % 2, z % 2, h * 2 + c)
    perms["home0"] = make(home)
    perms["home1"] = make(flip)
    perms["back0"] = [(d, s) for s, d in perms["home0"]]
    perms["back1"] = [(d, s) for s, d in perms["home1"]]
    return perms


PERMS = permutations()


AXES = ("z", "yh", "core", "yl", "x")


def move(value, name):
    return lax.ppermute(value, AXES, PERMS[name])


def after(values, *deps):
    return lax.optimization_barrier((values, deps))[0]


def per_device(s_bar, l21, panel_column_cotangent, l11, l11_bar, coords, sigma, length, tile_block):
    z, yh, core, yl, x = (lax.axis_index(a) for a in AXES)
    row_id = z * 4 + yh * 2 + core
    col_id = yl * 4 + x
    count, _, width, tiles_c = s_bar.shape[:4]
    part = l21.shape[2]
    rows, cols = count * width, tiles_c * width
    own = l21.reshape(count, part, width)
    own_bar = panel_column_cotangent.reshape(count * part, width)
    ints = lambda vals: jnp.stack([jnp.asarray(v, jnp.int32) for v in vals])

    row_tiles = [i * 16 + row_id for i in range(count)]
    col_tiles = [j * 8 + col_id for j in range(tiles_c)]
    starts = jnp.take(tile_block, ints(row_tiles + col_tiles)) * width
    s_view = s_bar.reshape(rows * cols // 128, 128)
    sig, len_ = sigma.reshape(1, -1), length.reshape(1, -1)

    rw = {(0, 0): own}
    rw[1, 0] = move(own, "yl")
    rw[0, 3] = move(own, "x+")
    rw[0, 1] = move(own, "x-")
    home = move(own, "home0")

    part_blocks = rows // ROWS // 2
    feats = (s_view, coords, sig, len_)
    bufs = prep(0, part_blocks, starts, *feats, None, rows, cols)
    near, left, right, home = after((rw[1, 0], rw[0, 3], rw[0, 1], home), bufs[3])
    rw[0, 1] = right
    starts = after(starts, near, left, right, home)
    col_own = lax.all_gather(home, ("z", "yh"))
    rw[1, 3] = move(near, "x+")
    rw[1, 1] = move(near, "x-")
    rw[0, 2] = move(left, "x+")
    s_hi, s_lo, rsum, csum = prep(part_blocks, part_blocks, starts, *feats, bufs, rows, cols)
    rw[1, 2] = move(after(rw[1, 1], csum), "x-")

    flat = own.reshape(count * part, width)
    inv, invt, c_mat, base = inverse(after(l11, csum), l11_bar, own_bar, flat)

    row_keys = [(a, b) for a in range(2) for b in range(4)]
    scal = ints(
        [(yh ^ a) * 2 + (core ^ b) for a in range(2) for b in range(2)]
        + [(yl ^ a) * 4 + (x + b) % 4 for a, b in row_keys]
    )
    own_t, other_t, th, tl = trans_product(
        after(scal, inv), [rw[k] for k in row_keys], s_hi, s_lo, csum
    )
    other_t = move(other_t, "core")
    col_other = move(after(col_own, th), "core")
    t_sum = own_t + other_t
    t_sum = lax.psum_scatter(t_sum.reshape(4, 2, -1, width), "z", scatter_dimension=0)

    y, eo, ex = direct_product(
        after(ints([core]), inv), col_own, col_other, s_hi, s_lo, th, tl, rsum, base
    )
    y = lax.psum_scatter(y, ("yl", "x"), scatter_dimension=0)
    others, n_others = ("z", "yh", "yl", "x"), 64
    e = eo + move(ex, "core")
    e = lax.all_to_all(e.reshape(n_others, -1, 128), others, 0, 0).sum(0)
    e = lax.all_to_all(jnp.broadcast_to(e[None], (n_others,) + e.shape), others, 0, 0)
    t_sum = after(t_sum, eo)
    t0 = move(t_sum[0], "back0")
    t1 = move(t_sum[1], "back1")
    e = e.reshape(eo.shape)
    grad11 = final(ints([core]), e, move(e, "core"), c_mat, inv, invt)
    grad21, row_grad = panel(ints([x % 2]), own_bar, inv, [y, t0, t1])
    return (
        grad21.reshape(count, 1, part, width),
        grad11,
        row_grad.reshape(count, 1, part),
    )


def solution(mesh):
    fine = jax.sharding.Mesh(mesh.devices.reshape(4, 2, 2, 2, 4), AXES)
    prow, pcol = AXES[:3], AXES[3:]
    in_specs = (
        P(None, prow, None, None, pcol, None),
        P(None, prow, pcol, None),
        P(None, prow, pcol, None),
        P(),
        P(),
        P(),
        P(),
        P(),
        P(),
    )
    out_specs = (P(None, prow, pcol, None), P(), P(None, prow, pcol))
    return jax.shard_map(
        per_device, mesh=fine, in_specs=in_specs, out_specs=out_specs, check_vma=False
    )
```

```python
import math

import jax
import jax.numpy as jnp
from jax import lax
from jax.experimental import pallas as pl
from jax.experimental.pallas import tpu as pltpu
from jax.sharding import PartitionSpec as P

HIGH_PRECISION = lax.Precision.HIGHEST
F32 = jnp.float32
BF16 = jnp.bfloat16
SCALE = math.sqrt(12.0) * math.log2(math.e)
MIB = 1024 * 1024
LIMIT = 64
COST = pl.CostEstimate(flops=10**8, bytes_accessed=10**5, transcendentals=0)


def params(mib, dims=1):
    return pltpu.CompilerParams(
        vmem_limit_bytes=mib * MIB, dimension_semantics=("arbitrary",) * dims
    )


def split(value):
    high = value.astype(BF16)
    low = (value - high.astype(F32)).astype(BF16)
    return high, low


def dot(a, b):
    return jnp.dot(a, b, preferred_element_type=F32)


def dot3(a_high, a_low, b_high, b_low):
    return dot(a_high, b_high) + dot(a_low, b_high) + dot(a_high, b_low)


def full(shape, **kw):
    return pl.BlockSpec(shape, lambda *_: (0,) * len(shape), **kw)


def once(shape):
    return full(shape, pipeline_mode=pl.Buffered(1))


ROWS = 128
GROUP = 32


def prep_kernel(first, starts, *refs):
    s_ref, co_ref, sg_ref, le_ref = refs[:4]
    hi_ref, lo_ref, rs_ref, cs_ref, cacc, feat, racc_ref = refs[-7:]
    step = pl.program_id(0)
    tiles_c = cs_ref.shape[0] // 4
    chunks = 4 * tiles_c
    block = first + step
    row_off = pl.multiple_of(starts[block // 4] + (block % 4) * ROWS, ROWS)

    @pl.when(step == 0)
    def _():
        cacc[...] = jnp.zeros_like(cacc)
        for j in range(tiles_c):
            off = pl.multiple_of(starts[3 + j], 512)
            for k in range(4):
                c = j * 4 + k
                at = pl.ds(pl.multiple_of(off + k * 128, 128), 128)
                feat[0, pl.ds(c, 1), :] = co_ref[0:1, at]
                feat[1, pl.ds(c, 1), :] = co_ref[1:2, at]
                feat[2, pl.ds(c, 1), :] = sg_ref[0:1, at]
                feat[3, pl.ds(c, 1), :] = le_ref[0:1, at] * (1.0 / SCALE)

    at = pl.ds(row_off, ROWS)

    def column(row):
        return jnp.broadcast_to(row, (ROWS, ROWS)).T

    racc_ref[1] = column(co_ref[0:1, at])
    racc_ref[2] = column(co_ref[1:2, at])
    racc_ref[3] = column(sg_ref[0:1, at])
    racc_ref[4] = column(le_ref[0:1, at] * (1.0 / SCALE))

    def body(g, _):
        base = pl.multiple_of(g * GROUP, GROUP)
        rows = pl.ds(base, GROUP)
        row_x, row_y, row_s, row_l = (racc_ref[k, rows, :] for k in range(1, 5))
        acc = jnp.zeros((GROUP, 128), F32)
        for c in range(chunks):
            s = s_ref[pl.ds(base * chunks + c, GROUP, stride=chunks), :]
            dx = row_x - feat[0, c : c + 1, :]
            dy = row_y - feat[1, c : c + 1, :]
            dist2 = dx * dx + dy * dy
            scale = row_l + feat[3, c : c + 1, :]
            g2 = dist2 * lax.rsqrt(jnp.maximum(dist2 * (scale * scale), 1e-30))
            weighted = s * ((1.0 + g2 * math.log(2.0)) * jnp.exp2(-g2))
            acc = acc + weighted * feat[2, c : c + 1, :]
            by_row = weighted * row_s
            cacc[c] += by_row.reshape(GROUP // 8, 8, 128).sum(0)
            high, low = split(s)
            hi_ref[rows, c * 128 : (c + 1) * 128] = high
            lo_ref[rows, c * 128 : (c + 1) * 128] = low
        racc_ref[0, rows, :] = acc * row_s
        return 0

    lax.fori_loop(0, ROWS // GROUP, body, 0)
    rs_ref[0] = racc_ref[0].T.sum(0, keepdims=True)

    @pl.when(step == pl.num_programs(0) - 1)
    def _():
        total = cacc[...].sum(1) * feat[2]
        cs_ref[...] = total if first == 0 else refs[7][...] + total


def prep(first, per, starts, s_view, coords, sigma, length, bufs, rows, cols):
    chunks = cols // 128
    any_spec = pl.BlockSpec(memory_space=pl.ANY)
    out_map = lambda s, st: (first + s, 0)
    args = [starts, s_view, coords, sigma, length]
    in_specs = [
        pl.BlockSpec((ROWS * chunks, 128), out_map),
        full(coords.shape),
        full(sigma.shape),
        full(length.shape),
    ]
    aliases = {}
    if first:
        args += list(bufs)
        in_specs += [any_spec, any_spec, any_spec, full((chunks, 128))]
        aliases = {5: 0, 6: 1, 7: 2}
    return pl.pallas_call(
        lambda *refs: prep_kernel(first, *refs),
        grid_spec=pltpu.PrefetchScalarGridSpec(
            num_scalar_prefetch=1,
            grid=(per,),
            in_specs=in_specs,
            out_specs=[
                pl.BlockSpec((ROWS, cols), out_map),
                pl.BlockSpec((ROWS, cols), out_map),
                pl.BlockSpec((1, 1, ROWS), lambda s, st: (first + s, 0, 0)),
                pl.BlockSpec((chunks, 128), lambda s, st: (0, 0)),
            ],
            scratch_shapes=[
                pltpu.VMEM((chunks, 8, 128), F32),
                pltpu.VMEM((4, chunks, 128), F32),
                pltpu.VMEM((5, ROWS, ROWS), F32),
            ],
        ),
        out_shape=[
            jax.ShapeDtypeStruct((rows, cols), BF16),
            jax.ShapeDtypeStruct((rows, cols), BF16),
            jax.ShapeDtypeStruct((rows // ROWS, 1, ROWS), F32),
            jax.ShapeDtypeStruct((chunks, 128), F32),
        ],
        input_output_aliases=aliases,
        compiler_params=params(LIMIT),
        cost_estimate=COST,
        name="kernel_sums",
    )(*args)


def put_row(ref, base, at, value):
    rows = pl.ds(base, 8)
    mask = lax.broadcasted_iota(jnp.int32, (8, 128), 0) == at
    ref[rows, :128] = jnp.where(mask, value, ref[rows, :128])


def trans_kernel(sc, *refs):
    pieces, refs = refs[:8], refs[8:]
    count, part, width = pieces[0].shape
    s_high, s_low, cs_ref = refs[:count], refs[count : 2 * count], refs[2 * count]
    own_ref, other_ref, th_ref, tl_ref, rows_ref = refs[2 * count + 1 : -count]
    tmps = refs[-count:]
    zp = pl.program_id(0)
    base = count * part

    @pl.when(zp == 0)
    def _():
        for r in range(8):
            for i in range(count):
                at = pl.multiple_of(i * 512 + sc[4 + r] * part, part)
                rows_ref[pl.ds(at, part), :] = pieces[r][i]
        for k in range(count * 4):
            at = slice(k * 128, (k + 1) * 128)
            high, low = split(rows_ref[at, :].T)
            th_ref[:, at] = high
            tl_ref[:, at] = low

    for i in range(count):
        out = dot3(th_ref[...], tl_ref[...], s_high[i][...], s_low[i][...])
        tmps[i][...] = out.T
    for ref, dcore in ((own_ref, 0), (other_ref, 1)):
        for dyh in range(2):
            sub = sc[dyh * 2 + dcore]
            at = pl.ds(pl.multiple_of(sub * part, part), part)
            ref[dyh, base:, :] = jnp.zeros((8, width), F32)
            for i in range(count):
                ref[dyh, i * part : (i + 1) * part, :] = tmps[i][at, :]
                ref[dyh, base + i : base + i + 1, :128] = cs_ref[
                    pl.ds(i * 8 + zp * 2 + sub // 2, 1), :
                ]


def trans_product(scal, pieces, s_hi, s_lo, csum):
    count, part, width = pieces[0].shape
    rows, cols = s_hi.shape
    high = count * part + 8
    s_specs = [
        pl.BlockSpec((rows, 256), lambda step, sc, i=i: (0, i * 4 + step)) for i in range(count)
    ]
    o_spec = pl.BlockSpec((2, high, width), lambda step, sc: (step, 0, 0))
    return pl.pallas_call(
        trans_kernel,
        grid_spec=pltpu.PrefetchScalarGridSpec(
            num_scalar_prefetch=1,
            grid=(4,),
            in_specs=[once(p.shape) for p in pieces] + s_specs * 2 + [full(csum.shape)],
            out_specs=[o_spec] * 2 + [full((width, rows))] * 2,
            scratch_shapes=[pltpu.VMEM((rows, width), F32)]
            + [pltpu.VMEM((256, width), F32)] * count,
        ),
        out_shape=[jax.ShapeDtypeStruct((8, high, width), F32)] * 2
        + [jax.ShapeDtypeStruct((width, rows), BF16)] * 2,
        compiler_params=params(LIMIT),
        cost_estimate=COST,
        name="transposed_product",
    )(scal, *pieces, *[s_hi] * count, *[s_lo] * count, csum)


def lower_blocks(n):
    return [(i, j) for i in range(n // 128) for j in range(i + 1)]


def direct_kernel(sc, own_ref, other_ref, sh_ref, sl_ref, th_ref, tl_ref, rs_ref, base_ref, *refs):
    y_ref, eo_ref, ex_ref, ch_ref, cl_ref, acc, packed = refs
    groups, count, part, width = own_ref.shape
    step = pl.program_id(0)
    tile = step % count
    base = count * part

    @pl.when(step == 0)
    def _():
        for ref, core in ((own_ref, sc[0]), (other_ref, 1 - sc[0])):
            for g in range(groups):
                for i in range(count):
                    at = pl.multiple_of(i * 1024 + (g * 2 + core) * part, part)
                    high, low = split(ref[g, i])
                    ch_ref[pl.ds(at, part), :] = high
                    cl_ref[pl.ds(at, part), :] = low

    out = dot3(sh_ref[...], sl_ref[...], ch_ref[...], cl_ref[...])
    high, low = split(out)
    gram = dot3(th_ref[...], tl_ref[...], high, low)
    rows_at = pl.ds(pl.multiple_of(tile * part, part), part)

    @pl.when(tile == 0)
    def _():
        y_ref[:, base:, :] = jnp.zeros((4, 8, width), F32)

    for x in range(4):
        y_ref[x, rows_at, :] = out[x * part : (x + 1) * part, :]
        put_row(y_ref.at[x], base, tile, rs_ref[tile * 4 + step // count * 2 + x // 2])

    @pl.when(step == 0)
    def _():
        acc[...] = gram

    @pl.when(step > 0)
    def _():
        acc[...] += gram

    @pl.when(step == pl.num_programs(0) - 1)
    def _():
        total = acc[...]
        acc[...] = base_ref[...] - total - total.T
        for k, (i, j) in enumerate(lower_blocks(width)):
            packed[k * 128 : (k + 1) * 128, :] = acc[
                i * 128 : (i + 1) * 128, j * 128 : (j + 1) * 128
            ]
        half = packed.shape[0] // 2
        eo_ref[...] = packed[pl.ds(pl.multiple_of(sc[0] * half, half), half), :]
        ex_ref[...] = packed[pl.ds(pl.multiple_of((1 - sc[0]) * half, half), half), :]


def direct_product(scal, own, other, s_hi, s_lo, th, tl, rsum, base):
    groups, count, part, width = own.shape
    rows, cols = s_hi.shape
    high = count * part + 8
    half = len(lower_blocks(width)) * 64
    row_block = lambda step: step % count * 2 + step // count
    s_spec = pl.BlockSpec((256, cols), lambda step, sc: (row_block(step), 0))
    t_spec = pl.BlockSpec((width, 256), lambda step, sc: (0, row_block(step)))
    return pl.pallas_call(
        direct_kernel,
        grid_spec=pltpu.PrefetchScalarGridSpec(
            num_scalar_prefetch=1,
            grid=(2 * count,),
            in_specs=[once(own.shape)] * 2
            + [s_spec] * 2
            + [t_spec] * 2
            + [full(rsum.shape), once(base.shape)],
            out_specs=[pl.BlockSpec((4, high, width), lambda step, sc: (step // count, 0, 0))]
            + [full((half, 128))] * 2,
            scratch_shapes=[pltpu.VMEM((cols, width), BF16)] * 2
            + [pltpu.VMEM((width, width), F32), pltpu.VMEM((2 * half, 128), F32)],
        ),
        out_shape=[jax.ShapeDtypeStruct((8, high, width), F32)]
        + [jax.ShapeDtypeStruct((half, 128), F32)] * 2,
        compiler_params=params(LIMIT),
        cost_estimate=COST,
        name="direct_product",
    )(scal, own, other, s_hi, s_lo, th, tl, rsum, base)


def hdot(a, b):
    return jnp.dot(a, b, precision=HIGH_PRECISION, preferred_element_type=F32)


def inverse_kernel(l_ref, bar_ref, own_bar_ref, own_ref, inv_ref, invt_ref, c_ref, base_ref):
    n = l_ref.shape[0]
    size = 128
    row = lax.broadcasted_iota(jnp.int32, (size, size), 0)
    col = lax.broadcasted_iota(jnp.int32, (size, size), 1)
    powers, results, scales = [], [], []
    for k in range(n // size):
        at = slice(k * size, (k + 1) * size)
        block = l_ref[at, at]
        diag = jnp.where(row == col, block, 0.0)
        by_row = 1.0 / diag.sum(1, keepdims=True)
        scales.append(1.0 / diag.sum(0, keepdims=True))
        nil = jnp.where(row > col, block, 0.0) * (-by_row)
        results.append(jnp.where(row == col, 1.0, 0.0) + nil)
        powers.append(nil)
    for _ in range(6):
        powers = [hdot(p, p) for p in powers]
        results = [r + hdot(r, p) for r, p in zip(results, powers)]
    inv_ref[...] = jnp.zeros_like(inv_ref)
    for k in range(n // size):
        at = slice(k * size, (k + 1) * size)
        inv_ref[at, at] = results[k] * scales[k]
    while size < n:
        for k in range(0, n, 2 * size):
            a, b = slice(k, k + size), slice(k + size, k + 2 * size)
            inv_ref[b, a] = -hdot(inv_ref[b, b], hdot(l_ref[b, a], inv_ref[a, a]))
        size *= 2
    invt_ref[...] = inv_ref[...].T
    c_ref[...] = dot3(*split(l_ref[...].T), *split(bar_ref[...]))
    base_ref[...] = dot3(*split(own_bar_ref[...].T), *split(own_ref[...]))


def inverse(l11, l11_bar, own_bar, own):
    out = jax.ShapeDtypeStruct(l11.shape, F32)
    return pl.pallas_call(
        inverse_kernel,
        out_shape=[out] * 4,
        compiler_params=pltpu.CompilerParams(vmem_limit_bytes=LIMIT * MIB),
        cost_estimate=COST,
        name="inverse",
    )(l11, l11_bar, own_bar, own)


def final_kernel(sc, own_ref, other_ref, c_ref, inv_ref, invt_ref, out_ref, packed, p_ref):
    n = c_ref.shape[0]
    half = packed.shape[0] // 2
    packed[pl.ds(pl.multiple_of(sc[0] * half, half), half), :] = own_ref[...]
    packed[pl.ds(pl.multiple_of((1 - sc[0]) * half, half), half), :] = other_ref[...]
    p_ref[...] = jnp.zeros_like(p_ref)
    row = lax.broadcasted_iota(jnp.int32, (128, 128), 0)
    col = lax.broadcasted_iota(jnp.int32, (128, 128), 1)
    for k, (i, j) in enumerate(lower_blocks(n)):
        at = (slice(i * 128, (i + 1) * 128), slice(j * 128, (j + 1) * 128))
        x = c_ref[at] - packed[k * 128 : (k + 1) * 128, :]
        if i == j:
            x = jnp.where(row > col, x, jnp.where(row == col, 0.5 * x, 0.0))
        p_ref[at] = x
    q = dot3(*split(invt_ref[...]), *split(p_ref[...]))
    q = dot3(*split(q), *split(inv_ref[...]))
    out_ref[...] = 0.5 * (q + q.T)


def final(scal, own, other, c, inv, invt):
    return pl.pallas_call(
        final_kernel,
        grid_spec=pltpu.PrefetchScalarGridSpec(
            num_scalar_prefetch=1,
            grid=(1,),
            in_specs=[full(own.shape)] * 2 + [full(c.shape)] * 3,
            out_specs=full(c.shape),
            scratch_shapes=[
                pltpu.VMEM((2 * own.shape[0], own.shape[1]), F32),
                pltpu.VMEM(c.shape, F32),
            ],
        ),
        out_shape=jax.ShapeDtypeStruct(c.shape, F32),
        compiler_params=params(LIMIT),
        name="diagonal_tile",
    )(scal, own, other, c, inv, invt)


def panel_kernel(sc, bar_ref, inv_ref, *refs):
    parts, (out_ref, rg_ref) = refs[:-2], refs[-2:]
    n = bar_ref.shape[0]
    total = parts[0][...]
    for part in parts[1:]:
        total = total + part[...]
    out_ref[...] = dot3(*split(bar_ref[...] - total[:n, :]), *split(inv_ref[...]))
    sums = total[n:, :128]
    sums = jnp.where(sc[0] == 1, sums[:, 64:], sums[:, :64])
    rg_ref[...] = sums[: rg_ref.shape[0], :]


def panel(scal, bar, inv, parts):
    n, width = bar.shape
    return pl.pallas_call(
        panel_kernel,
        grid_spec=pltpu.PrefetchScalarGridSpec(
            num_scalar_prefetch=1,
            grid=(1,),
            in_specs=[full(bar.shape), full(inv.shape)] + [full(p.shape) for p in parts],
            out_specs=[full(bar.shape), full((n // 64, 64))],
        ),
        out_shape=[
            jax.ShapeDtypeStruct(bar.shape, F32),
            jax.ShapeDtypeStruct((n // 64, 64), F32),
        ],
        compiler_params=params(LIMIT),
        name="panel_tiles",
    )(scal, bar, inv, *parts)


def permutations():
    def make(move):
        pairs = []
        for z in range(4):
            for yh in range(2):
                for core in range(2):
                    for yl in range(2):
                        for x in range(4):
                            nz, nyh, nc, nyl, nx = move(z, yh, core, yl, x)
                            src = (z * 4 + yh * 2 + core) * 8 + yl * 4 + x
                            dst = (nz * 4 + nyh * 2 + nc) * 8 + nyl * 4 + nx
                            pairs.append((src, dst))
        return pairs

    perms = {
        "x+": make(lambda z, h, c, l, x: (z, h, c, l, (x + 1) % 4)),
        "x-": make(lambda z, h, c, l, x: (z, h, c, l, (x + 3) % 4)),
        "x2": make(lambda z, h, c, l, x: (z, h, c, l, (x + 2) % 4)),
        "z+": make(lambda z, h, c, l, x: ((z + 1) % 4, h, c, l, x)),
        "z-": make(lambda z, h, c, l, x: ((z + 3) % 4, h, c, l, x)),
        "z^1": make(lambda z, h, c, l, x: (z ^ 1, h, c, l, x)),
        "z^2": make(lambda z, h, c, l, x: (z ^ 2, h, c, l, x)),
        "z^3": make(lambda z, h, c, l, x: (z ^ 3, h, c, l, x)),
        "yl": make(lambda z, h, c, l, x: (z, h, c, 1 - l, x)),
        "yh": make(lambda z, h, c, l, x: (z, 1 - h, c, l, x)),
        "yhl": make(lambda z, h, c, l, x: (z, 1 - h, c, 1 - l, x)),
        "core": make(lambda z, h, c, l, x: (z, h, 1 - c, l, x)),
    }
    home = lambda z, h, c, l, x: ((z // 2) * 2 + l, x // 2, x % 2, z % 2, h * 2 + c)
    flip = lambda z, h, c, l, x: ((z // 2) * 2 + l, 1 - x // 2, x % 2, z % 2, h * 2 + c)
    perms["home0"] = make(home)
    perms["home1"] = make(flip)
    perms["back0"] = [(d, s) for s, d in perms["home0"]]
    perms["back1"] = [(d, s) for s, d in perms["home1"]]
    return perms


PERMS = permutations()


AXES = ("z", "yh", "core", "yl", "x")


def move(value, name):
    return lax.ppermute(value, AXES, PERMS[name])


def after(values, *deps):
    return lax.optimization_barrier((values, deps))[0]


def per_device(s_bar, l21, panel_column_cotangent, l11, l11_bar, coords, sigma, length, tile_block):
    z, yh, core, yl, x = (lax.axis_index(a) for a in AXES)
    row_id = z * 4 + yh * 2 + core
    col_id = yl * 4 + x
    count, _, width, tiles_c = s_bar.shape[:4]
    part = l21.shape[2]
    rows, cols = count * width, tiles_c * width
    own = l21.reshape(count, part, width)
    own_bar = panel_column_cotangent.reshape(count * part, width)
    ints = lambda vals: jnp.stack([jnp.asarray(v, jnp.int32) for v in vals])

    row_tiles = [i * 16 + row_id for i in range(count)]
    col_tiles = [j * 8 + col_id for j in range(tiles_c)]
    starts = jnp.take(tile_block, ints(row_tiles + col_tiles)) * width
    s_view = s_bar.reshape(rows * cols // 128, 128)
    sig, len_ = sigma.reshape(1, -1), length.reshape(1, -1)

    rw = {(0, 0): own}
    rw[1, 0] = move(own, "yl")
    rw[0, 3] = move(own, "x+")
    rw[0, 1] = move(own, "x-")
    home = move(own, "home0")

    part_blocks = rows // ROWS // 2
    feats = (s_view, coords, sig, len_)
    bufs = prep(0, part_blocks, starts, *feats, None, rows, cols)
    near, left, right, home = after((rw[1, 0], rw[0, 3], rw[0, 1], home), bufs[3])
    rw[0, 1] = right
    starts = after(starts, near, left, right, home)
    col_own = lax.all_gather(home, ("z", "yh"))
    rw[1, 3] = move(near, "x+")
    rw[1, 1] = move(near, "x-")
    rw[0, 2] = move(left, "x+")
    s_hi, s_lo, rsum, csum = prep(part_blocks, part_blocks, starts, *feats, bufs, rows, cols)
    rw[1, 2] = move(after(rw[1, 1], csum), "x-")

    flat = own.reshape(count * part, width)
    inv, invt, c_mat, base = inverse(after(l11, csum), l11_bar, own_bar, flat)

    row_keys = [(a, b) for a in range(2) for b in range(4)]
    scal = ints(
        [(yh ^ a) * 2 + (core ^ b) for a in range(2) for b in range(2)]
        + [(yl ^ a) * 4 + (x + b) % 4 for a, b in row_keys]
    )
    own_t, other_t, th, tl = trans_product(
        after(scal, inv), [rw[k] for k in row_keys], s_hi, s_lo, csum
    )
    other_t = move(other_t, "core")
    col_other = move(after(col_own, th), "core")
    t_sum = own_t + other_t
    t_sum = lax.psum_scatter(t_sum.reshape(4, 2, -1, width), "z", scatter_dimension=0)

    y, eo, ex = direct_product(
        after(ints([core]), inv), col_own, col_other, s_hi, s_lo, th, tl, rsum, base
    )
    y = lax.psum_scatter(y, ("yl", "x"), scatter_dimension=0)
    others, n_others = ("z", "yh", "yl", "x"), 64
    e = eo + move(ex, "core")
    e = lax.all_to_all(e.reshape(n_others, -1, 128), others, 0, 0).sum(0)
    e = lax.all_to_all(jnp.broadcast_to(e[None], (n_others,) + e.shape), others, 0, 0)
    t_sum = after(t_sum, eo)
    t0 = move(t_sum[0], "back0")
    t1 = move(t_sum[1], "back1")
    e = e.reshape(eo.shape)
    grad11 = final(ints([core]), e, move(e, "core"), c_mat, inv, invt)
    grad21, row_grad = panel(ints([x % 2]), own_bar, inv, [y, t0, t1])
    return (
        grad21.reshape(count, 1, part, width),
        grad11,
        row_grad.reshape(count, 1, part),
    )


def solution(mesh):
    fine = jax.sharding.Mesh(mesh.devices.reshape(4, 2, 2, 2, 4), AXES)
    prow, pcol = AXES[:3], AXES[3:]
    in_specs = (
        P(None, prow, None, None, pcol, None),
        P(None, prow, pcol, None),
        P(None, prow, pcol, None),
        P(),
        P(),
        P(),
        P(),
        P(),
        P(),
    )
    out_specs = (P(None, prow, pcol, None), P(), P(None, prow, pcol))
    return jax.shard_map(
        per_device, mesh=fine, in_specs=in_specs, out_specs=out_specs, check_vma=False
    )
```
